32 devices in a mesh: ctx: 16 (over z, y, x), head: 2 (over core).
Axes of the slice: x: 2, y: 2, z: 4, core: 2. Of those that a mesh axis runs over, the one named last changes fastest.
Arguments:
- window_queries: bfloat16 [4096, 4096], P('ctx', 'head'), may hold values from -260 to 260
- window_keys: bfloat16 [4096, 512], P('ctx', 'head'), may hold values from -7 to 7
- window_values: bfloat16 [4096, 512], P('ctx', 'head'), may hold values from -6 to 6
- out_weight: bfloat16 [4096, 2880], P('head'), may hold values from -0.09375 to 0.09375
- norm_gain: float32 [2880], replicated, may hold values from 0.5 to 1.5
- query_weight: bfloat16 [2880, 4096], P(None, 'head'), may hold values from -4.5280377 to 4.5280377
- key_weight: bfloat16 [2880, 512], P(None, 'head'), may hold values from -0.1118034 to 0.1118034
- value_weight: bfloat16 [2880, 512], P(None, 'head'), may hold values from -0.109375 to 0.109375
- doc_lengths: int32 [32], replicated, may hold values from 1 to 256, as said below
Outputs:
- first_branch: bfloat16 [4096, 2880], P(('ctx', 'head'))
- causal_out: bfloat16 [4096, 4096], P('ctx', 'head')
The draws below stay inside these ranges and needn't reach their ends.
Inputs may be any that keep to these rules, and one draw needn't show every extreme that they name: `doc_lengths`: the first two documents cover 256 / 2 positions together; each following pair of documents except the last two covers exactly 256 positions; the second-to-last document has exactly 256 positions and the last 128.
All inputs are finite; a program needn't handle non-finite values.
Results may differ from the reference program's by a relative error of at most 0.025.
Values may be sent and summed in bfloat16 or wider, within the bound.
No kernel may reach another device: no remote copies, remote signals or barrier semaphores. Data moves between devices by JAX's collectives and lax.ppermute only.
A program may use at most 128 MiB of HBM per device.

```python
import jax
import jax.numpy as jnp
from jax import lax

D = 2880
QH = 64
KVH = 8
HD = 64
WIN = 128
S_DEV = 256
NDOC = 32
S = 4096
DOC_MOST = 256
N_HEAD = 2


def shared_keys(key):
    return jnp.clip(jax.random.normal(jax.random.fold_in(key, 101), (S, KVH * HD), jnp.float32), -6.0, 6.0)


def shared_columns(key):
    return jnp.clip(jax.random.normal(jax.random.fold_in(key, 202), (D, KVH * HD), jnp.float32), -6.0, 6.0) * D ** (-0.5)


def draw_window_keys(key, part):
    return shared_keys(key).astype(jnp.bfloat16)


def draw_window_queries(key, part):
    key = jax.random.fold_in(key, 3)
    key_one = jax.random.fold_in(key, 0)
    values = 1.5 * jnp.clip(jax.random.normal(key_one, (S, QH * HD), jnp.float32), -6.0, 6.0)
    return values.astype(jnp.bfloat16)


def draw_key_weight(key, part):
    return shared_columns(key).astype(jnp.bfloat16)


def draw_query_weight(key, part):
    key = jax.random.fold_in(key, 5)
    key_one = jax.random.fold_in(key, 0)
    values = 1.5 * jnp.clip(jax.random.normal(key_one, (D, QH * HD), jnp.float32), -6.0, 6.0) * D ** (-0.5)
    return values.astype(jnp.bfloat16)


def draw_doc_lengths(key, part):
    key = jax.random.fold_in(key, 7)
    key_one, key_two = jax.random.split(key, 2)
    half_shard = S_DEV // 2
    opening = jax.random.randint(key_one, (1,), 1, half_shard, jnp.int32)
    middle = jax.random.randint(key_two, (NDOC // 2 - 2,), 1, S_DEV, jnp.int32)
    pairs = jnp.stack([middle, S_DEV - middle], axis=1).reshape(-1)
    closing = jnp.array([DOC_MOST, half_shard], jnp.int32)
    return jnp.concatenate([opening, half_shard - opening, pairs, closing]).astype(jnp.int32)


def shard_levels(own_key, dims, pieces, low, high):
    factor_of = 1.0
    for dim, parts in pieces:
        steps = jax.random.uniform(jax.random.fold_in(jax.random.fold_in(own_key, 6), dim), (parts,), jnp.float32, low / len(pieces), high / len(pieces))
        factor_of = factor_of * jnp.repeat(jnp.exp(steps), dims[dim] // parts).reshape((-1,) + (1,) * (len(dims) - 1 - dim))
    return factor_of


def noise(own_key, extent, width, most, shards=(), held_as=jnp.bfloat16):
    drawn = width * jax.random.normal(own_key, extent, jnp.float32)
    if shards:
        drawn = drawn * shard_levels(own_key, extent, shards, -0.22, 0.18)
    return jnp.clip(drawn, -most, most).astype(held_as)


def setup_inputs(seed: int = 0) -> dict:
    streams_of = jax.random.split(jax.random.key(seed), 10)
    window_queries = draw_window_queries(jax.random.fold_in(streams_of[9], 71), 0)
    window_keys = draw_window_keys(jax.random.fold_in(streams_of[9], 71), 0)
    window_values = noise(streams_of[2], (S, KVH * HD), 1.0, 6.0, ((0, 16), (1, 2)))
    out_weight = noise(streams_of[3], (QH * HD, D), (QH * HD) ** -0.5, 0.09375, ((0, 2),))
    norm_gain = jnp.clip(1.0 + 0.1 * jax.random.normal(streams_of[4], (D,), jnp.float32), 0.5, 1.5)
    query_weight = draw_query_weight(jax.random.fold_in(streams_of[9], 71), 0)
    key_weight = draw_key_weight(jax.random.fold_in(streams_of[9], 71), 0)
    value_weight = noise(streams_of[7], (D, KVH * HD), D ** -0.5, 0.109375, ((1, 2),))
    doc_lengths = draw_doc_lengths(jax.random.fold_in(streams_of[9], 71), 0)
    return dict(window_queries=window_queries, window_keys=window_keys, window_values=window_values, out_weight=out_weight, norm_gain=norm_gain, query_weight=query_weight, key_weight=key_weight, value_weight=value_weight, doc_lengths=doc_lengths)


def doc_index(positions, doc_lengths):
    starts = jnp.cumsum(doc_lengths) - doc_lengths
    return lax.optimization_barrier(jnp.sum((positions[:, None] >= starts[None, :]).astype(jnp.int32), axis=1)) - 1

def attend(queries, key_part, value_part, allowed):
    row_count = queries.shape[0]
    key_count = key_part.shape[0]
    kv_heads = key_part.shape[1] // HD
    groups = queries.shape[1] // key_part.shape[1]
    query_four = queries.astype(jnp.float32).reshape(row_count, kv_heads, groups, HD)
    key_three = key_part.astype(jnp.float32).reshape(key_count, kv_heads, HD)
    value_three = value_part.astype(jnp.float32).reshape(key_count, kv_heads, HD)
    scores = jnp.einsum('rkgd,lkd->kgrl', query_four, key_three) * HD ** (-0.5)
    scores = jnp.where(allowed[None, None], scores, -1e+30)
    highest = lax.optimization_barrier(jnp.max(scores, axis=-1, keepdims=True))
    exponent = jnp.where(allowed[None, None], jnp.exp(scores - highest), 0.0)
    denominator = lax.optimization_barrier(jnp.sum(exponent, axis=-1))
    pattern = exponent.astype(jnp.bfloat16).astype(jnp.float32)
    weighted = jnp.einsum('kgrl,lkd->rkgd', pattern, value_three)
    result = weighted / jnp.transpose(denominator, (2, 0, 1))[..., None]
    return result.reshape(row_count, -1).astype(jnp.bfloat16)

def reference(window_queries, window_keys, window_values, out_weight, norm_gain, query_weight, key_weight, value_weight, doc_lengths):
    block_count = S // S_DEV
    kv_width = KVH * HD
    padded_keys = jnp.concatenate([jnp.zeros((WIN, kv_width), jnp.bfloat16), window_keys], axis=0)
    padded_values = jnp.concatenate([jnp.zeros((WIN, kv_width), jnp.bfloat16), window_values], axis=0)

    def window_block(block_index):
        first_row = (block_index * S_DEV).astype(jnp.int32)
        query_pos = first_row + jnp.arange(S_DEV, dtype=jnp.int32)
        key_pos = first_row - WIN + jnp.arange(S_DEV + WIN, dtype=jnp.int32)
        query_doc = doc_index(query_pos, doc_lengths)
        key_doc = doc_index(key_pos, doc_lengths)
        allowed = (key_doc[None, :] == query_doc[:, None]) & (key_pos[None, :] <= query_pos[:, None]) & (key_pos[None, :] > query_pos[:, None] - WIN)
        queries = lax.dynamic_slice_in_dim(window_queries, first_row, S_DEV, 0)
        key_part = lax.dynamic_slice_in_dim(padded_keys, first_row, S_DEV + WIN, 0)
        value_part = lax.dynamic_slice_in_dim(padded_values, first_row, S_DEV + WIN, 0)
        return attend(queries, key_part, value_part, allowed)
    window_attn = lax.map(window_block, jnp.arange(block_count, dtype=jnp.int32)).reshape(S, QH * HD)
    group_width = QH * HD // N_HEAD
    branch = jnp.zeros((S, D), jnp.float32)
    for group in range(N_HEAD):
        partial_value = jnp.dot(window_attn[:, group * group_width:(group + 1) * group_width], out_weight[group * group_width:(group + 1) * group_width], preferred_element_type=jnp.float32)
        partial_value = lax.optimization_barrier(partial_value.astype(jnp.bfloat16)).astype(jnp.float32)
        branch = branch + partial_value
    first_branch = branch.astype(jnp.bfloat16)
    normed = (branch * lax.rsqrt(lax.optimization_barrier(jnp.mean(branch * branch, axis=-1, keepdims=True)) + 1e-05) * norm_gain).astype(jnp.bfloat16)
    causal_queries = jnp.dot(normed, query_weight, preferred_element_type=jnp.float32).astype(jnp.bfloat16)
    causal_keys = jnp.dot(normed, key_weight, preferred_element_type=jnp.float32).astype(jnp.bfloat16)
    causal_values = jnp.dot(normed, value_weight, preferred_element_type=jnp.float32).astype(jnp.bfloat16)
    lead_keys = jnp.concatenate([jnp.zeros((DOC_MOST, kv_width), jnp.bfloat16), causal_keys], axis=0)
    lead_values = jnp.concatenate([jnp.zeros((DOC_MOST, kv_width), jnp.bfloat16), causal_values], axis=0)
    group_size = QH // KVH

    def causal_block(block_index):
        first_row = (block_index * S_DEV).astype(jnp.int32)
        query_pos = first_row + jnp.arange(S_DEV, dtype=jnp.int32)
        key_pos = first_row - DOC_MOST + jnp.arange(S_DEV + DOC_MOST, dtype=jnp.int32)
        query_doc = doc_index(query_pos, doc_lengths)
        key_doc = doc_index(key_pos, doc_lengths)
        allowed = (key_doc[None, :] == query_doc[:, None]) & (key_pos[None, :] <= query_pos[:, None])
        queries = lax.dynamic_slice_in_dim(causal_queries, first_row, S_DEV, 0)
        key_part = lax.dynamic_slice_in_dim(lead_keys, first_row, S_DEV + DOC_MOST, 0)
        value_part = lax.dynamic_slice_in_dim(lead_values, first_row, S_DEV + DOC_MOST, 0)

        def one_head(kv_index):
            head_queries = lax.dynamic_slice_in_dim(queries, kv_index * group_size * HD, group_size * HD, 1)
            head_keys = lax.dynamic_slice_in_dim(key_part, kv_index * HD, HD, 1)
            head_values = lax.dynamic_slice_in_dim(value_part, kv_index * HD, HD, 1)
            return attend(head_queries, head_keys, head_values, allowed)
        per_head = lax.map(one_head, jnp.arange(KVH, dtype=jnp.int32))
        return jnp.transpose(per_head, (1, 0, 2)).reshape(S_DEV, QH * HD)
    causal_out = lax.map(causal_block, jnp.arange(block_count, dtype=jnp.int32)).reshape(S, QH * HD)
    return (first_branch, causal_out)
```

```python
import functools

import jax
import jax.numpy as jnp
from jax import lax
from jax.experimental import pallas as pl
from jax.experimental.pallas import tpu as pltpu
from jax.sharding import PartitionSpec as P

HD = 64
WIN = 128
LANES = 128
NEG = -1e30
TAIL = 16

F32 = jnp.float32
BF16 = jnp.bfloat16
MIB = 1024 * 1024


def params(mib):
    return pltpu.CompilerParams(vmem_limit_bytes=mib * MIB)


def in_vmem(array):
    return pltpu.with_memory_space_constraint(array, pltpu.VMEM)


def vmem_specs(count):
    return [pl.BlockSpec(memory_space=pltpu.VMEM)] * count


SMEM_SPEC = pl.BlockSpec(memory_space=pltpu.SMEM)


def dot(a, b, dims):
    return lax.dot_general(a, b, (dims, ((), ())), preferred_element_type=F32)


def shifted(block, axis):
    size = lax.axis_size(axis)
    return lax.ppermute(block, axis, [(i, i + 1) for i in range(size - 1)])


def swapped(block, axis):
    size = lax.axis_size(axis)
    return lax.ppermute(block, axis, [(i, size - 1 - i) for i in range(size)])


def lower_bias(lengths_ref, half, width):
    ctx = lax.axis_index("ctx")
    first = jnp.where(ctx == 0, half, 0)
    split = first + lengths_ref[2 * ctx]
    return bias_of(2 * half, half, half, first, split, width)


def upper_bias(lengths_ref, half, width):
    ctx = lax.axis_index("ctx")
    last = lengths_ref.shape[0] - 1
    split = lengths_ref[jnp.minimum(2 * ctx + 2, last)]
    split = jnp.where(ctx == lax.axis_size("ctx") - 1, 2 * half, split)
    return bias_of(half, half, 0, 0, split, width)


def bias_of(keys, rows, row_offset, first, split, width):
    key = lax.broadcasted_iota(jnp.int32, (keys, rows), 0)
    row = lax.broadcasted_iota(jnp.int32, (keys, rows), 1) + row_offset
    lowest = jnp.where(row >= split, split, first)
    if width is not None:
        lowest = jnp.maximum(lowest, row - (width - 1))
    return jnp.where((key >= lowest) & (key <= row), 0.0, NEG).astype(F32)


def stage_keys(keys, keys_ref):
    scaled = (keys.astype(F32) * HD ** (-0.5)).astype(BF16)
    lane = lax.broadcasted_iota(jnp.int32, (keys.shape[0], LANES), 1)
    zero = jnp.zeros((keys.shape[0], LANES), BF16)
    for pair in range(keys.shape[1] // LANES):
        tile = scaled[:, pair * LANES : (pair + 1) * LANES]
        turned = jnp.concatenate([tile[:, HD:], tile[:, :HD]], axis=1)
        keys_ref[2 * pair, 0] = jnp.where(lane < HD, tile, zero)
        keys_ref[2 * pair, 1] = jnp.where(lane < HD, zero, turned)
        keys_ref[2 * pair + 1, 0] = jnp.where(lane < HD, turned, zero)
        keys_ref[2 * pair + 1, 1] = jnp.where(lane < HD, zero, tile)


def stage_values(values, values_ref):
    count = values.shape[0]
    turned = jnp.transpose(values.astype(F32)).astype(BF16)
    for head in range(values.shape[1] // HD):
        values_ref[head, :HD, :] = turned[head * HD : (head + 1) * HD]
        values_ref[head, HD:, :] = jnp.ones((TAIL, count), BF16)


def attend_head(key_tile, value_tile, query_pair, bias):
    scores = dot(key_tile, query_pair, ((1,), (1,))) + bias
    highest = jnp.max(scores, axis=0, keepdims=True)
    pattern = jnp.exp(scores - highest).astype(BF16)
    weighted = dot(value_tile, pattern, ((1,), (0,)))
    return weighted[:HD] * (1.0 / weighted[HD : HD + 1])


def window_heads(q_ref, rows, keys_ref, values_ref, bias_ref, out_ref, columns):
    kv_heads = keys_ref.shape[0]
    pairs = q_ref.shape[1] // kv_heads // LANES

    def one(g, carry):
        for t in range(pairs):
            lane = pl.multiple_of((g * pairs + t) * LANES, LANES)
            query_pair = q_ref[rows, pl.ds(lane, LANES)]
            for side in range(2):
                part = attend_head(keys_ref[g, side], values_ref[g], query_pair, bias_ref[...])
                start = pl.multiple_of(lane + side * HD, HD)
                out_ref[pl.ds(start, HD), columns] = part.astype(BF16)
        return carry

    lax.fori_loop(0, kv_heads, one, 0)


def causal_heads(q_ref, rows, keys_ref, values_ref, bias_ref, out_ref, out_rows):
    kv_heads = keys_ref.shape[0]
    pairs = q_ref.shape[1] // kv_heads // LANES

    def one(g, carry):
        for t in range(pairs):
            lane = pl.multiple_of((g * pairs + t) * LANES, LANES)
            query_pair = q_ref[rows, pl.ds(lane, LANES)]
            both = [
                attend_head(keys_ref[g, side], values_ref[g], query_pair, bias_ref[...])
                for side in range(2)
            ]
            turned = jnp.transpose(jnp.concatenate(both, axis=0))
            out_ref[out_rows, pl.ds(lane, LANES)] = turned.astype(BF16)
        return carry

    lax.fori_loop(0, kv_heads, one, 0)


def window_upper_kernel(lengths_ref, q_ref, k_ref, v_ref, out_ref, keys_s, values_s, bias_s):
    half = q_ref.shape[0] // 2
    bias_s[...] = upper_bias(lengths_ref, half, WIN)
    stage_keys(k_ref[half:], keys_s)
    stage_values(v_ref[half:], values_s)
    window_heads(q_ref, pl.ds(half, half), keys_s, values_s, bias_s, out_ref, slice(None))


def window_lower_kernel(
    lengths_ref, q_ref, k_ref, v_ref, halo_ref, upper_ref, weight_ref, out_ref,
    attn_s, keys_s, values_s, bias_s, *, chunk
):
    half = q_ref.shape[0] // 2
    kv_width = k_ref.shape[1]
    bias_s[...] = lower_bias(lengths_ref, half, WIN)
    stage_keys(jnp.concatenate([halo_ref[:, :kv_width], k_ref[:half]], axis=0), keys_s)
    stage_values(jnp.concatenate([halo_ref[:, kv_width:], v_ref[:half]], axis=0), values_s)
    attn_s[:, half:] = upper_ref[...]
    window_heads(q_ref, pl.ds(0, half), keys_s, values_s, bias_s, attn_s, pl.ds(0, half))

    def project(c, carry):
        rows = pl.ds(pl.multiple_of(c * chunk, 16), chunk)
        out_ref[rows, :] = dot(weight_ref[rows, :], attn_s[...], ((1,), (0,))).astype(BF16)
        return carry

    lax.fori_loop(0, out_ref.shape[0] // chunk, project, 0)


def norm_kernel(
    own_ref, other_ref, gain_ref, kw_ref, vw_ref, branch_ref, normed_ref, kv_ref, sum_s, *, chunk
):
    width, rows = own_ref.shape
    half = rows // 2
    head = lax.axis_index("head")

    def add(c, squares):
        part = pl.ds(pl.multiple_of(c * chunk, 16), chunk)
        total = own_ref[part, :].astype(F32) + other_ref[part, :].astype(F32)
        sum_s[part, :] = total
        branch_ref[part, :] = jnp.where(head == 0, total[:, :half], total[:, half:]).astype(BF16)
        return squares + jnp.sum(total * total, axis=0, keepdims=True)

    squares = lax.fori_loop(0, width // chunk, add, jnp.zeros((1, rows), F32))
    factor = lax.rsqrt(squares * (1.0 / width) + 1e-05)
    for first in range(0, width, LANES):
        last = min(first + LANES, width)
        piece = jnp.transpose(sum_s[first:last, :] * factor) * gain_ref[:, first:last]
        normed_ref[:, first:last] = piece.astype(BF16)
    kv_width = kw_ref.shape[1]
    kv_ref[:, :kv_width] = dot(normed_ref[...], kw_ref[...], ((1,), (0,))).astype(BF16)
    kv_ref[:, kv_width:] = dot(normed_ref[...], vw_ref[...], ((1,), (0,))).astype(BF16)


def query_kernel(
    lengths_ref, normed_ref, qw_ref, kv_ref, q_ref, out_ref, keys_s, values_s, bias_s, *, chunk
):
    half = normed_ref.shape[0] // 2
    kv_width = kv_ref.shape[1] // 2
    for first in range(0, qw_ref.shape[1], chunk):
        columns = slice(first, first + chunk)
        q_ref[:, columns] = dot(normed_ref[...], qw_ref[:, columns], ((1,), (0,))).astype(BF16)
    bias_s[...] = upper_bias(lengths_ref, half, None)
    stage_keys(kv_ref[half:, :kv_width], keys_s)
    stage_values(kv_ref[half:, kv_width:], values_s)
    causal_heads(q_ref, pl.ds(half, half), keys_s, values_s, bias_s, out_ref, slice(None))


def causal_lower_kernel(
    lengths_ref, q_ref, kv_ref, halo_ref, upper_ref, out_ref, keys_s, values_s, bias_s
):
    half = q_ref.shape[0] // 2
    kv_width = kv_ref.shape[1] // 2
    bias_s[...] = lower_bias(lengths_ref, half, None)
    stage_keys(
        jnp.concatenate([halo_ref[:, :kv_width], kv_ref[:half, :kv_width]], axis=0), keys_s
    )
    stage_values(
        jnp.concatenate([halo_ref[:, kv_width:], kv_ref[:half, kv_width:]], axis=0), values_s
    )
    out_ref[half:, :] = upper_ref[...]
    causal_heads(q_ref, pl.ds(0, half), keys_s, values_s, bias_s, out_ref, pl.ds(0, half))


def attention_scratch(kv_heads, keys, rows):
    return [
        pltpu.VMEM((kv_heads, 2, keys, LANES), BF16),
        pltpu.VMEM((kv_heads, HD + TAIL, keys), BF16),
        pltpu.VMEM((keys, rows), F32),
    ]


def local(
    window_queries,
    window_keys,
    window_values,
    out_weight,
    norm_gain,
    query_weight,
    key_weight,
    value_weight,
    doc_lengths,
):
    rows, q_width = window_queries.shape
    kv_width = window_keys.shape[1]
    kv_heads = kv_width // HD
    width = out_weight.shape[1]
    half = rows // 2

    halo = shifted(jnp.concatenate([window_keys[half:], window_values[half:]], axis=1), "ctx")
    upper = pl.pallas_call(
        window_upper_kernel,
        out_shape=jax.ShapeDtypeStruct((q_width, half), BF16),
        in_specs=[SMEM_SPEC] + vmem_specs(3),
        out_specs=vmem_specs(1)[0],
        scratch_shapes=attention_scratch(kv_heads, half, half),
        compiler_params=params(16),
        name="window_upper",
    )(doc_lengths, window_queries, window_keys, window_values)
    partial = pl.pallas_call(
        functools.partial(window_lower_kernel, chunk=576),
        out_shape=jax.ShapeDtypeStruct((width, rows), BF16),
        in_specs=[SMEM_SPEC] + vmem_specs(6),
        out_specs=vmem_specs(1)[0],
        scratch_shapes=[pltpu.VMEM((q_width, rows), BF16)]
        + attention_scratch(kv_heads, 2 * half, half),
        compiler_params=params(16),
        name="window_lower",
    )(
        doc_lengths, window_queries, window_keys, window_values, halo, upper,
        in_vmem(jnp.transpose(out_weight)),
    )
    other = swapped(partial, "head")
    branch, normed, pairs = pl.pallas_call(
        functools.partial(norm_kernel, chunk=192),
        out_shape=(
            jax.ShapeDtypeStruct((width, half), BF16),
            jax.ShapeDtypeStruct((rows, width), BF16),
            jax.ShapeDtypeStruct((rows, 2 * kv_width), BF16),
        ),
        in_specs=vmem_specs(5),
        out_specs=tuple(vmem_specs(3)),
        scratch_shapes=[pltpu.VMEM((width, rows), F32)],
        compiler_params=params(16),
        name="norm_and_pairs",
    )(
        partial, other, norm_gain.reshape(1, width),
        in_vmem(key_weight), in_vmem(value_weight),
    )
    earlier = shifted(pairs[half:], "ctx")
    queries, causal_upper = pl.pallas_call(
        functools.partial(query_kernel, chunk=512),
        out_shape=(
            jax.ShapeDtypeStruct((rows, q_width), BF16),
            jax.ShapeDtypeStruct((half, q_width), BF16),
        ),
        in_specs=[SMEM_SPEC] + vmem_specs(3),
        out_specs=tuple(vmem_specs(2)),
        scratch_shapes=attention_scratch(kv_heads, half, half),
        compiler_params=params(16),
        name="queries_and_upper",
    )(doc_lengths, normed, in_vmem(query_weight), pairs)
    causal_out = pl.pallas_call(
        causal_lower_kernel,
        out_shape=jax.ShapeDtypeStruct((rows, q_width), BF16),
        in_specs=[SMEM_SPEC] + vmem_specs(4),
        out_specs=vmem_specs(1)[0],
        scratch_shapes=attention_scratch(kv_heads, 2 * half, half),
        compiler_params=params(16),
        name="causal_lower",
    )(doc_lengths, queries, pairs, earlier, causal_upper)
    return (jnp.transpose(branch), causal_out)


def solution(mesh):
    placed = (
        P("ctx", "head"),
        P("ctx", "head"),
        P("ctx", "head"),
        P("head", None),
        P(),
        P(None, "head"),
        P(None, "head"),
        P(None, "head"),
        P(),
    )
    return jax.shard_map(
        local,
        mesh=mesh,
        in_specs=placed,
        out_specs=(P(("ctx", "head"), None), P("ctx", "head")),
        check_vma=False,
    )
```

```python
import functools

import jax
import jax.numpy as jnp
from jax import lax
from jax.experimental import pallas as pl
from jax.experimental.pallas import tpu as pltpu
from jax.sharding import PartitionSpec as P

HD = 64
WIN = 128
LANES = 128
NEG = -1e30
TAIL = 16

F32 = jnp.float32
BF16 = jnp.bfloat16
MIB = 1024 * 1024


def params(mib):
    return pltpu.CompilerParams(vmem_limit_bytes=mib * MIB)


def in_vmem(array):
    return pltpu.with_memory_space_constraint(array, pltpu.VMEM)


def in_hbm(array):
    return pltpu.with_memory_space_constraint(array, pltpu.HBM)


def hbm_specs(count):
    return [pl.BlockSpec(memory_space=pltpu.HBM)] * count


def vmem_specs(count):
    return [pl.BlockSpec(memory_space=pltpu.VMEM)] * count


def dot(a, b, dims):
    return lax.dot_general(a, b, (dims, ((), ())), preferred_element_type=F32)


def shifted(block, axis):
    size = lax.axis_size(axis)
    return lax.ppermute(block, axis, [(i, (i + 1) % size) for i in range(size)])


def swapped(block, axis):
    size = lax.axis_size(axis)
    return lax.ppermute(block, axis, [(i, size - 1 - i) for i in range(size)])


def lower_bias(lengths_ref, half, width):
    ctx = lax.axis_index("ctx")
    first = jnp.where(ctx == 0, half, 0)
    split = first + lengths_ref[2 * ctx]
    return bias_of(2 * half, half, half, first, split, width)


def upper_bias(lengths_ref, half, width):
    ctx = lax.axis_index("ctx")
    last = lengths_ref.shape[0] - 1
    split = lengths_ref[jnp.minimum(2 * ctx + 2, last)]
    split = jnp.where(ctx == lax.axis_size("ctx") - 1, 2 * half, split)
    return bias_of(half, half, 0, 0, split, width)


def bias_of(keys, rows, row_offset, first, split, width):
    key = lax.broadcasted_iota(jnp.int32, (keys, rows), 0)
    row = lax.broadcasted_iota(jnp.int32, (keys, rows), 1) + row_offset
    lowest = jnp.where(row >= split, split, first)
    if width is not None:
        lowest = jnp.maximum(lowest, row - (width - 1))
    return jnp.where((key >= lowest) & (key <= row), 0.0, NEG).astype(F32)


def stage_keys(keys, keys_ref):
    scaled = (keys.astype(F32) * HD ** (-0.5)).astype(BF16)
    lane = lax.broadcasted_iota(jnp.int32, (keys.shape[0], LANES), 1)
    zero = jnp.zeros((keys.shape[0], LANES), BF16)
    for pair in range(keys.shape[1] // LANES):
        tile = scaled[:, pair * LANES : (pair + 1) * LANES]
        turned = jnp.concatenate([tile[:, HD:], tile[:, :HD]], axis=1)
        keys_ref[2 * pair, 0] = jnp.where(lane < HD, tile, zero)
        keys_ref[2 * pair, 1] = jnp.where(lane < HD, zero, turned)
        keys_ref[2 * pair + 1, 0] = jnp.where(lane < HD, turned, zero)
        keys_ref[2 * pair + 1, 1] = jnp.where(lane < HD, zero, tile)


def stage_values(values, values_ref):
    count = values.shape[0]
    turned = jnp.transpose(values.astype(F32)).astype(BF16)
    for head in range(values.shape[1] // HD):
        values_ref[head, :HD, :] = turned[head * HD : (head + 1) * HD]
        values_ref[head, HD:, :] = jnp.ones((TAIL, count), BF16)


def heads_of(g, query_tiles, keys_ref, values_ref, bias):
    count = bias.shape[0]
    queries = jnp.concatenate(query_tiles, axis=0)
    keys = jnp.concatenate([keys_ref[g, 0], keys_ref[g, 1]], axis=0)
    scores = dot(keys, queries, ((1,), (1,)))
    wide = jnp.concatenate([bias] * len(query_tiles), axis=1)
    patterns = []
    for side in range(2):
        masked = scores[side * count : (side + 1) * count] + wide
        highest = jnp.max(masked, axis=0, keepdims=True)
        patterns.append(jnp.exp(masked - highest).astype(BF16))
    pattern = jnp.concatenate(patterns, axis=1)
    weighted = dot(values_ref[g], pattern, ((1,), (0,)))
    return weighted[:HD] * (1.0 / weighted[HD : HD + 1])


def window_heads(q_ref, keys_ref, values_ref, bias_ref, out_ref):
    kv_heads = keys_ref.shape[0]
    rows = q_ref.shape[0]
    tiles = q_ref.shape[1] // kv_heads // LANES
    for g in range(kv_heads):
        lanes = [(g * tiles + t) * LANES for t in range(tiles)]
        part = heads_of(
            g, [q_ref[:, lane : lane + LANES] for lane in lanes], keys_ref, values_ref, bias_ref[...]
        ).astype(BF16)
        for side in range(2):
            for t, lane in enumerate(lanes):
                at = (side * tiles + t) * rows
                start = lane + side * HD
                out_ref[start : start + HD, :] = part[:, at : at + rows]


def causal_heads(g, query_tiles, keys_ref, values_ref, bias_ref, out_ref, first_row):
    tiles = len(query_tiles)
    rows = query_tiles[0].shape[0]
    part = heads_of(g, query_tiles, keys_ref, values_ref, bias_ref[...])
    for t in range(tiles):
        low = part[:, t * rows : (t + 1) * rows]
        high = part[:, (tiles + t) * rows : (tiles + t + 1) * rows]
        turned = jnp.transpose(jnp.concatenate([low, high], axis=0)).astype(BF16)
        lane = (g * tiles + t) * LANES
        out_ref[first_row : first_row + rows, lane : lane + LANES] = turned


def pack_kernel(k_ref, v_ref, out_ref, sems):
    half = out_ref.shape[0]
    kv_width = k_ref.shape[1]
    copies = [
        pltpu.make_async_copy(k_ref.at[pl.ds(half, half)], out_ref.at[:, pl.ds(0, kv_width)], sems.at[0]),
        pltpu.make_async_copy(
            v_ref.at[pl.ds(half, half)], out_ref.at[:, pl.ds(kv_width, kv_width)], sems.at[1]
        ),
    ]
    for copy in copies:
        copy.start()
    for copy in copies:
        copy.wait()


def window_upper_kernel(
    lengths_ref, q_ref, k_ref, v_ref, weight_ref, out_ref, held_ref,
    lengths_s, q_s, k_s, v_s, attn_s, keys_s, values_s, bias_s, sems, weight_sems, *, chunk
):
    half = q_s.shape[0]
    upper = pl.ds(half, half)
    copies = [
        pltpu.make_async_copy(lengths_ref, lengths_s, sems.at[0]),
        pltpu.make_async_copy(k_ref.at[upper], k_s, sems.at[1]),
        pltpu.make_async_copy(v_ref.at[upper], v_s, sems.at[2]),
        pltpu.make_async_copy(q_ref.at[upper], q_s, sems.at[3]),
    ]
    count = held_ref.shape[0] // chunk
    weights = [
        pltpu.make_async_copy(
            weight_ref.at[pl.ds(c * chunk, chunk)], held_ref.at[pl.ds(c * chunk, chunk)], weight_sems.at[c]
        )
        for c in range(count)
    ]
    for copy in copies + weights:
        copy.start()
    copies[0].wait()
    bias_s[...] = upper_bias(lengths_s, half, WIN)
    copies[1].wait()
    stage_keys(k_s[...], keys_s)
    copies[2].wait()
    stage_values(v_s[...], values_s)
    copies[3].wait()
    window_heads(q_s, keys_s, values_s, bias_s, attn_s)
    for c in range(count):
        weights[c].wait()
        part = slice(c * chunk, (c + 1) * chunk)
        out_ref[part, :] = dot(held_ref[part, :], attn_s[...], ((1,), (0,))).astype(BF16)


def window_lower_kernel(
    lengths_ref, q_ref, k_ref, v_ref, halo_ref, held_ref, out_ref,
    lengths_s, q_s, k_s, v_s, attn_s, keys_s, values_s, bias_s, sems, *, chunk
):
    half = q_s.shape[0]
    kv_width = k_s.shape[1]
    lower = pl.ds(0, half)
    copies = [
        pltpu.make_async_copy(lengths_ref, lengths_s, sems.at[0]),
        pltpu.make_async_copy(k_ref.at[lower], k_s, sems.at[1]),
        pltpu.make_async_copy(v_ref.at[lower], v_s, sems.at[2]),
        pltpu.make_async_copy(q_ref.at[lower], q_s, sems.at[3]),
    ]
    for copy in copies:
        copy.start()
    copies[0].wait()
    bias_s[...] = lower_bias(lengths_s, half, WIN)
    copies[1].wait()
    stage_keys(jnp.concatenate([halo_ref[:, :kv_width], k_s[...]], axis=0), keys_s)
    copies[2].wait()
    stage_values(jnp.concatenate([halo_ref[:, kv_width:], v_s[...]], axis=0), values_s)
    copies[3].wait()
    window_heads(q_s, keys_s, values_s, bias_s, attn_s)
    for first in range(0, out_ref.shape[0], chunk):
        part = slice(first, first + chunk)
        out_ref[part, :] = dot(held_ref[part, :], attn_s[...], ((1,), (0,))).astype(BF16)


def add_and_norm(own_ref, other_ref, gain_ref, branch_ref, normed_ref, first_row, sum_s, keep_ref, chunk):
    width, rows = own_ref.shape
    head = lax.axis_index("head")

    def add(c, squares):
        part = pl.ds(pl.multiple_of(c * chunk, 16), chunk)
        total = own_ref[part, :].astype(F32) + other_ref[part, :].astype(F32)
        sum_s[part, :] = total
        rounded = total.astype(BF16)
        if keep_ref is not None:
            rounded = jnp.where(head == 0, rounded, keep_ref[part, :])
        branch_ref[part, :] = rounded
        return squares + jnp.sum(total * total, axis=0, keepdims=True)

    squares = lax.fori_loop(0, width // chunk, add, jnp.zeros((1, rows), F32))
    factor = lax.rsqrt(squares * (1.0 / width) + 1e-05)
    for first in range(0, width, LANES):
        last = min(first + LANES, width)
        piece = jnp.transpose(sum_s[first:last, :] * factor) * gain_ref[:, first:last]
        normed_ref[first_row : first_row + rows, first:last] = piece.astype(BF16)


def norm_upper_kernel(
    own_ref, other_ref, gain_ref, kw_ref, vw_ref, branch_ref, normed_ref, kv_ref, sum_s, *, chunk
):
    add_and_norm(own_ref, other_ref, gain_ref, branch_ref, normed_ref, 0, sum_s, None, chunk)
    kv_width = kw_ref.shape[1]
    kv_ref[:, :kv_width] = dot(normed_ref[...], kw_ref[...], ((1,), (0,))).astype(BF16)
    kv_ref[:, kv_width:] = dot(normed_ref[...], vw_ref[...], ((1,), (0,))).astype(BF16)


def causal_upper_kernel(
    lengths_ref, own_ref, other_ref, gain_ref, kw_ref, vw_ref, qw_ref, kept_ref, normed_ref, kv_up_ref,
    branch_ref, q_ref, kv_ref, out_ref, lengths_s, normed_s, sum_s, keys_s, values_s, bias_s, sem, *, chunk
):
    half = own_ref.shape[1]
    kv_width = kw_ref.shape[1]
    copy = pltpu.make_async_copy(lengths_ref, lengths_s, sem)
    copy.start()
    normed_s[half:, :] = normed_ref[...]
    add_and_norm(own_ref, other_ref, gain_ref, branch_ref, normed_s, 0, sum_s, kept_ref, chunk)
    copy.wait()
    bias_s[...] = upper_bias(lengths_s, half, None)
    stage_keys(kv_up_ref[:, :kv_width], keys_s)
    stage_values(kv_up_ref[:, kv_width:], values_s)
    kv_heads = keys_s.shape[0]
    group = qw_ref.shape[1] // kv_heads
    for g in range(kv_heads):
        columns = slice(g * group, (g + 1) * group)
        queries = dot(normed_s[...], qw_ref[:, columns], ((1,), (0,))).astype(BF16)
        q_ref[:, columns] = queries[:half]
        tiles = [queries[half:, at : at + LANES] for at in range(0, group, LANES)]
        causal_heads(g, tiles, keys_s, values_s, bias_s, out_ref, 0)
    kv_ref[:, :kv_width] = dot(normed_s[:half, :], kw_ref[...], ((1,), (0,))).astype(BF16)
    kv_ref[:, kv_width:] = dot(normed_s[:half, :], vw_ref[...], ((1,), (0,))).astype(BF16)


def causal_lower_kernel(
    lengths_ref, q_ref, kv_ref, halo_ref, upper_ref, out_ref, lengths_s, keys_s, values_s, bias_s, sem
):
    half = q_ref.shape[0]
    kv_width = kv_ref.shape[1] // 2
    copy = pltpu.make_async_copy(lengths_ref, lengths_s, sem)
    copy.start()
    stage_keys(jnp.concatenate([halo_ref[:, :kv_width], kv_ref[:, :kv_width]], axis=0), keys_s)
    stage_values(jnp.concatenate([halo_ref[:, kv_width:], kv_ref[:, kv_width:]], axis=0), values_s)
    out_ref[half:, :] = upper_ref[...]
    copy.wait()
    bias_s[...] = lower_bias(lengths_s, half, None)
    kv_heads = keys_s.shape[0]
    group = q_ref.shape[1] // kv_heads
    for g in range(kv_heads):
        tiles = [q_ref[:, at : at + LANES] for at in range(g * group, (g + 1) * group, LANES)]
        causal_heads(g, tiles, keys_s, values_s, bias_s, out_ref, 0)


def attention_scratch(kv_heads, keys, rows):
    return [
        pltpu.VMEM((kv_heads, 2, keys, LANES), BF16),
        pltpu.VMEM((kv_heads, HD + TAIL, keys), BF16),
        pltpu.VMEM((keys, rows), F32),
    ]


def local(
    window_queries,
    window_keys,
    window_values,
    out_weight,
    norm_gain,
    query_weight,
    key_weight,
    value_weight,
    doc_lengths,
):
    rows, q_width = window_queries.shape
    kv_width = window_keys.shape[1]
    kv_heads = kv_width // HD
    width = out_weight.shape[1]
    half = rows // 2
    chunk = 576
    dma = pltpu.SemaphoreType.DMA
    lengths_s = pltpu.SMEM(doc_lengths.shape, jnp.int32)
    lengths, queries, keys, values = [
        in_hbm(x) for x in (doc_lengths, window_queries, window_keys, window_values)
    ]

    packed = pl.pallas_call(
        pack_kernel,
        out_shape=jax.ShapeDtypeStruct((half, 2 * kv_width), BF16),
        in_specs=hbm_specs(2),
        out_specs=vmem_specs(1)[0],
        scratch_shapes=[dma((2,))],
        compiler_params=params(16),
        name="pack",
    )(keys, values)
    halo = shifted(packed, "ctx")
    inputs_s = [
        lengths_s,
        pltpu.VMEM((half, q_width), BF16),
        pltpu.VMEM((half, kv_width), BF16),
        pltpu.VMEM((half, kv_width), BF16),
        pltpu.VMEM((q_width, half), BF16),
    ]
    own_upper, held = pl.pallas_call(
        functools.partial(window_upper_kernel, chunk=chunk),
        out_shape=(pltpu.VMEM((width, half), BF16), pltpu.VMEM((width, q_width), BF16)),
        in_specs=hbm_specs(5),
        out_specs=tuple(vmem_specs(2)),
        scratch_shapes=inputs_s + attention_scratch(kv_heads, half, half) + [dma((4,)), dma((width // chunk,))],
        compiler_params=params(16),
        name="window_upper",
    )(lengths, queries, keys, values, in_hbm(jnp.transpose(out_weight)))
    other_upper = swapped(own_upper, "head")
    own_lower = pl.pallas_call(
        functools.partial(window_lower_kernel, chunk=chunk),
        out_shape=pltpu.VMEM((width, half), BF16),
        in_specs=hbm_specs(4) + vmem_specs(2),
        out_specs=vmem_specs(1)[0],
        scratch_shapes=inputs_s + attention_scratch(kv_heads, 2 * half, half) + [dma((4,))],
        compiler_params=params(16),
        name="window_lower",
    )(lengths, queries, keys, values, in_vmem(halo), held)
    other_lower = swapped(own_lower, "head")
    gain = norm_gain.reshape(1, width)
    key_held, value_held, query_held = [in_vmem(x) for x in (key_weight, value_weight, query_weight)]
    branch_upper, normed_upper, pairs_upper = pl.pallas_call(
        functools.partial(norm_upper_kernel, chunk=192),
        out_shape=(
            pltpu.VMEM((width, half), BF16),
            pltpu.VMEM((half, width), BF16),
            pltpu.VMEM((half, 2 * kv_width), BF16),
        ),
        in_specs=vmem_specs(5),
        out_specs=tuple(vmem_specs(3)),
        scratch_shapes=[pltpu.VMEM((width, half), F32)],
        compiler_params=params(16),
        name="norm_upper",
    )(own_upper, other_upper, gain, key_held, value_held)
    earlier = shifted(pairs_upper, "ctx")
    branch, causal_queries, pairs_lower, causal_upper = pl.pallas_call(
        functools.partial(causal_upper_kernel, chunk=192),
        out_shape=(
            jax.ShapeDtypeStruct((width, half), BF16),
            pltpu.VMEM((half, q_width), BF16),
            pltpu.VMEM((half, 2 * kv_width), BF16),
            pltpu.VMEM((half, q_width), BF16),
        ),
        in_specs=hbm_specs(1) + vmem_specs(9),
        out_specs=tuple(vmem_specs(4)),
        scratch_shapes=[lengths_s, pltpu.VMEM((rows, width), BF16), pltpu.VMEM((width, half), F32)]
        + attention_scratch(kv_heads, half, half)
        + [dma],
        compiler_params=params(16),
        name="causal_upper",
    )(
        lengths, own_lower, other_lower, gain, key_held, value_held, query_held,
        branch_upper, normed_upper, pairs_upper,
    )
    causal_out = pl.pallas_call(
        causal_lower_kernel,
        out_shape=jax.ShapeDtypeStruct((rows, q_width), BF16),
        in_specs=hbm_specs(1) + vmem_specs(4),
        out_specs=vmem_specs(1)[0],
        scratch_shapes=[lengths_s] + attention_scratch(kv_heads, 2 * half, half) + [dma],
        compiler_params=params(16),
        name="causal_lower",
    )(lengths, causal_queries, pairs_lower, in_vmem(earlier), causal_upper)
    return (jnp.transpose(branch), causal_out)


def solution(mesh):
    placed = (
        P("ctx", "head"),
        P("ctx", "head"),
        P("ctx", "head"),
        P("head", None),
        P(),
        P(None, "head"),
        P(None, "head"),
        P(None, "head"),
        P(),
    )
    return jax.shard_map(
        local,
        mesh=mesh,
        in_specs=placed,
        out_specs=(P(("ctx", "head"), None), P("ctx", "head")),
        check_vma=False,
    )
```

```python
import functools

import jax
import jax.numpy as jnp
from jax import lax
from jax.experimental import pallas as pl
from jax.experimental.pallas import tpu as pltpu
from jax.sharding import PartitionSpec as P

HD = 64
WIN = 128
LANES = 128
NEG = -1e30
TAIL = 16

F32 = jnp.float32
BF16 = jnp.bfloat16
MIB = 1024 * 1024


def params(mib):
    return pltpu.CompilerParams(vmem_limit_bytes=mib * MIB)


def in_vmem(array):
    return pltpu.with_memory_space_constraint(array, pltpu.VMEM)


def in_hbm(array):
    return pltpu.with_memory_space_constraint(array, pltpu.HBM)


def hbm_specs(count):
    return [pl.BlockSpec(memory_space=pltpu.HBM)] * count


def vmem_specs(count):
    return [pl.BlockSpec(memory_space=pltpu.VMEM)] * count


def dot(a, b, dims):
    return lax.dot_general(a, b, (dims, ((), ())), preferred_element_type=F32)


def shifted(block, axis):
    size = lax.axis_size(axis)
    return lax.ppermute(block, axis, [(i, (i + 1) % size) for i in range(size)])


def swapped(block, axis):
    size = lax.axis_size(axis)
    return lax.ppermute(block, axis, [(i, size - 1 - i) for i in range(size)])


def lower_bias(lengths_ref, half, width):
    ctx = lax.axis_index("ctx")
    first = jnp.where(ctx == 0, half, 0)
    split = first + lengths_ref[2 * ctx]
    return bias_of(2 * half, half, half, first, split, width)


def upper_bias(lengths_ref, half, width):
    ctx = lax.axis_index("ctx")
    last = lengths_ref.shape[0] - 1
    split = lengths_ref[jnp.minimum(2 * ctx + 2, last)]
    split = jnp.where(ctx == lax.axis_size("ctx") - 1, 2 * half, split)
    return bias_of(half, half, 0, 0, split, width)


def bias_of(keys, rows, row_offset, first, split, width):
    key = lax.broadcasted_iota(jnp.int32, (keys, rows), 0)
    row = lax.broadcasted_iota(jnp.int32, (keys, rows), 1) + row_offset
    lowest = jnp.where(row >= split, split, first)
    if width is not None:
        lowest = jnp.maximum(lowest, row - (width - 1))
    return jnp.where((key >= lowest) & (key <= row), 0.0, NEG).astype(F32)


def stage_keys(keys, keys_ref):
    scaled = (keys.astype(F32) * HD ** (-0.5)).astype(BF16)
    lane = lax.broadcasted_iota(jnp.int32, (keys.shape[0], LANES), 1)
    zero = jnp.zeros((keys.shape[0], LANES), BF16)
    for pair in range(keys.shape[1] // LANES):
        tile = scaled[:, pair * LANES : (pair + 1) * LANES]
        turned = jnp.concatenate([tile[:, HD:], tile[:, :HD]], axis=1)
        keys_ref[2 * pair, 0] = jnp.where(lane < HD, tile, zero)
        keys_ref[2 * pair, 1] = jnp.where(lane < HD, zero, turned)
        keys_ref[2 * pair + 1, 0] = jnp.where(lane < HD, turned, zero)
        keys_ref[2 * pair + 1, 1] = jnp.where(lane < HD, zero, tile)


def stage_values(values, values_ref):
    count = values.shape[0]
    turned = jnp.transpose(values.astype(F32)).astype(BF16)
    for head in range(values.shape[1] // HD):
        values_ref[head, :HD, :] = turned[head * HD : (head + 1) * HD]
        values_ref[head, HD:, :] = jnp.ones((TAIL, count), BF16)


class Unit:
    def __init__(self, g, lane):
        self.g, self.lane = g, lane


def units_of(kv_heads, q_width):
    step = 2 * LANES
    group = q_width // kv_heads
    return [Unit(lane // group, lane) for lane in range(0, q_width, step)]


def unit_scores(queries, unit, keys_ref):
    stacked = jnp.concatenate([queries[:, :LANES], queries[:, LANES:]], axis=0)
    keys = jnp.concatenate([keys_ref[unit.g, 0], keys_ref[unit.g, 1]], axis=0)
    return dot(keys, stacked, ((1,), (1,)))


def unit_attend(scores, unit, values_ref, bias):
    count = bias.shape[0]
    wide = jnp.concatenate([bias, bias], axis=1)
    patterns = []
    for side in range(2):
        masked = scores[side * count : (side + 1) * count] + wide
        highest = jnp.max(masked, axis=0, keepdims=True)
        patterns.append(jnp.exp(masked - highest).astype(BF16))
    weighted = dot(values_ref[unit.g], jnp.concatenate(patterns, axis=1), ((1,), (0,)))
    return weighted[:HD] * (1.0 / weighted[HD : HD + 1])


def pipelined(units, queries_of, keys_ref, values_ref, bias, write):
    count = len(units)
    queries = queries_of(units[0])
    scores = unit_scores(queries, units[0], keys_ref)
    queries = queries_of(units[1])
    for i, unit in enumerate(units):
        now = scores
        if i + 1 < count:
            scores = unit_scores(queries, units[i + 1], keys_ref)
        if i + 2 < count:
            queries = queries_of(units[i + 2])
        write(unit, unit_attend(now, unit, values_ref, bias))


def window_heads(queries_of, keys_ref, values_ref, bias_ref, out_ref, q_width):
    def write(unit, part):
        rows = part.shape[1] // 4
        rounded = part.astype(BF16)
        for side in range(2):
            for t in range(2):
                at = (side * 2 + t) * rows
                start = unit.lane + t * LANES + side * HD
                out_ref[start : start + HD, :] = rounded[:, at : at + rows]

    pipelined(units_of(keys_ref.shape[0], q_width), queries_of, keys_ref, values_ref, bias_ref[...], write)


def causal_heads(queries_of, keys_ref, values_ref, bias_ref, out_ref, q_width, ready):
    def write(unit, part):
        rows = part.shape[1] // 4
        for t in range(2):
            low = part[:, t * rows : (t + 1) * rows]
            high = part[:, (2 + t) * rows : (3 + t) * rows]
            lane = unit.lane + t * LANES
            out_ref[:, lane : lane + LANES] = jnp.transpose(
                jnp.concatenate([low, high], axis=0)
            ).astype(BF16)
        ready(unit)

    pipelined(units_of(keys_ref.shape[0], q_width), queries_of, keys_ref, values_ref, bias_ref[...], write)


def pack_kernel(k_ref, v_ref, out_ref, sems):
    half = out_ref.shape[0]
    kv_width = k_ref.shape[1]
    copies = [
        pltpu.make_async_copy(k_ref.at[pl.ds(half, half)], out_ref.at[:, pl.ds(0, kv_width)], sems.at[0]),
        pltpu.make_async_copy(
            v_ref.at[pl.ds(half, half)], out_ref.at[:, pl.ds(kv_width, kv_width)], sems.at[1]
        ),
    ]
    for copy in copies:
        copy.start()
    for copy in copies:
        copy.wait()


def window_upper_kernel(
    lengths_ref, q_ref, k_ref, v_ref, weight_ref, gain_ref,
    out_ref, held_ref, q_held, k_held, v_held, window_bias, upper_causal, lower_causal, gain_held,
    lengths_s, attn_s, keys_s, values_s, bias_s, sems, weight_sems, *, chunk
):
    half = out_ref.shape[1]
    upper, lower = pl.ds(half, half), pl.ds(0, half)
    first = [
        pltpu.make_async_copy(lengths_ref, lengths_s, sems.at[0]),
        pltpu.make_async_copy(k_ref.at[upper], k_held.at[upper], sems.at[1]),
        pltpu.make_async_copy(v_ref.at[upper], v_held.at[upper], sems.at[2]),
        pltpu.make_async_copy(q_ref.at[upper], q_held.at[upper], sems.at[3]),
    ]
    count = held_ref.shape[0] // chunk
    weights = [
        pltpu.make_async_copy(
            weight_ref.at[pl.ds(c * chunk, chunk)], held_ref.at[pl.ds(c * chunk, chunk)], weight_sems.at[c]
        )
        for c in range(count)
    ]
    last = [
        pltpu.make_async_copy(k_ref.at[lower], k_held.at[lower], sems.at[4]),
        pltpu.make_async_copy(v_ref.at[lower], v_held.at[lower], sems.at[5]),
        pltpu.make_async_copy(q_ref.at[lower], q_held.at[lower], sems.at[6]),
        pltpu.make_async_copy(gain_ref, gain_held, sems.at[7]),
    ]
    for copy in first + weights + last:
        copy.start()
    first[0].wait()
    bias_s[...] = upper_bias(lengths_s, half, WIN)
    first[1].wait()
    stage_keys(k_held[half:], keys_s)
    first[2].wait()
    stage_values(v_held[half:], values_s)
    first[3].wait()

    def queries_of(unit):
        return q_held[half:, unit.lane : unit.lane + 2 * LANES]

    window_heads(queries_of, keys_s, values_s, bias_s, attn_s, q_held.shape[1])
    window_bias[...] = lower_bias(lengths_s, half, WIN)
    upper_causal[...] = upper_bias(lengths_s, half, None)
    lower_causal[...] = lower_bias(lengths_s, half, None)
    for c in range(count):
        weights[c].wait()
        part = slice(c * chunk, (c + 1) * chunk)
        out_ref[part, :] = dot(held_ref[part, :], attn_s[...], ((1,), (0,))).astype(BF16)
    for copy in last:
        copy.wait()


def window_lower_kernel(
    q_ref, k_ref, v_ref, halo_ref, held_ref, bias_ref, kw_ref, vw_ref, qw_ref,
    out_ref, key_held, value_held, query_held, attn_s, keys_s, values_s, sems, *, chunk
):
    half = halo_ref.shape[0]
    kv_width = k_ref.shape[1]
    copies = [
        pltpu.make_async_copy(kw_ref, key_held, sems.at[0]),
        pltpu.make_async_copy(vw_ref, value_held, sems.at[1]),
        pltpu.make_async_copy(qw_ref.at[:, pl.ds(0, query_held.shape[1])], query_held, sems.at[2]),
    ]
    for copy in copies:
        copy.start()
    stage_keys(jnp.concatenate([halo_ref[:, :kv_width], k_ref[:half]], axis=0), keys_s)
    stage_values(jnp.concatenate([halo_ref[:, kv_width:], v_ref[:half]], axis=0), values_s)

    def queries_of(unit):
        return q_ref[:half, unit.lane : unit.lane + 2 * LANES]

    window_heads(queries_of, keys_s, values_s, bias_ref, attn_s, q_ref.shape[1])
    for first in range(0, out_ref.shape[0], chunk):
        part = slice(first, first + chunk)
        out_ref[part, :] = dot(held_ref[part, :], attn_s[...], ((1,), (0,))).astype(BF16)
    for copy in copies:
        copy.wait()


def add_and_norm(own_ref, other_ref, gain_ref, branch_ref, normed_ref, first_row, sum_s, keep_ref, chunk):
    width, rows = own_ref.shape
    head = lax.axis_index("head")

    def add(c, squares):
        part = pl.ds(pl.multiple_of(c * chunk, 16), chunk)
        total = own_ref[part, :].astype(F32) + other_ref[part, :].astype(F32)
        sum_s[part, :] = total
        rounded = total.astype(BF16)
        if keep_ref is not None:
            rounded = jnp.where(head == 0, rounded, keep_ref[part, :])
        branch_ref[part, :] = rounded
        return squares + jnp.sum(total * total, axis=0, keepdims=True)

    squares = lax.fori_loop(0, width // chunk, add, jnp.zeros((1, rows), F32))
    factor = lax.rsqrt(squares * (1.0 / width) + 1e-05)
    for first in range(0, width, LANES):
        last = min(first + LANES, width)
        piece = jnp.transpose(sum_s[first:last, :] * factor) * gain_ref[first:last][None, :]
        normed_ref[first_row : first_row + rows, first:last] = piece.astype(BF16)


def norm_upper_kernel(
    own_ref, other_ref, gain_ref, kw_ref, vw_ref, branch_ref, normed_ref, kv_ref, sum_s, *, chunk
):
    add_and_norm(own_ref, other_ref, gain_ref, branch_ref, normed_ref, 0, sum_s, None, chunk)
    kv_width = kw_ref.shape[1]
    kv_ref[:, :kv_width] = dot(normed_ref[...], kw_ref[...], ((1,), (0,))).astype(BF16)
    kv_ref[:, kv_width:] = dot(normed_ref[...], vw_ref[...], ((1,), (0,))).astype(BF16)


def causal_upper_kernel(
    own_ref, other_ref, gain_ref, kw_ref, vw_ref, query_held, kept_ref, normed_ref, kv_up_ref, bias_ref,
    qw_ref, branch_ref, q_ref, kv_ref, out_ref,
    rest_s, branch_s, out_s, normed_s, sum_s, keys_s, values_s, sems, *, chunk
):
    half = own_ref.shape[1]
    kv_width = kw_ref.shape[1]
    q_width = qw_ref.shape[1]
    present = query_held.shape[1]
    rest_in = pltpu.make_async_copy(
        qw_ref.at[:, pl.ds(present, q_width - present)], rest_s, sems.at[2]
    )
    rest_in.start()
    normed_s[half:, :] = normed_ref[...]
    add_and_norm(own_ref, other_ref, gain_ref, branch_s, normed_s, 0, sum_s, kept_ref, chunk)
    branch_out = pltpu.make_async_copy(branch_s, branch_ref, sems.at[0])
    branch_out.start()
    stage_keys(kv_up_ref[:, :kv_width], keys_s)
    stage_values(kv_up_ref[:, kv_width:], values_s)

    def queries_of(unit):
        columns = slice(unit.lane, unit.lane + 2 * LANES)
        if unit.lane == present:
            rest_in.wait()
        if unit.lane < present:
            weight = query_held[:, columns]
        else:
            weight = rest_s[:, unit.lane - present : unit.lane - present + 2 * LANES]
        queries = dot(normed_s[...], weight, ((1,), (0,))).astype(BF16)
        q_ref[:, columns] = queries[:half]
        return queries[half:]

    causal_heads(queries_of, keys_s, values_s, bias_ref, out_s, q_width, lambda unit: None)
    upper_out = pltpu.make_async_copy(out_s, out_ref.at[pl.ds(half, half)], sems.at[1])
    upper_out.start()
    kv_ref[:, :kv_width] = dot(normed_s[:half, :], kw_ref[...], ((1,), (0,))).astype(BF16)
    kv_ref[:, kv_width:] = dot(normed_s[:half, :], vw_ref[...], ((1,), (0,))).astype(BF16)
    branch_out.wait()
    upper_out.wait()


def causal_lower_kernel(
    q_ref, kv_ref, halo_ref, bias_ref, given_ref, out_ref, out_s, keys_s, values_s, sems
):
    half, q_width = q_ref.shape
    kv_width = kv_ref.shape[1] // 2
    stage_keys(jnp.concatenate([halo_ref[:, :kv_width], kv_ref[:, :kv_width]], axis=0), keys_s)
    stage_values(jnp.concatenate([halo_ref[:, kv_width:], kv_ref[:, kv_width:]], axis=0), values_s)
    copies = []

    def queries_of(unit):
        return q_ref[:, unit.lane : unit.lane + 2 * LANES]

    def ready(unit):
        columns = pl.ds(unit.lane, 2 * LANES)
        copy = pltpu.make_async_copy(
            out_s.at[:, columns], out_ref.at[pl.ds(0, half), columns], sems.at[len(copies)]
        )
        copy.start()
        copies.append(copy)

    causal_heads(queries_of, keys_s, values_s, bias_ref, out_s, q_width, ready)
    for copy in copies:
        copy.wait()


def attention_scratch(kv_heads, keys):
    return [
        pltpu.VMEM((kv_heads, 2, keys, LANES), BF16),
        pltpu.VMEM((kv_heads, HD + TAIL, keys), BF16),
    ]


def local(
    window_queries,
    window_keys,
    window_values,
    out_weight,
    norm_gain,
    query_weight,
    key_weight,
    value_weight,
    doc_lengths,
):
    rows, q_width = window_queries.shape
    kv_width = window_keys.shape[1]
    kv_heads = kv_width // HD
    width = out_weight.shape[1]
    half = rows // 2
    chunk = 576
    dma = pltpu.SemaphoreType.DMA
    lengths, queries, keys, values = [
        in_hbm(x) for x in (doc_lengths, window_queries, window_keys, window_values)
    ]

    packed = pl.pallas_call(
        pack_kernel,
        out_shape=jax.ShapeDtypeStruct((half, 2 * kv_width), BF16),
        in_specs=hbm_specs(2),
        out_specs=vmem_specs(1)[0],
        scratch_shapes=[dma((2,))],
        compiler_params=params(16),
        name="pack",
    )(keys, values)
    halo = shifted(packed, "ctx")
    attn_s = pltpu.VMEM((q_width, half), BF16)
    (
        own_upper, held, q_held, k_held, v_held, window_bias, upper_causal, lower_causal, gain
    ) = pl.pallas_call(
        functools.partial(window_upper_kernel, chunk=chunk),
        out_shape=(
            pltpu.VMEM((width, half), BF16),
            pltpu.VMEM((width, q_width), BF16),
            pltpu.VMEM((rows, q_width), BF16),
            pltpu.VMEM((rows, kv_width), BF16),
            pltpu.VMEM((rows, kv_width), BF16),
            pltpu.VMEM((rows, half), F32),
            pltpu.VMEM((half, half), F32),
            pltpu.VMEM((rows, half), F32),
            pltpu.VMEM((width,), F32),
        ),
        in_specs=hbm_specs(6),
        out_specs=tuple(vmem_specs(9)),
        scratch_shapes=[pltpu.SMEM(doc_lengths.shape, jnp.int32), attn_s]
        + attention_scratch(kv_heads, half)
        + [pltpu.VMEM((half, half), F32), dma((8,)), dma((width // chunk,))],
        compiler_params=params(16),
        name="window_upper",
    )(lengths, queries, keys, values, in_hbm(jnp.transpose(out_weight)), in_hbm(norm_gain))
    key_weight, value_weight, query_weight = [
        in_hbm(x) for x in (key_weight, value_weight, query_weight)
    ]
    other_upper = swapped(own_upper, "head")
    own_lower, key_held, value_held, query_held = pl.pallas_call(
        functools.partial(window_lower_kernel, chunk=chunk),
        out_shape=(
            pltpu.VMEM((width, half), BF16),
            pltpu.VMEM((width, kv_width), BF16),
            pltpu.VMEM((width, kv_width), BF16),
            pltpu.VMEM((width, q_width // 2), BF16),
        ),
        in_specs=vmem_specs(6) + hbm_specs(3),
        out_specs=tuple(vmem_specs(4)),
        scratch_shapes=[attn_s] + attention_scratch(kv_heads, rows) + [dma((3,))],
        compiler_params=params(16),
        name="window_lower",
    )(
        q_held, k_held, v_held, in_vmem(halo), held, window_bias,
        key_weight, value_weight, query_weight,
    )
    other_lower = swapped(own_lower, "head")
    branch_upper, normed_upper, pairs_upper = pl.pallas_call(
        functools.partial(norm_upper_kernel, chunk=192),
        out_shape=(
            pltpu.VMEM((width, half), BF16),
            pltpu.VMEM((half, width), BF16),
            pltpu.VMEM((half, 2 * kv_width), BF16),
        ),
        in_specs=vmem_specs(5),
        out_specs=tuple(vmem_specs(3)),
        scratch_shapes=[pltpu.VMEM((width, half), F32)],
        compiler_params=params(16),
        name="norm_upper",
    )(own_upper, other_upper, gain, key_held, value_held)
    earlier = shifted(pairs_upper, "ctx")
    branch, causal_queries, pairs_lower, causal_out = pl.pallas_call(
        functools.partial(causal_upper_kernel, chunk=192),
        out_shape=(
            pltpu.HBM((width, half), BF16),
            pltpu.VMEM((half, q_width), BF16),
            pltpu.VMEM((half, 2 * kv_width), BF16),
            pltpu.HBM((rows, q_width), BF16),
        ),
        in_specs=vmem_specs(10) + hbm_specs(1),
        out_specs=(hbm_specs(1)[0], *vmem_specs(2), hbm_specs(1)[0]),
        scratch_shapes=[
            pltpu.VMEM((width, q_width // 2), BF16),
            pltpu.VMEM((width, half), BF16),
            pltpu.VMEM((half, q_width), BF16),
            pltpu.VMEM((rows, width), BF16),
            pltpu.VMEM((width, half), F32),
        ]
        + attention_scratch(kv_heads, half)
        + [dma((3,))],
        compiler_params=params(20),
        name="causal_upper",
    )(
        own_lower, other_lower, gain, key_held, value_held, query_held,
        branch_upper, normed_upper, pairs_upper, upper_causal, query_weight,
    )
    causal_out = pl.pallas_call(
        causal_lower_kernel,
        out_shape=pltpu.HBM((rows, q_width), BF16),
        in_specs=vmem_specs(4) + hbm_specs(1),
        out_specs=hbm_specs(1)[0],
        scratch_shapes=[pltpu.VMEM((half, q_width), BF16)]
        + attention_scratch(kv_heads, rows)
        + [dma((q_width // (2 * LANES),))],
        input_output_aliases={4: 0},
        compiler_params=params(16),
        name="causal_lower",
    )(causal_queries, pairs_lower, in_vmem(earlier), lower_causal, causal_out)
    return (jnp.transpose(branch), causal_out)


def solution(mesh):
    placed = (
        P("ctx", "head"),
        P("ctx", "head"),
        P("ctx", "head"),
        P("head", None),
        P(),
        P(None, "head"),
        P(None, "head"),
        P(None, "head"),
        P(),
    )
    return jax.shard_map(
        local,
        mesh=mesh,
        in_specs=placed,
        out_specs=(P(("ctx", "head"), None), P("ctx", "head")),
        check_vma=False,
    )
```

```python
import functools

import jax
import jax.numpy as jnp
from jax import lax
from jax.experimental import pallas as pl
from jax.experimental.pallas import tpu as pltpu
from jax.sharding import PartitionSpec as P

HD = 64
WIN = 128
LANES = 128
NEG = -1e30
TAIL = 16

F32 = jnp.float32
BF16 = jnp.bfloat16
MIB = 1024 * 1024


def params(mib):
    return pltpu.CompilerParams(vmem_limit_bytes=mib * MIB)


def in_vmem(array):
    return pltpu.with_memory_space_constraint(array, pltpu.VMEM)


def in_hbm(array):
    return pltpu.with_memory_space_constraint(array, pltpu.HBM)


def hbm_specs(count):
    return [pl.BlockSpec(memory_space=pltpu.HBM)] * count


def vmem_specs(count):
    return [pl.BlockSpec(memory_space=pltpu.VMEM)] * count


def dot(a, b, dims):
    return lax.dot_general(a, b, (dims, ((), ())), preferred_element_type=F32)


def shifted(block, axis):
    size = lax.axis_size(axis)
    return lax.ppermute(block, axis, [(i, (i + 1) % size) for i in range(size)])


def swapped(block, axis):
    size = lax.axis_size(axis)
    return lax.ppermute(block, axis, [(i, size - 1 - i) for i in range(size)])


def lower_bias(lengths_ref, half, width):
    ctx = lax.axis_index("ctx")
    first = jnp.where(ctx == 0, half, 0)
    split = first + lengths_ref[2 * ctx]
    return bias_of(2 * half, half, half, first, split, width)


def upper_bias(lengths_ref, half, width):
    ctx = lax.axis_index("ctx")
    last = lengths_ref.shape[0] - 1
    split = lengths_ref[jnp.minimum(2 * ctx + 2, last)]
    split = jnp.where(ctx == lax.axis_size("ctx") - 1, 2 * half, split)
    return bias_of(half, half, 0, 0, split, width)


def bias_of(keys, rows, row_offset, first, split, width):
    key = lax.broadcasted_iota(jnp.int32, (keys, rows), 0)
    row = lax.broadcasted_iota(jnp.int32, (keys, rows), 1) + row_offset
    lowest = jnp.where(row >= split, split, first)
    if width is not None:
        lowest = jnp.maximum(lowest, row - (width - 1))
    return jnp.where((key >= lowest) & (key <= row), 0.0, NEG).astype(F32)


def stage_keys(keys, keys_ref):
    scaled = (keys.astype(F32) * HD ** (-0.5)).astype(BF16)
    lane = lax.broadcasted_iota(jnp.int32, (keys.shape[0], LANES), 1)
    zero = jnp.zeros((keys.shape[0], LANES), BF16)
    for pair in range(keys.shape[1] // LANES):
        tile = scaled[:, pair * LANES : (pair + 1) * LANES]
        turned = jnp.concatenate([tile[:, HD:], tile[:, :HD]], axis=1)
        keys_ref[2 * pair, 0] = jnp.where(lane < HD, tile, zero)
        keys_ref[2 * pair, 1] = jnp.where(lane < HD, zero, turned)
        keys_ref[2 * pair + 1, 0] = jnp.where(lane < HD, turned, zero)
        keys_ref[2 * pair + 1, 1] = jnp.where(lane < HD, zero, tile)


def stage_values(values, values_ref):
    count = values.shape[0]
    turned = jnp.transpose(values.astype(F32)).astype(BF16)
    for head in range(values.shape[1] // HD):
        values_ref[head, :HD, :] = turned[head * HD : (head + 1) * HD]
        values_ref[head, HD:, :] = jnp.ones((TAIL, count), BF16)


class Unit:
    def __init__(self, g, lane):
        self.g, self.lane = g, lane


def units_of(kv_heads, q_width):
    step = 2 * LANES
    group = q_width // kv_heads
    return [Unit(lane // group, lane) for lane in range(0, q_width, step)]


def unit_scores(queries, unit, keys_ref):
    stacked = jnp.concatenate([queries[:, :LANES], queries[:, LANES:]], axis=0)
    keys = jnp.concatenate([keys_ref[unit.g, 0], keys_ref[unit.g, 1]], axis=0)
    return dot(keys, stacked, ((1,), (1,)))


def unit_attend(scores, unit, values_ref, bias):
    count = bias.shape[0]
    wide = jnp.concatenate([bias, bias], axis=1)
    patterns = []
    for side in range(2):
        masked = scores[side * count : (side + 1) * count] + wide
        highest = jnp.max(masked, axis=0, keepdims=True)
        patterns.append(jnp.exp(masked - highest).astype(BF16))
    weighted = dot(values_ref[unit.g], jnp.concatenate(patterns, axis=1), ((1,), (0,)))
    return weighted[:HD] * (1.0 / weighted[HD : HD + 1])


def pipelined(units, queries_of, keys_ref, values_ref, bias, write):
    count = len(units)
    queries = queries_of(units[0])
    scores = unit_scores(queries, units[0], keys_ref)
    queries = queries_of(units[1])
    for i, unit in enumerate(units):
        now = scores
        if i + 1 < count:
            scores = unit_scores(queries, units[i + 1], keys_ref)
        if i + 2 < count:
            queries = queries_of(units[i + 2])
        write(unit, unit_attend(now, unit, values_ref, bias))


def window_heads(queries_of, keys_ref, values_ref, bias_ref, out_ref, q_width):
    def write(unit, part):
        rows = part.shape[1] // 4
        rounded = part.astype(BF16)
        for side in range(2):
            for t in range(2):
                at = (side * 2 + t) * rows
                start = unit.lane + t * LANES + side * HD
                out_ref[start : start + HD, :] = rounded[:, at : at + rows]

    pipelined(units_of(keys_ref.shape[0], q_width), queries_of, keys_ref, values_ref, bias_ref[...], write)


def causal_heads(queries_of, keys_ref, values_ref, bias_ref, out_ref, q_width, ready):
    def write(unit, part):
        rows = part.shape[1] // 4
        for t in range(2):
            low = part[:, t * rows : (t + 1) * rows]
            high = part[:, (2 + t) * rows : (3 + t) * rows]
            lane = unit.lane + t * LANES
            out_ref[:, lane : lane + LANES] = jnp.transpose(
                jnp.concatenate([low, high], axis=0)
            ).astype(BF16)
        ready(unit)

    pipelined(units_of(keys_ref.shape[0], q_width), queries_of, keys_ref, values_ref, bias_ref[...], write)


def pack_kernel(k_ref, v_ref, out_ref, sems):
    half = out_ref.shape[0]
    kv_width = k_ref.shape[1]
    copies = [
        pltpu.make_async_copy(k_ref.at[pl.ds(half, half)], out_ref.at[:, pl.ds(0, kv_width)], sems.at[0]),
        pltpu.make_async_copy(
            v_ref.at[pl.ds(half, half)], out_ref.at[:, pl.ds(kv_width, kv_width)], sems.at[1]
        ),
    ]
    for copy in copies:
        copy.start()
    for copy in copies:
        copy.wait()


def window_upper_kernel(
    lengths_ref, q_ref, k_ref, v_ref, gain_ref,
    attn_ref, q_held, k_held, v_held, window_bias, upper_causal, lower_causal, gain_held,
    lengths_s, keys_s, values_s, bias_s, sems
):
    half = attn_ref.shape[1]
    upper, lower = pl.ds(half, half), pl.ds(0, half)
    first = [
        pltpu.make_async_copy(lengths_ref, lengths_s, sems.at[0]),
        pltpu.make_async_copy(k_ref.at[upper], k_held.at[upper], sems.at[1]),
        pltpu.make_async_copy(v_ref.at[upper], v_held.at[upper], sems.at[2]),
        pltpu.make_async_copy(q_ref.at[upper], q_held.at[upper], sems.at[3]),
    ]
    last = [
        pltpu.make_async_copy(k_ref.at[lower], k_held.at[lower], sems.at[4]),
        pltpu.make_async_copy(v_ref.at[lower], v_held.at[lower], sems.at[5]),
        pltpu.make_async_copy(q_ref.at[lower], q_held.at[lower], sems.at[6]),
        pltpu.make_async_copy(gain_ref, gain_held, sems.at[7]),
    ]
    for copy in first + last:
        copy.start()
    first[0].wait()
    bias_s[...] = upper_bias(lengths_s, half, WIN)
    window_bias[...] = lower_bias(lengths_s, half, WIN)
    upper_causal[...] = upper_bias(lengths_s, half, None)
    lower_causal[...] = lower_bias(lengths_s, half, None)
    first[1].wait()
    stage_keys(k_held[half:], keys_s)
    first[2].wait()
    stage_values(v_held[half:], values_s)
    first[3].wait()

    def queries_of(unit):
        return q_held[half:, unit.lane : unit.lane + 2 * LANES]

    window_heads(queries_of, keys_s, values_s, bias_s, attn_ref, q_held.shape[1])
    for copy in last:
        copy.wait()


def project(weight_ref, attn_ref, out_ref, chunk):
    for first in range(0, out_ref.shape[0], chunk):
        part = slice(first, first + chunk)
        out_ref[part, :] = dot(weight_ref[part, :], attn_ref[...], ((1,), (0,))).astype(BF16)


def project_upper_kernel(weight_ref, attn_ref, out_ref, *, chunk):
    project(weight_ref, attn_ref, out_ref, chunk)


def window_lower_kernel(
    q_ref, k_ref, v_ref, halo_ref, weight_ref, bias_ref, out_ref, attn_s, keys_s, values_s, *, chunk
):
    half = halo_ref.shape[0]
    kv_width = k_ref.shape[1]
    stage_keys(jnp.concatenate([halo_ref[:, :kv_width], k_ref[:half]], axis=0), keys_s)
    stage_values(jnp.concatenate([halo_ref[:, kv_width:], v_ref[:half]], axis=0), values_s)

    def queries_of(unit):
        return q_ref[:half, unit.lane : unit.lane + 2 * LANES]

    window_heads(queries_of, keys_s, values_s, bias_ref, attn_s, q_ref.shape[1])
    project(weight_ref, attn_s, out_ref, chunk)


def add_and_norm(own_ref, other_ref, gain_ref, branch_ref, normed_ref, first_row, sum_s, keep_ref, chunk):
    width, rows = own_ref.shape
    head = lax.axis_index("head")

    def add(c, squares):
        part = pl.ds(pl.multiple_of(c * chunk, 16), chunk)
        total = own_ref[part, :].astype(F32) + other_ref[part, :].astype(F32)
        sum_s[part, :] = total
        rounded = total.astype(BF16)
        if keep_ref is not None:
            rounded = jnp.where(head == 0, rounded, keep_ref[part, :])
        branch_ref[part, :] = rounded
        return squares + jnp.sum(total * total, axis=0, keepdims=True)

    squares = lax.fori_loop(0, width // chunk, add, jnp.zeros((1, rows), F32))
    factor = lax.rsqrt(squares * (1.0 / width) + 1e-05)
    for first in range(0, width, LANES):
        last = min(first + LANES, width)
        piece = jnp.transpose(sum_s[first:last, :] * factor) * gain_ref[first:last][None, :]
        normed_ref[first_row : first_row + rows, first:last] = piece.astype(BF16)


def norm_upper_kernel(
    own_ref, other_ref, gain_ref, kw_ref, vw_ref, branch_ref, normed_ref, kv_ref, sum_s, *, chunk
):
    add_and_norm(own_ref, other_ref, gain_ref, branch_ref, normed_ref, 0, sum_s, None, chunk)
    kv_width = kw_ref.shape[1]
    kv_ref[:, :kv_width] = dot(normed_ref[...], kw_ref[...], ((1,), (0,))).astype(BF16)
    kv_ref[:, kv_width:] = dot(normed_ref[...], vw_ref[...], ((1,), (0,))).astype(BF16)


def causal_upper_kernel(
    own_ref, other_ref, gain_ref, kw_ref, vw_ref, qw_ref, kept_ref, normed_ref, kv_up_ref, bias_ref,
    branch_ref, q_ref, kv_ref, out_ref,
    branch_s, out_s, normed_s, sum_s, keys_s, values_s, sems, *, chunk
):
    half = own_ref.shape[1]
    kv_width = kw_ref.shape[1]
    q_width = qw_ref.shape[1]
    normed_s[half:, :] = normed_ref[...]
    add_and_norm(own_ref, other_ref, gain_ref, branch_s, normed_s, 0, sum_s, kept_ref, chunk)
    branch_out = pltpu.make_async_copy(branch_s, branch_ref, sems.at[0])
    branch_out.start()
    stage_keys(kv_up_ref[:, :kv_width], keys_s)
    stage_values(kv_up_ref[:, kv_width:], values_s)

    def queries_of(unit):
        columns = slice(unit.lane, unit.lane + 2 * LANES)
        queries = dot(normed_s[...], qw_ref[:, columns], ((1,), (0,))).astype(BF16)
        q_ref[:, columns] = queries[:half]
        return queries[half:]

    causal_heads(queries_of, keys_s, values_s, bias_ref, out_s, q_width, lambda unit: None)
    upper_out = pltpu.make_async_copy(out_s, out_ref.at[pl.ds(half, half)], sems.at[1])
    upper_out.start()
    kv_ref[:, :kv_width] = dot(normed_s[:half, :], kw_ref[...], ((1,), (0,))).astype(BF16)
    kv_ref[:, kv_width:] = dot(normed_s[:half, :], vw_ref[...], ((1,), (0,))).astype(BF16)
    branch_out.wait()
    upper_out.wait()


def causal_lower_kernel(
    q_ref, kv_ref, halo_ref, bias_ref, given_ref, out_ref, out_s, keys_s, values_s, sems
):
    half, q_width = q_ref.shape
    kv_width = kv_ref.shape[1] // 2
    stage_keys(jnp.concatenate([halo_ref[:, :kv_width], kv_ref[:, :kv_width]], axis=0), keys_s)
    stage_values(jnp.concatenate([halo_ref[:, kv_width:], kv_ref[:, kv_width:]], axis=0), values_s)
    copies = []

    def queries_of(unit):
        return q_ref[:, unit.lane : unit.lane + 2 * LANES]

    def ready(unit):
        columns = pl.ds(unit.lane, 2 * LANES)
        copy = pltpu.make_async_copy(
            out_s.at[:, columns], out_ref.at[pl.ds(0, half), columns], sems.at[len(copies)]
        )
        copy.start()
        copies.append(copy)

    causal_heads(queries_of, keys_s, values_s, bias_ref, out_s, q_width, ready)
    for copy in copies:
        copy.wait()


def attention_scratch(kv_heads, keys):
    return [
        pltpu.VMEM((kv_heads, 2, keys, LANES), BF16),
        pltpu.VMEM((kv_heads, HD + TAIL, keys), BF16),
    ]


def local(
    window_queries,
    window_keys,
    window_values,
    out_weight,
    norm_gain,
    query_weight,
    key_weight,
    value_weight,
    doc_lengths,
):
    rows, q_width = window_queries.shape
    kv_width = window_keys.shape[1]
    kv_heads = kv_width // HD
    width = out_weight.shape[1]
    half = rows // 2
    chunk = 576
    dma = pltpu.SemaphoreType.DMA
    lengths, queries, keys, values = [
        in_hbm(x) for x in (doc_lengths, window_queries, window_keys, window_values)
    ]

    packed = pl.pallas_call(
        pack_kernel,
        out_shape=jax.ShapeDtypeStruct((half, 2 * kv_width), BF16),
        in_specs=hbm_specs(2),
        out_specs=vmem_specs(1)[0],
        scratch_shapes=[dma((2,))],
        compiler_params=params(16),
        cost_estimate=pl.CostEstimate(flops=10**10, bytes_accessed=10**6, transcendentals=0),
        name="pack",
    )(keys, values)
    halo = shifted(packed, "ctx")
    attn_s = pltpu.VMEM((q_width, half), BF16)
    (
        attn_upper, q_held, k_held, v_held, window_bias, upper_causal, lower_causal, gain
    ) = pl.pallas_call(
        window_upper_kernel,
        out_shape=(
            attn_s,
            pltpu.VMEM((rows, q_width), BF16),
            pltpu.VMEM((rows, kv_width), BF16),
            pltpu.VMEM((rows, kv_width), BF16),
            pltpu.VMEM((rows, half), F32),
            pltpu.VMEM((half, half), F32),
            pltpu.VMEM((rows, half), F32),
            pltpu.VMEM((width,), F32),
        ),
        in_specs=hbm_specs(5),
        out_specs=tuple(vmem_specs(8)),
        scratch_shapes=[pltpu.SMEM(doc_lengths.shape, jnp.int32)]
        + attention_scratch(kv_heads, half)
        + [pltpu.VMEM((half, half), F32), dma((8,))],
        compiler_params=params(8),
        name="window_upper",
    )(lengths, queries, keys, values, in_hbm(norm_gain))
    held = in_vmem(jnp.transpose(out_weight))
    own_upper = pl.pallas_call(
        functools.partial(project_upper_kernel, chunk=chunk),
        out_shape=pltpu.VMEM((width, half), BF16),
        in_specs=vmem_specs(2),
        out_specs=vmem_specs(1)[0],
        compiler_params=params(8),
        name="project_upper",
    )(held, attn_upper)
    key_held, value_held, query_held = [in_vmem(x) for x in (key_weight, value_weight, query_weight)]
    other_upper = swapped(own_upper, "head")
    own_lower = pl.pallas_call(
        functools.partial(window_lower_kernel, chunk=chunk),
        out_shape=pltpu.VMEM((width, half), BF16),
        in_specs=vmem_specs(6),
        out_specs=vmem_specs(1)[0],
        scratch_shapes=[attn_s] + attention_scratch(kv_heads, rows),
        compiler_params=params(16),
        name="window_lower",
    )(q_held, k_held, v_held, in_vmem(halo), held, window_bias)
    other_lower = swapped(own_lower, "head")
    branch_upper, normed_upper, pairs_upper = pl.pallas_call(
        functools.partial(norm_upper_kernel, chunk=192),
        out_shape=(
            pltpu.VMEM((width, half), BF16),
            pltpu.VMEM((half, width), BF16),
            pltpu.VMEM((half, 2 * kv_width), BF16),
        ),
        in_specs=vmem_specs(5),
        out_specs=tuple(vmem_specs(3)),
        scratch_shapes=[pltpu.VMEM((width, half), F32)],
        compiler_params=params(16),
        name="norm_upper",
    )(own_upper, other_upper, gain, key_held, value_held)
    earlier = shifted(pairs_upper, "ctx")
    branch, causal_queries, pairs_lower, causal_out = pl.pallas_call(
        functools.partial(causal_upper_kernel, chunk=192),
        out_shape=(
            pltpu.HBM((width, half), BF16),
            pltpu.VMEM((half, q_width), BF16),
            pltpu.VMEM((half, 2 * kv_width), BF16),
            pltpu.HBM((rows, q_width), BF16),
        ),
        in_specs=vmem_specs(10),
        out_specs=(hbm_specs(1)[0], *vmem_specs(2), hbm_specs(1)[0]),
        scratch_shapes=[
            pltpu.VMEM((width, half), BF16),
            pltpu.VMEM((half, q_width), BF16),
            pltpu.VMEM((rows, width), BF16),
            pltpu.VMEM((width, half), F32),
        ]
        + attention_scratch(kv_heads, half)
        + [dma((2,))],
        compiler_params=params(16),
        name="causal_upper",
    )(
        own_lower, other_lower, gain, key_held, value_held, query_held,
        branch_upper, normed_upper, pairs_upper, upper_causal,
    )
    causal_out = pl.pallas_call(
        causal_lower_kernel,
        out_shape=pltpu.HBM((rows, q_width), BF16),
        in_specs=vmem_specs(4) + hbm_specs(1),
        out_specs=hbm_specs(1)[0],
        scratch_shapes=[pltpu.VMEM((half, q_width), BF16)]
        + attention_scratch(kv_heads, rows)
        + [dma((q_width // (2 * LANES),))],
        input_output_aliases={4: 0},
        compiler_params=params(16),
        name="causal_lower",
    )(causal_queries, pairs_lower, in_vmem(earlier), lower_causal, causal_out)
    return (jnp.transpose(branch), causal_out)


def solution(mesh):
    placed = (
        P("ctx", "head"),
        P("ctx", "head"),
        P("ctx", "head"),
        P("head", None),
        P(),
        P(None, "head"),
        P(None, "head"),
        P(None, "head"),
        P(),
    )
    return jax.shard_map(
        local,
        mesh=mesh,
        in_specs=placed,
        out_specs=(P(("ctx", "head"), None), P("ctx", "head")),
        check_vma=False,
    )
```

```python
import functools

import jax
import jax.numpy as jnp
from jax import lax
from jax.experimental import pallas as pl
from jax.experimental.pallas import tpu as pltpu
from jax.sharding import PartitionSpec as P

HD = 64
WIN = 128
LANES = 128
NEG = -1e30
TAIL = 16

F32 = jnp.float32
BF16 = jnp.bfloat16
MIB = 1024 * 1024


def params(mib):
    return pltpu.CompilerParams(vmem_limit_bytes=mib * MIB)


def in_vmem(array):
    return pltpu.with_memory_space_constraint(array, pltpu.VMEM)


def in_hbm(array):
    return pltpu.with_memory_space_constraint(array, pltpu.HBM)


def hbm_specs(count):
    return [pl.BlockSpec(memory_space=pltpu.HBM)] * count


def vmem_specs(count):
    return [pl.BlockSpec(memory_space=pltpu.VMEM)] * count


def dot(a, b, dims):
    return lax.dot_general(a, b, (dims, ((), ())), preferred_element_type=F32)


def shifted(block, axis):
    size = lax.axis_size(axis)
    return lax.ppermute(block, axis, [(i, (i + 1) % size) for i in range(size)])


def swapped(block, axis):
    size = lax.axis_size(axis)
    return lax.ppermute(block, axis, [(i, size - 1 - i) for i in range(size)])


def lower_bias(lengths_ref, half, width):
    ctx = lax.axis_index("ctx")
    first = jnp.where(ctx == 0, half, 0)
    split = first + lengths_ref[2 * ctx]
    return bias_of(2 * half, half, half, first, split, width)


def upper_bias(lengths_ref, half, width):
    ctx = lax.axis_index("ctx")
    last = lengths_ref.shape[0] - 1
    split = lengths_ref[jnp.minimum(2 * ctx + 2, last)]
    split = jnp.where(ctx == lax.axis_size("ctx") - 1, 2 * half, split)
    return bias_of(half, half, 0, 0, split, width)


def bias_of(keys, rows, row_offset, first, split, width):
    key = lax.broadcasted_iota(jnp.int32, (keys, rows), 0)
    row = lax.broadcasted_iota(jnp.int32, (keys, rows), 1) + row_offset
    lowest = jnp.where(row >= split, split, first)
    if width is not None:
        lowest = jnp.maximum(lowest, row - (width - 1))
    return jnp.where((key >= lowest) & (key <= row), 0.0, NEG).astype(F32)


def stage_keys(keys, keys_ref):
    scaled = (keys.astype(F32) * HD ** (-0.5)).astype(BF16)
    lane = lax.broadcasted_iota(jnp.int32, (keys.shape[0], LANES), 1)
    zero = jnp.zeros((keys.shape[0], LANES), BF16)
    for pair in range(keys.shape[1] // LANES):
        tile = scaled[:, pair * LANES : (pair + 1) * LANES]
        turned = jnp.concatenate([tile[:, HD:], tile[:, :HD]], axis=1)
        keys_ref[2 * pair, 0] = jnp.where(lane < HD, tile, zero)
        keys_ref[2 * pair, 1] = jnp.where(lane < HD, zero, turned)
        keys_ref[2 * pair + 1, 0] = jnp.where(lane < HD, turned, zero)
        keys_ref[2 * pair + 1, 1] = jnp.where(lane < HD, zero, tile)


def stage_values(values, values_ref):
    count = values.shape[0]
    turned = jnp.transpose(values.astype(F32)).astype(BF16)
    for head in range(values.shape[1] // HD):
        values_ref[head, :HD, :] = turned[head * HD : (head + 1) * HD]
        values_ref[head, HD:, :] = jnp.ones((TAIL, count), BF16)


class Unit:
    def __init__(self, g, lane):
        self.g, self.lane = g, lane


def units_of(kv_heads, q_width):
    step = 2 * LANES
    group = q_width // kv_heads
    return [Unit(lane // group, lane) for lane in range(0, q_width, step)]


def unit_scores(queries, unit, keys_ref):
    stacked = jnp.concatenate([queries[:, :LANES], queries[:, LANES:]], axis=0)
    keys = jnp.concatenate([keys_ref[unit.g, 0], keys_ref[unit.g, 1]], axis=0)
    return dot(keys, stacked, ((1,), (1,)))


def unit_attend(scores, unit, values_ref, bias):
    count = bias.shape[0]
    wide = jnp.concatenate([bias, bias], axis=1)
    patterns = []
    for side in range(2):
        masked = scores[side * count : (side + 1) * count] + wide
        highest = jnp.max(masked, axis=0, keepdims=True)
        patterns.append(jnp.exp((masked - highest).astype(BF16)))
    weighted = dot(values_ref[unit.g], jnp.concatenate(patterns, axis=1), ((1,), (0,)))
    return weighted[:HD] * (1.0 / weighted[HD : HD + 1])


def pipelined(units, queries_of, keys_ref, values_ref, bias, write):
    count = len(units)
    queries = queries_of(units[0])
    scores = unit_scores(queries, units[0], keys_ref)
    queries = queries_of(units[1])
    for i, unit in enumerate(units):
        now = scores
        if i + 1 < count:
            scores = unit_scores(queries, units[i + 1], keys_ref)
        if i + 2 < count:
            queries = queries_of(units[i + 2])
        write(unit, unit_attend(now, unit, values_ref, bias))


def window_heads(queries_of, keys_ref, values_ref, bias_ref, out_ref, q_width):
    def write(unit, part):
        rows = part.shape[1] // 4
        rounded = part.astype(BF16)
        for side in range(2):
            for t in range(2):
                at = (side * 2 + t) * rows
                start = unit.lane + t * LANES + side * HD
                out_ref[start : start + HD, :] = rounded[:, at : at + rows]

    pipelined(units_of(keys_ref.shape[0], q_width), queries_of, keys_ref, values_ref, bias_ref[...], write)


def causal_heads(queries_of, keys_ref, values_ref, bias_ref, out_ref, q_width, ready):
    def write(unit, part):
        rows = part.shape[1] // 4
        for t in range(2):
            low = part[:, t * rows : (t + 1) * rows]
            high = part[:, (2 + t) * rows : (3 + t) * rows]
            lane = unit.lane + t * LANES
            out_ref[:, lane : lane + LANES] = jnp.transpose(
                jnp.concatenate([low, high], axis=0)
            ).astype(BF16)
        ready(unit)

    pipelined(units_of(keys_ref.shape[0], q_width), queries_of, keys_ref, values_ref, bias_ref[...], write)


def pack_kernel(k_ref, v_ref, out_ref, sems):
    half = out_ref.shape[0]
    kv_width = k_ref.shape[1]
    copies = [
        pltpu.make_async_copy(k_ref.at[pl.ds(half, half)], out_ref.at[:, pl.ds(0, kv_width)], sems.at[0]),
        pltpu.make_async_copy(
            v_ref.at[pl.ds(half, half)], out_ref.at[:, pl.ds(kv_width, kv_width)], sems.at[1]
        ),
    ]
    for copy in copies:
        copy.start()
    for copy in copies:
        copy.wait()


def window_upper_kernel(
    lengths_ref, q_ref, k_ref, v_ref, gain_ref,
    attn_ref, q_held, k_held, v_held, window_bias, upper_causal, lower_causal, gain_held,
    lengths_s, keys_s, values_s, bias_s, sems
):
    half = attn_ref.shape[1]
    upper, lower = pl.ds(half, half), pl.ds(0, half)
    first = [
        pltpu.make_async_copy(lengths_ref, lengths_s, sems.at[0]),
        pltpu.make_async_copy(k_ref.at[upper], k_held.at[upper], sems.at[1]),
        pltpu.make_async_copy(v_ref.at[upper], v_held.at[upper], sems.at[2]),
        pltpu.make_async_copy(q_ref.at[upper], q_held.at[upper], sems.at[3]),
    ]
    last = [
        pltpu.make_async_copy(k_ref.at[lower], k_held.at[lower], sems.at[4]),
        pltpu.make_async_copy(v_ref.at[lower], v_held.at[lower], sems.at[5]),
        pltpu.make_async_copy(q_ref.at[lower], q_held.at[lower], sems.at[6]),
        pltpu.make_async_copy(gain_ref, gain_held, sems.at[7]),
    ]
    for copy in first + last:
        copy.start()
    first[0].wait()
    bias_s[...] = upper_bias(lengths_s, half, WIN)
    window_bias[...] = lower_bias(lengths_s, half, WIN)
    upper_causal[...] = upper_bias(lengths_s, half, None)
    lower_causal[...] = lower_bias(lengths_s, half, None)
    first[1].wait()
    stage_keys(k_held[half:], keys_s)
    first[2].wait()
    stage_values(v_held[half:], values_s)
    first[3].wait()

    def queries_of(unit):
        return q_held[half:, unit.lane : unit.lane + 2 * LANES]

    window_heads(queries_of, keys_s, values_s, bias_s, attn_ref, q_held.shape[1])
    for copy in last:
        copy.wait()


def project(weight_ref, attn_ref, out_ref, chunk):
    for first in range(0, out_ref.shape[0], chunk):
        part = slice(first, first + chunk)
        out_ref[part, :] = dot(weight_ref[part, :], attn_ref[...], ((1,), (0,))).astype(BF16)


def project_upper_kernel(weight_ref, attn_ref, out_ref, *, chunk):
    project(weight_ref, attn_ref, out_ref, chunk)


def window_lower_kernel(
    q_ref, k_ref, v_ref, halo_ref, weight_ref, bias_ref, out_ref, attn_s, keys_s, values_s, *, chunk
):
    half = halo_ref.shape[0]
    kv_width = k_ref.shape[1]
    stage_keys(jnp.concatenate([halo_ref[:, :kv_width], k_ref[:half]], axis=0), keys_s)
    stage_values(jnp.concatenate([halo_ref[:, kv_width:], v_ref[:half]], axis=0), values_s)

    def queries_of(unit):
        return q_ref[:half, unit.lane : unit.lane + 2 * LANES]

    window_heads(queries_of, keys_s, values_s, bias_ref, attn_s, q_ref.shape[1])
    project(weight_ref, attn_s, out_ref, chunk)


def add_and_norm(own_ref, other_ref, gain_ref, branch_ref, normed_ref, first_row, sum_s, keep_ref, chunk):
    width, rows = own_ref.shape
    head = lax.axis_index("head")

    def add(c, squares):
        part = pl.ds(pl.multiple_of(c * chunk, 16), chunk)
        total = own_ref[part, :].astype(F32) + other_ref[part, :].astype(F32)
        sum_s[part, :] = total
        rounded = total.astype(BF16)
        if keep_ref is not None:
            rounded = jnp.where(head == 0, rounded, keep_ref[part, :])
        branch_ref[part, :] = rounded
        return squares + jnp.sum(total * total, axis=0, keepdims=True)

    squares = lax.fori_loop(0, width // chunk, add, jnp.zeros((1, rows), F32))
    factor = lax.rsqrt(squares * (1.0 / width) + 1e-05)
    for first in range(0, width, LANES):
        last = min(first + LANES, width)
        piece = jnp.transpose(sum_s[first:last, :] * factor) * gain_ref[first:last][None, :]
        normed_ref[first_row : first_row + rows, first:last] = piece.astype(BF16)


def norm_upper_kernel(
    own_ref, other_ref, gain_ref, kw_ref, vw_ref, branch_ref, normed_ref, kv_ref, sum_s, *, chunk
):
    add_and_norm(own_ref, other_ref, gain_ref, branch_ref, normed_ref, 0, sum_s, None, chunk)
    kv_width = kw_ref.shape[1]
    kv_ref[:, :kv_width] = dot(normed_ref[...], kw_ref[...], ((1,), (0,))).astype(BF16)
    kv_ref[:, kv_width:] = dot(normed_ref[...], vw_ref[...], ((1,), (0,))).astype(BF16)


def causal_upper_kernel(
    own_ref, other_ref, gain_ref, kw_ref, vw_ref, qw_ref, kept_ref, normed_ref, kv_up_ref, bias_ref,
    branch_ref, q_ref, kv_ref, out_ref,
    branch_s, out_s, upper_q_s, normed_s, sum_s, keys_s, values_s, sems, *, chunk
):
    half = own_ref.shape[1]
    kv_width = kw_ref.shape[1]
    q_width = qw_ref.shape[1]
    normed_s[half:, :] = normed_ref[...]
    add_and_norm(own_ref, other_ref, gain_ref, branch_s, normed_s, 0, sum_s, kept_ref, chunk)
    branch_out = pltpu.make_async_copy(branch_s, branch_ref, sems.at[0])
    branch_out.start()
    stage_keys(kv_up_ref[:, :kv_width], keys_s)
    stage_values(kv_up_ref[:, kv_width:], values_s)

    piece = q_width // 2
    for first in range(0, q_width, piece):
        columns = slice(first, first + piece)
        queries = dot(normed_s[...], qw_ref[:, columns], ((1,), (0,))).astype(BF16)
        q_ref[:, columns] = queries[:half]
        upper_q_s[:, columns] = queries[half:]

    def queries_of(unit):
        return upper_q_s[:, unit.lane : unit.lane + 2 * LANES]

    causal_heads(queries_of, keys_s, values_s, bias_ref, out_s, q_width, lambda unit: None)
    upper_out = pltpu.make_async_copy(out_s, out_ref.at[pl.ds(half, half)], sems.at[1])
    upper_out.start()
    kv_ref[:, :kv_width] = dot(normed_s[:half, :], kw_ref[...], ((1,), (0,))).astype(BF16)
    kv_ref[:, kv_width:] = dot(normed_s[:half, :], vw_ref[...], ((1,), (0,))).astype(BF16)
    branch_out.wait()
    upper_out.wait()


def causal_lower_kernel(
    q_ref, kv_ref, halo_ref, bias_ref, given_ref, out_ref, out_s, keys_s, values_s, sems
):
    half, q_width = q_ref.shape
    kv_width = kv_ref.shape[1] // 2
    stage_keys(jnp.concatenate([halo_ref[:, :kv_width], kv_ref[:, :kv_width]], axis=0), keys_s)
    stage_values(jnp.concatenate([halo_ref[:, kv_width:], kv_ref[:, kv_width:]], axis=0), values_s)
    copies = []

    def queries_of(unit):
        return q_ref[:, unit.lane : unit.lane + 2 * LANES]

    def ready(unit):
        columns = pl.ds(unit.lane, 2 * LANES)
        copy = pltpu.make_async_copy(
            out_s.at[:, columns], out_ref.at[pl.ds(0, half), columns], sems.at[len(copies)]
        )
        copy.start()
        copies.append(copy)

    causal_heads(queries_of, keys_s, values_s, bias_ref, out_s, q_width, ready)
    for copy in copies:
        copy.wait()


def attention_scratch(kv_heads, keys):
    return [
        pltpu.VMEM((kv_heads, 2, keys, LANES), BF16),
        pltpu.VMEM((kv_heads, HD + TAIL, keys), BF16),
    ]


def local(
    window_queries,
    window_keys,
    window_values,
    out_weight,
    norm_gain,
    query_weight,
    key_weight,
    value_weight,
    doc_lengths,
):
    rows, q_width = window_queries.shape
    kv_width = window_keys.shape[1]
    kv_heads = kv_width // HD
    width = out_weight.shape[1]
    half = rows // 2
    chunk = 576
    dma = pltpu.SemaphoreType.DMA
    lengths, queries, keys, values = [
        in_hbm(x) for x in (doc_lengths, window_queries, window_keys, window_values)
    ]

    packed = pl.pallas_call(
        pack_kernel,
        out_shape=jax.ShapeDtypeStruct((half, 2 * kv_width), BF16),
        in_specs=hbm_specs(2),
        out_specs=vmem_specs(1)[0],
        scratch_shapes=[dma((2,))],
        compiler_params=params(16),
        cost_estimate=pl.CostEstimate(flops=10**10, bytes_accessed=10**6, transcendentals=0),
        name="pack",
    )(keys, values)
    halo = shifted(packed, "ctx")
    attn_s = pltpu.VMEM((q_width, half), BF16)
    (
        attn_upper, q_held, k_held, v_held, window_bias, upper_causal, lower_causal, gain
    ) = pl.pallas_call(
        window_upper_kernel,
        out_shape=(
            attn_s,
            pltpu.VMEM((rows, q_width), BF16),
            pltpu.VMEM((rows, kv_width), BF16),
            pltpu.VMEM((rows, kv_width), BF16),
            pltpu.VMEM((rows, half), F32),
            pltpu.VMEM((half, half), F32),
            pltpu.VMEM((rows, half), F32),
            pltpu.VMEM((width,), F32),
        ),
        in_specs=hbm_specs(5),
        out_specs=tuple(vmem_specs(8)),
        scratch_shapes=[pltpu.SMEM(doc_lengths.shape, jnp.int32)]
        + attention_scratch(kv_heads, half)
        + [pltpu.VMEM((half, half), F32), dma((8,))],
        compiler_params=params(8),
        name="window_upper",
    )(lengths, queries, keys, values, in_hbm(norm_gain))
    held = in_vmem(jnp.transpose(out_weight))
    own_upper = pl.pallas_call(
        functools.partial(project_upper_kernel, chunk=chunk),
        out_shape=pltpu.VMEM((width, half), BF16),
        in_specs=vmem_specs(2),
        out_specs=vmem_specs(1)[0],
        compiler_params=params(8),
        name="project_upper",
    )(held, attn_upper)
    key_held, value_held, query_held = [in_vmem(x) for x in (key_weight, value_weight, query_weight)]
    other_upper = swapped(own_upper, "head")
    own_lower = pl.pallas_call(
        functools.partial(window_lower_kernel, chunk=chunk),
        out_shape=pltpu.VMEM((width, half), BF16),
        in_specs=vmem_specs(6),
        out_specs=vmem_specs(1)[0],
        scratch_shapes=[attn_s] + attention_scratch(kv_heads, rows),
        compiler_params=params(16),
        name="window_lower",
    )(q_held, k_held, v_held, in_vmem(halo), held, window_bias)
    other_lower = swapped(own_lower, "head")
    branch_upper, normed_upper, pairs_upper = pl.pallas_call(
        functools.partial(norm_upper_kernel, chunk=192),
        out_shape=(
            pltpu.VMEM((width, half), BF16),
            pltpu.VMEM((half, width), BF16),
            pltpu.VMEM((half, 2 * kv_width), BF16),
        ),
        in_specs=vmem_specs(5),
        out_specs=tuple(vmem_specs(3)),
        scratch_shapes=[pltpu.VMEM((width, half), F32)],
        compiler_params=params(16),
        name="norm_upper",
    )(own_upper, other_upper, gain, key_held, value_held)
    earlier = shifted(pairs_upper, "ctx")
    branch, causal_queries, pairs_lower, causal_out = pl.pallas_call(
        functools.partial(causal_upper_kernel, chunk=192),
        out_shape=(
            pltpu.HBM((width, half), BF16),
            pltpu.VMEM((half, q_width), BF16),
            pltpu.VMEM((half, 2 * kv_width), BF16),
            pltpu.HBM((rows, q_width), BF16),
        ),
        in_specs=vmem_specs(10),
        out_specs=(hbm_specs(1)[0], *vmem_specs(2), hbm_specs(1)[0]),
        scratch_shapes=[
            pltpu.VMEM((width, half), BF16),
            pltpu.VMEM((half, q_width), BF16),
            pltpu.VMEM((half, q_width), BF16),
            pltpu.VMEM((rows, width), BF16),
            pltpu.VMEM((width, half), F32),
        ]
        + attention_scratch(kv_heads, half)
        + [dma((2,))],
        compiler_params=params(16),
        name="causal_upper",
    )(
        own_lower, other_lower, gain, key_held, value_held, query_held,
        branch_upper, normed_upper, pairs_upper, upper_causal,
    )
    causal_out = pl.pallas_call(
        causal_lower_kernel,
        out_shape=pltpu.HBM((rows, q_width), BF16),
        in_specs=vmem_specs(4) + hbm_specs(1),
        out_specs=hbm_specs(1)[0],
        scratch_shapes=[pltpu.VMEM((half, q_width), BF16)]
        + attention_scratch(kv_heads, rows)
        + [dma((q_width // (2 * LANES),))],
        input_output_aliases={4: 0},
        compiler_params=params(16),
        name="causal_lower",
    )(causal_queries, pairs_lower, in_vmem(earlier), lower_causal, causal_out)
    return (jnp.transpose(branch), causal_out)


def solution(mesh):
    placed = (
        P("ctx", "head"),
        P("ctx", "head"),
        P("ctx", "head"),
        P("head", None),
        P(),
        P(None, "head"),
        P(None, "head"),
        P(None, "head"),
        P(),
    )
    return jax.shard_map(
        local,
        mesh=mesh,
        in_specs=placed,
        out_specs=(P(("ctx", "head"), None), P("ctx", "head")),
        check_vma=False,
    )
```

```python
import functools

import jax
import jax.numpy as jnp
from jax import lax
from jax.experimental import pallas as pl
from jax.experimental.pallas import tpu as pltpu
from jax.sharding import PartitionSpec as P

HD = 64
WIN = 128
LANES = 128
NEG = -1e30
TAIL = 16

F32 = jnp.float32
BF16 = jnp.bfloat16
MIB = 1024 * 1024


def params(mib):
    return pltpu.CompilerParams(vmem_limit_bytes=mib * MIB)


def in_vmem(array):
    return pltpu.with_memory_space_constraint(array, pltpu.VMEM)


def in_hbm(array):
    return pltpu.with_memory_space_constraint(array, pltpu.HBM)


def hbm_specs(count):
    return [pl.BlockSpec(memory_space=pltpu.HBM)] * count


def vmem_specs(count):
    return [pl.BlockSpec(memory_space=pltpu.VMEM)] * count


def dot(a, b, dims):
    return lax.dot_general(a, b, (dims, ((), ())), preferred_element_type=F32)


def neighbours(block, axis):
    size = lax.axis_size(axis)

    def swap(first):
        partner = list(range(size))
        for i in range(first, size - 1, 2):
            partner[i], partner[i + 1] = i + 1, i
        return lax.ppermute(block, axis, list(enumerate(partner)))

    odd, even = swap(1), swap(0)
    return even, odd


def chosen(even_ref, odd_ref):
    is_odd = lax.rem(lax.axis_index("ctx"), 2) == 1
    return jnp.where(is_odd, even_ref[...], odd_ref[...])


def swapped(block, axis):
    size = lax.axis_size(axis)
    return lax.ppermute(block, axis, [(i, size - 1 - i) for i in range(size)])


def lower_bias(lengths_ref, half, width):
    ctx = lax.axis_index("ctx")
    first = jnp.where(ctx == 0, half, 0)
    split = first + lengths_ref[2 * ctx]
    return bias_of(2 * half, half, half, first, split, width)


def upper_bias(lengths_ref, half, width):
    ctx = lax.axis_index("ctx")
    last = lengths_ref.shape[0] - 1
    split = lengths_ref[jnp.minimum(2 * ctx + 2, last)]
    split = jnp.where(ctx == lax.axis_size("ctx") - 1, 2 * half, split)
    return bias_of(half, half, 0, 0, split, width)


def bias_of(keys, rows, row_offset, first, split, width):
    key = lax.broadcasted_iota(jnp.int32, (keys, rows), 0)
    row = lax.broadcasted_iota(jnp.int32, (keys, rows), 1) + row_offset
    lowest = jnp.where(row >= split, split, first)
    if width is not None:
        lowest = jnp.maximum(lowest, row - (width - 1))
    return jnp.where((key >= lowest) & (key <= row), 0.0, NEG).astype(F32)


def stage_keys(keys, keys_ref):
    scaled = (keys.astype(F32) * HD ** (-0.5)).astype(BF16)
    lane = lax.broadcasted_iota(jnp.int32, (keys.shape[0], LANES), 1)
    zero = jnp.zeros((keys.shape[0], LANES), BF16)
    for pair in range(keys.shape[1] // LANES):
        tile = scaled[:, pair * LANES : (pair + 1) * LANES]
        turned = jnp.concatenate([tile[:, HD:], tile[:, :HD]], axis=1)
        keys_ref[2 * pair, 0] = jnp.where(lane < HD, tile, zero)
        keys_ref[2 * pair, 1] = jnp.where(lane < HD, zero, turned)
        keys_ref[2 * pair + 1, 0] = jnp.where(lane < HD, turned, zero)
        keys_ref[2 * pair + 1, 1] = jnp.where(lane < HD, zero, tile)


def stage_values(values, values_ref):
    count = values.shape[0]
    turned = jnp.transpose(values.astype(F32)).astype(BF16)
    for head in range(values.shape[1] // HD):
        values_ref[head, :HD, :] = turned[head * HD : (head + 1) * HD]
        values_ref[head, HD:, :] = jnp.ones((TAIL, count), BF16)


class Unit:
    def __init__(self, g, lane):
        self.g, self.lane = g, lane


def units_of(kv_heads, q_width):
    step = 2 * LANES
    group = q_width // kv_heads
    return [Unit(lane // group, lane) for lane in range(0, q_width, step)]


def unit_scores(queries, unit, keys_ref):
    stacked = jnp.concatenate([queries[:, :LANES], queries[:, LANES:]], axis=0)
    keys = jnp.concatenate([keys_ref[unit.g, 0], keys_ref[unit.g, 1]], axis=0)
    return dot(keys, stacked, ((1,), (1,)))


def unit_attend(scores, unit, values_ref, bias):
    count = bias.shape[0]
    wide = jnp.concatenate([bias, bias], axis=1)
    patterns = []
    for side in range(2):
        masked = scores[side * count : (side + 1) * count] + wide
        highest = jnp.max(masked, axis=0, keepdims=True)
        patterns.append(jnp.exp((masked - highest).astype(BF16)))
    weighted = dot(values_ref[unit.g], jnp.concatenate(patterns, axis=1), ((1,), (0,)))
    return weighted[:HD] * (1.0 / weighted[HD : HD + 1])


def pipelined(units, queries_of, keys_ref, values_ref, bias, write):
    count = len(units)
    queries = queries_of(units[0])
    scores = unit_scores(queries, units[0], keys_ref)
    queries = queries_of(units[1])
    for i, unit in enumerate(units):
        now = scores
        if i + 1 < count:
            scores = unit_scores(queries, units[i + 1], keys_ref)
        if i + 2 < count:
            queries = queries_of(units[i + 2])
        write(unit, unit_attend(now, unit, values_ref, bias))


def window_heads(queries_of, keys_ref, values_ref, bias_ref, out_ref, q_width):
    def write(unit, part):
        rows = part.shape[1] // 4
        rounded = part.astype(BF16)
        for side in range(2):
            for t in range(2):
                at = (side * 2 + t) * rows
                start = unit.lane + t * LANES + side * HD
                out_ref[start : start + HD, :] = rounded[:, at : at + rows]

    pipelined(units_of(keys_ref.shape[0], q_width), queries_of, keys_ref, values_ref, bias_ref[...], write)


def causal_heads(queries_of, keys_ref, values_ref, bias_ref, out_ref, q_width, ready):
    def write(unit, part):
        rows = part.shape[1] // 4
        for t in range(2):
            low = part[:, t * rows : (t + 1) * rows]
            high = part[:, (2 + t) * rows : (3 + t) * rows]
            lane = unit.lane + t * LANES
            out_ref[:, lane : lane + LANES] = jnp.transpose(
                jnp.concatenate([low, high], axis=0)
            ).astype(BF16)
        ready(unit)

    pipelined(units_of(keys_ref.shape[0], q_width), queries_of, keys_ref, values_ref, bias_ref[...], write)


def pack_kernel(k_ref, v_ref, out_ref, sems):
    half = out_ref.shape[0]
    kv_width = k_ref.shape[1]
    copies = [
        pltpu.make_async_copy(k_ref.at[pl.ds(half, half)], out_ref.at[:, pl.ds(0, kv_width)], sems.at[0]),
        pltpu.make_async_copy(
            v_ref.at[pl.ds(half, half)], out_ref.at[:, pl.ds(kv_width, kv_width)], sems.at[1]
        ),
    ]
    for copy in copies:
        copy.start()
    for copy in copies:
        copy.wait()


def window_upper_kernel(
    lengths_ref, q_ref, k_ref, v_ref, gain_ref,
    attn_ref, q_held, k_held, v_held, window_bias, upper_causal, lower_causal, gain_held,
    lengths_s, keys_s, values_s, bias_s, sems
):
    half = attn_ref.shape[1]
    upper, lower = pl.ds(half, half), pl.ds(0, half)
    first = [
        pltpu.make_async_copy(lengths_ref, lengths_s, sems.at[0]),
        pltpu.make_async_copy(k_ref.at[upper], k_held.at[upper], sems.at[1]),
        pltpu.make_async_copy(v_ref.at[upper], v_held.at[upper], sems.at[2]),
        pltpu.make_async_copy(q_ref.at[upper], q_held.at[upper], sems.at[3]),
    ]
    last = [
        pltpu.make_async_copy(k_ref.at[lower], k_held.at[lower], sems.at[4]),
        pltpu.make_async_copy(v_ref.at[lower], v_held.at[lower], sems.at[5]),
        pltpu.make_async_copy(q_ref.at[lower], q_held.at[lower], sems.at[6]),
        pltpu.make_async_copy(gain_ref, gain_held, sems.at[7]),
    ]
    for copy in first + last:
        copy.start()
    first[0].wait()
    bias_s[...] = upper_bias(lengths_s, half, WIN)
    window_bias[...] = lower_bias(lengths_s, half, WIN)
    upper_causal[...] = upper_bias(lengths_s, half, None)
    lower_causal[...] = lower_bias(lengths_s, half, None)
    first[1].wait()
    stage_keys(k_held[half:], keys_s)
    first[2].wait()
    stage_values(v_held[half:], values_s)
    first[3].wait()

    def queries_of(unit):
        return q_held[half:, unit.lane : unit.lane + 2 * LANES]

    window_heads(queries_of, keys_s, values_s, bias_s, attn_ref, q_held.shape[1])
    for copy in last:
        copy.wait()


def project(weight_ref, attn_ref, out_ref, chunk):
    for first in range(0, out_ref.shape[0], chunk):
        part = slice(first, first + chunk)
        out_ref[part, :] = dot(weight_ref[part, :], attn_ref[...], ((1,), (0,))).astype(BF16)


def project_upper_kernel(weight_ref, attn_ref, out_ref, *, chunk):
    project(weight_ref, attn_ref, out_ref, chunk)


def window_lower_kernel(
    q_ref, k_ref, v_ref, even_ref, odd_ref, weight_ref, bias_ref,
    out_ref, attn_s, keys_s, values_s, *, chunk
):
    half = even_ref.shape[0]
    kv_width = k_ref.shape[1]
    halo = chosen(even_ref, odd_ref)
    stage_keys(jnp.concatenate([halo[:, :kv_width], k_ref[:half]], axis=0), keys_s)
    stage_values(jnp.concatenate([halo[:, kv_width:], v_ref[:half]], axis=0), values_s)

    def queries_of(unit):
        return q_ref[:half, unit.lane : unit.lane + 2 * LANES]

    window_heads(queries_of, keys_s, values_s, bias_ref, attn_s, q_ref.shape[1])
    project(weight_ref, attn_s, out_ref, chunk)


def add_and_norm(own_ref, other_ref, gain_ref, branch_ref, normed_ref, first_row, sum_s, keep_ref, chunk):
    width, rows = own_ref.shape
    head = lax.axis_index("head")

    def add(c, squares):
        part = pl.ds(pl.multiple_of(c * chunk, 16), chunk)
        total = own_ref[part, :].astype(F32) + other_ref[part, :].astype(F32)
        sum_s[part, :] = total
        rounded = total.astype(BF16)
        if keep_ref is not None:
            rounded = jnp.where(head == 0, rounded, keep_ref[part, :])
        branch_ref[part, :] = rounded
        return squares + jnp.sum(total * total, axis=0, keepdims=True)

    squares = lax.fori_loop(0, width // chunk, add, jnp.zeros((1, rows), F32))
    factor = lax.rsqrt(squares * (1.0 / width) + 1e-05)
    for first in range(0, width, LANES):
        last = min(first + LANES, width)
        piece = jnp.transpose(sum_s[first:last, :] * factor) * gain_ref[first:last][None, :]
        normed_ref[first_row : first_row + rows, first:last] = piece.astype(BF16)


def norm_upper_kernel(
    own_ref, other_ref, gain_ref, kw_ref, vw_ref, branch_ref, normed_ref, kv_ref, sum_s, *, chunk
):
    add_and_norm(own_ref, other_ref, gain_ref, branch_ref, normed_ref, 0, sum_s, None, chunk)
    kv_width = kw_ref.shape[1]
    kv_ref[:, :kv_width] = dot(normed_ref[...], kw_ref[...], ((1,), (0,))).astype(BF16)
    kv_ref[:, kv_width:] = dot(normed_ref[...], vw_ref[...], ((1,), (0,))).astype(BF16)


def causal_upper_kernel(
    own_ref, other_ref, gain_ref, kw_ref, vw_ref, qw_ref, kept_ref, normed_ref, kv_up_ref, bias_ref,
    branch_ref, q_ref, kv_ref, out_ref,
    branch_s, out_s, upper_q_s, normed_s, sum_s, keys_s, values_s, sems, *, chunk
):
    half = own_ref.shape[1]
    kv_width = kw_ref.shape[1]
    q_width = qw_ref.shape[1]
    normed_s[half:, :] = normed_ref[...]
    add_and_norm(own_ref, other_ref, gain_ref, branch_s, normed_s, 0, sum_s, kept_ref, chunk)
    branch_out = pltpu.make_async_copy(branch_s, branch_ref, sems.at[0])
    branch_out.start()
    stage_keys(kv_up_ref[:, :kv_width], keys_s)
    stage_values(kv_up_ref[:, kv_width:], values_s)

    piece = q_width // 2
    for first in range(0, q_width, piece):
        columns = slice(first, first + piece)
        queries = dot(normed_s[...], qw_ref[:, columns], ((1,), (0,))).astype(BF16)
        q_ref[:, columns] = queries[:half]
        upper_q_s[:, columns] = queries[half:]

    def queries_of(unit):
        return upper_q_s[:, unit.lane : unit.lane + 2 * LANES]

    causal_heads(queries_of, keys_s, values_s, bias_ref, out_s, q_width, lambda unit: None)
    upper_out = pltpu.make_async_copy(out_s, out_ref.at[pl.ds(half, half)], sems.at[1])
    upper_out.start()
    kv_ref[:, :kv_width] = dot(normed_s[:half, :], kw_ref[...], ((1,), (0,))).astype(BF16)
    kv_ref[:, kv_width:] = dot(normed_s[:half, :], vw_ref[...], ((1,), (0,))).astype(BF16)
    branch_out.wait()
    upper_out.wait()


def causal_lower_kernel(
    q_ref, kv_ref, even_ref, odd_ref, bias_ref, given_ref, out_ref, out_s, keys_s, values_s, sems
):
    half, q_width = q_ref.shape
    kv_width = kv_ref.shape[1] // 2
    halo = chosen(even_ref, odd_ref)
    stage_keys(jnp.concatenate([halo[:, :kv_width], kv_ref[:, :kv_width]], axis=0), keys_s)
    stage_values(jnp.concatenate([halo[:, kv_width:], kv_ref[:, kv_width:]], axis=0), values_s)
    copies = []

    def queries_of(unit):
        return q_ref[:, unit.lane : unit.lane + 2 * LANES]

    def ready(unit):
        columns = pl.ds(unit.lane, 2 * LANES)
        copy = pltpu.make_async_copy(
            out_s.at[:, columns], out_ref.at[pl.ds(0, half), columns], sems.at[len(copies)]
        )
        copy.start()
        copies.append(copy)

    causal_heads(queries_of, keys_s, values_s, bias_ref, out_s, q_width, ready)
    for copy in copies:
        copy.wait()


def attention_scratch(kv_heads, keys):
    return [
        pltpu.VMEM((kv_heads, 2, keys, LANES), BF16),
        pltpu.VMEM((kv_heads, HD + TAIL, keys), BF16),
    ]


def local(
    window_queries,
    window_keys,
    window_values,
    out_weight,
    norm_gain,
    query_weight,
    key_weight,
    value_weight,
    doc_lengths,
):
    rows, q_width = window_queries.shape
    kv_width = window_keys.shape[1]
    kv_heads = kv_width // HD
    width = out_weight.shape[1]
    half = rows // 2
    chunk = 576
    dma = pltpu.SemaphoreType.DMA
    lengths, queries, keys, values = [
        in_hbm(x) for x in (doc_lengths, window_queries, window_keys, window_values)
    ]

    packed = pl.pallas_call(
        pack_kernel,
        out_shape=jax.ShapeDtypeStruct((half, 2 * kv_width), BF16),
        in_specs=hbm_specs(2),
        out_specs=vmem_specs(1)[0],
        scratch_shapes=[dma((2,))],
        compiler_params=params(16),
        cost_estimate=pl.CostEstimate(flops=10**10, bytes_accessed=10**6, transcendentals=0),
        name="pack",
    )(keys, values)
    halos = [in_vmem(x) for x in neighbours(packed, "ctx")]
    attn_s = pltpu.VMEM((q_width, half), BF16)
    (
        attn_upper, q_held, k_held, v_held, window_bias, upper_causal, lower_causal, gain
    ) = pl.pallas_call(
        window_upper_kernel,
        out_shape=(
            attn_s,
            pltpu.VMEM((rows, q_width), BF16),
            pltpu.VMEM((rows, kv_width), BF16),
            pltpu.VMEM((rows, kv_width), BF16),
            pltpu.VMEM((rows, half), F32),
            pltpu.VMEM((half, half), F32),
            pltpu.VMEM((rows, half), F32),
            pltpu.VMEM((width,), F32),
        ),
        in_specs=hbm_specs(5),
        out_specs=tuple(vmem_specs(8)),
        scratch_shapes=[pltpu.SMEM(doc_lengths.shape, jnp.int32)]
        + attention_scratch(kv_heads, half)
        + [pltpu.VMEM((half, half), F32), dma((8,))],
        compiler_params=params(8),
        name="window_upper",
    )(lengths, queries, keys, values, in_hbm(norm_gain))
    held = in_vmem(jnp.transpose(out_weight))
    own_upper = pl.pallas_call(
        functools.partial(project_upper_kernel, chunk=chunk),
        out_shape=pltpu.VMEM((width, half), BF16),
        in_specs=vmem_specs(2),
        out_specs=vmem_specs(1)[0],
        compiler_params=params(8),
        name="project_upper",
    )(held, attn_upper)
    key_held, value_held, query_held = [in_vmem(x) for x in (key_weight, value_weight, query_weight)]
    other_upper = swapped(own_upper, "head")
    own_lower = pl.pallas_call(
        functools.partial(window_lower_kernel, chunk=chunk),
        out_shape=pltpu.VMEM((width, half), BF16),
        in_specs=vmem_specs(7),
        out_specs=vmem_specs(1)[0],
        scratch_shapes=[attn_s] + attention_scratch(kv_heads, rows),
        compiler_params=params(16),
        name="window_lower",
    )(q_held, k_held, v_held, *halos, held, window_bias)
    other_lower = swapped(own_lower, "head")
    branch_upper, normed_upper, pairs_upper = pl.pallas_call(
        functools.partial(norm_upper_kernel, chunk=192),
        out_shape=(
            pltpu.VMEM((width, half), BF16),
            pltpu.VMEM((half, width), BF16),
            pltpu.VMEM((half, 2 * kv_width), BF16),
        ),
        in_specs=vmem_specs(5),
        out_specs=tuple(vmem_specs(3)),
        scratch_shapes=[pltpu.VMEM((width, half), F32)],
        compiler_params=params(16),
        name="norm_upper",
    )(own_upper, other_upper, gain, key_held, value_held)
    earlier = [in_vmem(x) for x in neighbours(pairs_upper, "ctx")]
    branch, causal_queries, pairs_lower, causal_out = pl.pallas_call(
        functools.partial(causal_upper_kernel, chunk=192),
        out_shape=(
            pltpu.HBM((width, half), BF16),
            pltpu.VMEM((half, q_width), BF16),
            pltpu.VMEM((half, 2 * kv_width), BF16),
            pltpu.HBM((rows, q_width), BF16),
        ),
        in_specs=vmem_specs(10),
        out_specs=(hbm_specs(1)[0], *vmem_specs(2), hbm_specs(1)[0]),
        scratch_shapes=[
            pltpu.VMEM((width, half), BF16),
            pltpu.VMEM((half, q_width), BF16),
            pltpu.VMEM((half, q_width), BF16),
            pltpu.VMEM((rows, width), BF16),
            pltpu.VMEM((width, half), F32),
        ]
        + attention_scratch(kv_heads, half)
        + [dma((2,))],
        compiler_params=params(16),
        name="causal_upper",
    )(
        own_lower, other_lower, gain, key_held, value_held, query_held,
        branch_upper, normed_upper, pairs_upper, upper_causal,
    )
    causal_out = pl.pallas_call(
        causal_lower_kernel,
        out_shape=pltpu.HBM((rows, q_width), BF16),
        in_specs=vmem_specs(5) + hbm_specs(1),
        out_specs=hbm_specs(1)[0],
        scratch_shapes=[pltpu.VMEM((half, q_width), BF16)]
        + attention_scratch(kv_heads, rows)
        + [dma((q_width // (2 * LANES),))],
        input_output_aliases={5: 0},
        compiler_params=params(16),
        name="causal_lower",
    )(causal_queries, pairs_lower, *earlier, lower_causal, causal_out)
    return (jnp.transpose(branch), causal_out)


def solution(mesh):
    placed = (
        P("ctx", "head"),
        P("ctx", "head"),
        P("ctx", "head"),
        P("head", None),
        P(),
        P(None, "head"),
        P(None, "head"),
        P(None, "head"),
        P(),
    )
    return jax.shard_map(
        local,
        mesh=mesh,
        in_specs=placed,
        out_specs=(P(("ctx", "head"), None), P("ctx", "head")),
        check_vma=False,
    )
```

```python
import functools

import jax
import jax.numpy as jnp
from jax import lax
from jax.experimental import pallas as pl
from jax.experimental.pallas import tpu as pltpu
from jax.sharding import PartitionSpec as P

HD = 64
WIN = 128
LANES = 128
NEG = -1e30
TAIL = 16

F32 = jnp.float32
BF16 = jnp.bfloat16
MIB = 1024 * 1024


def params(mib):
    return pltpu.CompilerParams(vmem_limit_bytes=mib * MIB)


def in_vmem(array):
    return pltpu.with_memory_space_constraint(array, pltpu.VMEM)


def in_hbm(array):
    return pltpu.with_memory_space_constraint(array, pltpu.HBM)


def hbm_specs(count):
    return [pl.BlockSpec(memory_space=pltpu.HBM)] * count


def vmem_specs(count):
    return [pl.BlockSpec(memory_space=pltpu.VMEM)] * count


def dot(a, b, dims):
    return lax.dot_general(a, b, (dims, ((), ())), preferred_element_type=F32)


def shifted(block, axis):
    size = lax.axis_size(axis)
    return lax.ppermute(block, axis, [(i, (i + 1) % size) for i in range(size)])


def swapped(block, axis):
    size = lax.axis_size(axis)
    return lax.ppermute(block, axis, [(i, size - 1 - i) for i in range(size)])


def lower_bias(lengths_ref, half, width):
    ctx = lax.axis_index("ctx")
    first = jnp.where(ctx == 0, half, 0)
    split = first + lengths_ref[2 * ctx]
    return bias_of(2 * half, half, half, first, split, width)


def upper_bias(lengths_ref, half, width):
    ctx = lax.axis_index("ctx")
    last = lengths_ref.shape[0] - 1
    split = lengths_ref[jnp.minimum(2 * ctx + 2, last)]
    split = jnp.where(ctx == lax.axis_size("ctx") - 1, 2 * half, split)
    return bias_of(half, half, 0, 0, split, width)


def bias_of(keys, rows, row_offset, first, split, width):
    key = lax.broadcasted_iota(jnp.int32, (keys, rows), 0)
    row = lax.broadcasted_iota(jnp.int32, (keys, rows), 1) + row_offset
    lowest = jnp.where(row >= split, split, first)
    if width is not None:
        lowest = jnp.maximum(lowest, row - (width - 1))
    return jnp.where((key >= lowest) & (key <= row), 0.0, NEG).astype(F32)


def stage_keys(keys, keys_ref):
    scaled = (keys.astype(F32) * HD ** (-0.5)).astype(BF16)
    lane = lax.broadcasted_iota(jnp.int32, (keys.shape[0], LANES), 1)
    zero = jnp.zeros((keys.shape[0], LANES), BF16)
    for pair in range(keys.shape[1] // LANES):
        tile = scaled[:, pair * LANES : (pair + 1) * LANES]
        turned = jnp.concatenate([tile[:, HD:], tile[:, :HD]], axis=1)
        keys_ref[2 * pair, 0] = jnp.where(lane < HD, tile, zero)
        keys_ref[2 * pair, 1] = jnp.where(lane < HD, zero, turned)
        keys_ref[2 * pair + 1, 0] = jnp.where(lane < HD, turned, zero)
        keys_ref[2 * pair + 1, 1] = jnp.where(lane < HD, zero, tile)


def stage_values(values, values_ref):
    count = values.shape[0]
    turned = jnp.transpose(values.astype(F32)).astype(BF16)
    for head in range(values.shape[1] // HD):
        values_ref[head, :HD, :] = turned[head * HD : (head + 1) * HD]
        values_ref[head, HD:, :] = jnp.ones((TAIL, count), BF16)


class Unit:
    def __init__(self, g, lane):
        self.g, self.lane = g, lane


def units_of(kv_heads, q_width):
    step = 2 * LANES
    group = q_width // kv_heads
    return [Unit(lane // group, lane) for lane in range(0, q_width, step)]


def unit_scores(queries, unit, keys_ref):
    stacked = jnp.concatenate([queries[:, :LANES], queries[:, LANES:]], axis=0)
    keys = jnp.concatenate([keys_ref[unit.g, 0], keys_ref[unit.g, 1]], axis=0)
    return dot(keys, stacked, ((1,), (1,)))


def unit_attend(scores, unit, values_ref, bias):
    count = bias.shape[0]
    wide = jnp.concatenate([bias, bias], axis=1)
    patterns = []
    for side in range(2):
        masked = scores[side * count : (side + 1) * count] + wide
        highest = jnp.max(masked, axis=0, keepdims=True)
        patterns.append(jnp.exp((masked - highest).astype(BF16)))
    weighted = dot(values_ref[unit.g], jnp.concatenate(patterns, axis=1), ((1,), (0,)))
    return weighted[:HD] * (1.0 / weighted[HD : HD + 1])


def pipelined(units, queries_of, keys_ref, values_ref, bias, write):
    count = len(units)
    queries = queries_of(units[0])
    scores = unit_scores(queries, units[0], keys_ref)
    queries = queries_of(units[1])
    for i, unit in enumerate(units):
        now = scores
        if i + 1 < count:
            scores = unit_scores(queries, units[i + 1], keys_ref)
        if i + 2 < count:
            queries = queries_of(units[i + 2])
        write(unit, unit_attend(now, unit, values_ref, bias))


def window_heads(queries_of, keys_ref, values_ref, bias_ref, out_ref, q_width):
    def write(unit, part):
        rows = part.shape[1] // 4
        rounded = part.astype(BF16)
        for side in range(2):
            for t in range(2):
                at = (side * 2 + t) * rows
                start = unit.lane + t * LANES + side * HD
                out_ref[start : start + HD, :] = rounded[:, at : at + rows]

    pipelined(units_of(keys_ref.shape[0], q_width), queries_of, keys_ref, values_ref, bias_ref[...], write)


def causal_heads(queries_of, keys_ref, values_ref, bias_ref, out_ref, q_width, ready):
    def write(unit, part):
        rows = part.shape[1] // 4
        for t in range(2):
            low = part[:, t * rows : (t + 1) * rows]
            high = part[:, (2 + t) * rows : (3 + t) * rows]
            lane = unit.lane + t * LANES
            out_ref[:, lane : lane + LANES] = jnp.transpose(
                jnp.concatenate([low, high], axis=0)
            ).astype(BF16)
        ready(unit)

    pipelined(units_of(keys_ref.shape[0], q_width), queries_of, keys_ref, values_ref, bias_ref[...], write)


def pack_kernel(k_ref, v_ref, out_ref, sems):
    half = out_ref.shape[0]
    kv_width = k_ref.shape[1]
    copies = [
        pltpu.make_async_copy(k_ref.at[pl.ds(half, half)], out_ref.at[:, pl.ds(0, kv_width)], sems.at[0]),
        pltpu.make_async_copy(
            v_ref.at[pl.ds(half, half)], out_ref.at[:, pl.ds(kv_width, kv_width)], sems.at[1]
        ),
    ]
    for copy in copies:
        copy.start()
    for copy in copies:
        copy.wait()


def window_upper_kernel(
    lengths_ref, q_ref, k_ref, v_ref, gain_ref,
    attn_ref, q_held, k_held, v_held, window_bias, upper_causal, lower_causal, gain_held,
    lengths_s, keys_s, values_s, bias_s, sems
):
    half = attn_ref.shape[1]
    upper, lower = pl.ds(half, half), pl.ds(0, half)
    first = [
        pltpu.make_async_copy(lengths_ref, lengths_s, sems.at[0]),
        pltpu.make_async_copy(k_ref.at[upper], k_held.at[upper], sems.at[1]),
        pltpu.make_async_copy(v_ref.at[upper], v_held.at[upper], sems.at[2]),
        pltpu.make_async_copy(q_ref.at[upper], q_held.at[upper], sems.at[3]),
    ]
    last = [
        pltpu.make_async_copy(k_ref.at[lower], k_held.at[lower], sems.at[4]),
        pltpu.make_async_copy(v_ref.at[lower], v_held.at[lower], sems.at[5]),
        pltpu.make_async_copy(q_ref.at[lower], q_held.at[lower], sems.at[6]),
        pltpu.make_async_copy(gain_ref, gain_held, sems.at[7]),
    ]
    for copy in first + last:
        copy.start()
    first[0].wait()
    bias_s[...] = upper_bias(lengths_s, half, WIN)
    window_bias[...] = lower_bias(lengths_s, half, WIN)
    upper_causal[...] = upper_bias(lengths_s, half, None)
    lower_causal[...] = lower_bias(lengths_s, half, None)
    first[1].wait()
    stage_keys(k_held[half:], keys_s)
    first[2].wait()
    stage_values(v_held[half:], values_s)
    first[3].wait()

    def queries_of(unit):
        return q_held[half:, unit.lane : unit.lane + 2 * LANES]

    window_heads(queries_of, keys_s, values_s, bias_s, attn_ref, q_held.shape[1])
    for copy in last:
        copy.wait()


def project(weight_ref, attn_ref, out_ref, chunk):
    for first in range(0, out_ref.shape[0], chunk):
        part = slice(first, first + chunk)
        out_ref[part, :] = dot(weight_ref[part, :], attn_ref[...], ((1,), (0,))).astype(BF16)


def project_upper_kernel(
    weight_ref, attn_ref, q_ref, k_ref, v_ref, bias_ref, out_ref, first_ref, keys_s, values_s, *, chunk
):
    half = attn_ref.shape[1]
    project(weight_ref, attn_ref, out_ref, chunk)

    @pl.when(lax.axis_index("ctx") == 0)
    def _():
        stage_keys(k_ref[:half], keys_s)
        stage_values(v_ref[:half], values_s)

        def queries_of(unit):
            return q_ref[:half, unit.lane : unit.lane + 2 * LANES]

        window_heads(queries_of, keys_s, values_s, bias_ref.at[pl.ds(half, half)], first_ref, q_ref.shape[1])


def window_lower_kernel(
    q_ref, k_ref, v_ref, halo_ref, weight_ref, bias_ref, first_ref,
    out_ref, attn_s, keys_s, values_s, *, chunk
):
    half = halo_ref.shape[0]
    kv_width = k_ref.shape[1]
    ctx = lax.axis_index("ctx")

    @pl.when(ctx == 0)
    def _():
        attn_s[...] = first_ref[...]

    @pl.when(ctx != 0)
    def _():
        stage_keys(jnp.concatenate([halo_ref[:, :kv_width], k_ref[:half]], axis=0), keys_s)
        stage_values(jnp.concatenate([halo_ref[:, kv_width:], v_ref[:half]], axis=0), values_s)

        def queries_of(unit):
            return q_ref[:half, unit.lane : unit.lane + 2 * LANES]

        window_heads(queries_of, keys_s, values_s, bias_ref, attn_s, q_ref.shape[1])

    project(weight_ref, attn_s, out_ref, chunk)


def add_and_norm(own_ref, other_ref, gain_ref, branch_ref, normed_ref, first_row, sum_s, keep_ref, chunk):
    width, rows = own_ref.shape
    head = lax.axis_index("head")

    def add(c, squares):
        part = pl.ds(pl.multiple_of(c * chunk, 16), chunk)
        total = own_ref[part, :].astype(F32) + other_ref[part, :].astype(F32)
        sum_s[part, :] = total
        rounded = total.astype(BF16)
        if keep_ref is not None:
            rounded = jnp.where(head == 0, rounded, keep_ref[part, :])
        branch_ref[part, :] = rounded
        return squares + jnp.sum(total * total, axis=0, keepdims=True)

    squares = lax.fori_loop(0, width // chunk, add, jnp.zeros((1, rows), F32))
    factor = lax.rsqrt(squares * (1.0 / width) + 1e-05)
    for first in range(0, width, LANES):
        last = min(first + LANES, width)
        piece = jnp.transpose(sum_s[first:last, :] * factor) * gain_ref[first:last][None, :]
        normed_ref[first_row : first_row + rows, first:last] = piece.astype(BF16)


def norm_upper_kernel(
    own_ref, other_ref, gain_ref, kw_ref, vw_ref, branch_ref, normed_ref, kv_ref, sum_s, *, chunk
):
    add_and_norm(own_ref, other_ref, gain_ref, branch_ref, normed_ref, 0, sum_s, None, chunk)
    kv_width = kw_ref.shape[1]
    kv_ref[:, :kv_width] = dot(normed_ref[...], kw_ref[...], ((1,), (0,))).astype(BF16)
    kv_ref[:, kv_width:] = dot(normed_ref[...], vw_ref[...], ((1,), (0,))).astype(BF16)


def causal_upper_kernel(
    own_ref, other_ref, gain_ref, kw_ref, vw_ref, qw_ref, kept_ref, normed_ref, kv_up_ref, bias_ref,
    lower_bias_ref, branch_ref, q_ref, kv_ref, out_ref,
    branch_s, out_s, upper_q_s, normed_s, sum_s, keys_s, values_s, sems, *, chunk
):
    half = own_ref.shape[1]
    kv_width = kw_ref.shape[1]
    q_width = qw_ref.shape[1]
    normed_s[half:, :] = normed_ref[...]
    add_and_norm(own_ref, other_ref, gain_ref, branch_s, normed_s, 0, sum_s, kept_ref, chunk)
    branch_out = pltpu.make_async_copy(branch_s, branch_ref, sems.at[0])
    branch_out.start()
    stage_keys(kv_up_ref[:, :kv_width], keys_s)
    stage_values(kv_up_ref[:, kv_width:], values_s)

    piece = q_width // 2
    for first in range(0, q_width, piece):
        columns = slice(first, first + piece)
        queries = dot(normed_s[...], qw_ref[:, columns], ((1,), (0,))).astype(BF16)
        q_ref[:, columns] = queries[:half]
        upper_q_s[:, columns] = queries[half:]

    def queries_of(unit):
        return upper_q_s[:, unit.lane : unit.lane + 2 * LANES]

    causal_heads(queries_of, keys_s, values_s, bias_ref, out_s, q_width, lambda unit: None)
    upper_out = pltpu.make_async_copy(out_s, out_ref.at[pl.ds(half, half)], sems.at[1])
    upper_out.start()
    kv_ref[:, :kv_width] = dot(normed_s[:half, :], kw_ref[...], ((1,), (0,))).astype(BF16)
    kv_ref[:, kv_width:] = dot(normed_s[:half, :], vw_ref[...], ((1,), (0,))).astype(BF16)
    branch_out.wait()
    upper_out.wait()

    @pl.when(lax.axis_index("ctx") == 0)
    def _():
        stage_keys(kv_ref[:, :kv_width], keys_s)
        stage_values(kv_ref[:, kv_width:], values_s)

        def lower_queries_of(unit):
            return q_ref[:, unit.lane : unit.lane + 2 * LANES]

        causal_heads(
            lower_queries_of, keys_s, values_s, lower_bias_ref.at[pl.ds(half, half)], out_s, q_width,
            lambda unit: None,
        )
        lower_out = pltpu.make_async_copy(out_s, out_ref.at[pl.ds(0, half)], sems.at[2])
        lower_out.start()
        lower_out.wait()


def causal_lower_kernel(
    q_ref, kv_ref, halo_ref, bias_ref, given_ref, out_ref, out_s, keys_s, values_s, sems
):
    half, q_width = q_ref.shape
    kv_width = kv_ref.shape[1] // 2

    @pl.when(lax.axis_index("ctx") != 0)
    def _():
        stage_keys(jnp.concatenate([halo_ref[:, :kv_width], kv_ref[:, :kv_width]], axis=0), keys_s)
        stage_values(jnp.concatenate([halo_ref[:, kv_width:], kv_ref[:, kv_width:]], axis=0), values_s)
        copies = []

        def queries_of(unit):
            return q_ref[:, unit.lane : unit.lane + 2 * LANES]

        def ready(unit):
            columns = pl.ds(unit.lane, 2 * LANES)
            copy = pltpu.make_async_copy(
                out_s.at[:, columns], out_ref.at[pl.ds(0, half), columns], sems.at[len(copies)]
            )
            copy.start()
            copies.append(copy)

        causal_heads(queries_of, keys_s, values_s, bias_ref, out_s, q_width, ready)
        for copy in copies:
            copy.wait()


def attention_scratch(kv_heads, keys):
    return [
        pltpu.VMEM((kv_heads, 2, keys, LANES), BF16),
        pltpu.VMEM((kv_heads, HD + TAIL, keys), BF16),
    ]


def local(
    window_queries,
    window_keys,
    window_values,
    out_weight,
    norm_gain,
    query_weight,
    key_weight,
    value_weight,
    doc_lengths,
):
    rows, q_width = window_queries.shape
    kv_width = window_keys.shape[1]
    kv_heads = kv_width // HD
    width = out_weight.shape[1]
    half = rows // 2
    chunk = 576
    dma = pltpu.SemaphoreType.DMA
    lengths, queries, keys, values = [
        in_hbm(x) for x in (doc_lengths, window_queries, window_keys, window_values)
    ]

    packed = pl.pallas_call(
        pack_kernel,
        out_shape=jax.ShapeDtypeStruct((half, 2 * kv_width), BF16),
        in_specs=hbm_specs(2),
        out_specs=vmem_specs(1)[0],
        scratch_shapes=[dma((2,))],
        compiler_params=params(16),
        cost_estimate=pl.CostEstimate(flops=10**10, bytes_accessed=10**6, transcendentals=0),
        name="pack",
    )(keys, values)
    halo = shifted(packed, "ctx")
    attn_s = pltpu.VMEM((q_width, half), BF16)
    (
        attn_upper, q_held, k_held, v_held, window_bias, upper_causal, lower_causal, gain
    ) = pl.pallas_call(
        window_upper_kernel,
        out_shape=(
            attn_s,
            pltpu.VMEM((rows, q_width), BF16),
            pltpu.VMEM((rows, kv_width), BF16),
            pltpu.VMEM((rows, kv_width), BF16),
            pltpu.VMEM((rows, half), F32),
            pltpu.VMEM((half, half), F32),
            pltpu.VMEM((rows, half), F32),
            pltpu.VMEM((width,), F32),
        ),
        in_specs=hbm_specs(5),
        out_specs=tuple(vmem_specs(8)),
        scratch_shapes=[pltpu.SMEM(doc_lengths.shape, jnp.int32)]
        + attention_scratch(kv_heads, half)
        + [pltpu.VMEM((half, half), F32), dma((8,))],
        compiler_params=params(8),
        name="window_upper",
    )(lengths, queries, keys, values, in_hbm(norm_gain))
    held = in_vmem(jnp.transpose(out_weight))
    own_upper, attn_first = pl.pallas_call(
        functools.partial(project_upper_kernel, chunk=chunk),
        out_shape=(pltpu.VMEM((width, half), BF16), attn_s),
        in_specs=vmem_specs(6),
        out_specs=tuple(vmem_specs(2)),
        scratch_shapes=attention_scratch(kv_heads, half),
        compiler_params=params(8),
        name="project_upper",
    )(held, attn_upper, q_held, k_held, v_held, window_bias)
    key_held, value_held, query_held = [in_vmem(x) for x in (key_weight, value_weight, query_weight)]
    other_upper = swapped(own_upper, "head")
    own_lower = pl.pallas_call(
        functools.partial(window_lower_kernel, chunk=chunk),
        out_shape=pltpu.VMEM((width, half), BF16),
        in_specs=vmem_specs(7),
        out_specs=vmem_specs(1)[0],
        scratch_shapes=[attn_s] + attention_scratch(kv_heads, rows),
        compiler_params=params(16),
        name="window_lower",
    )(q_held, k_held, v_held, in_vmem(halo), held, window_bias, attn_first)
    other_lower = swapped(own_lower, "head")
    branch_upper, normed_upper, pairs_upper = pl.pallas_call(
        functools.partial(norm_upper_kernel, chunk=192),
        out_shape=(
            pltpu.VMEM((width, half), BF16),
            pltpu.VMEM((half, width), BF16),
            pltpu.VMEM((half, 2 * kv_width), BF16),
        ),
        in_specs=vmem_specs(5),
        out_specs=tuple(vmem_specs(3)),
        scratch_shapes=[pltpu.VMEM((width, half), F32)],
        compiler_params=params(16),
        name="norm_upper",
    )(own_upper, other_upper, gain, key_held, value_held)
    earlier = shifted(pairs_upper, "ctx")
    branch, causal_queries, pairs_lower, causal_out = pl.pallas_call(
        functools.partial(causal_upper_kernel, chunk=192),
        out_shape=(
            pltpu.HBM((width, half), BF16),
            pltpu.VMEM((half, q_width), BF16),
            pltpu.VMEM((half, 2 * kv_width), BF16),
            pltpu.HBM((rows, q_width), BF16),
        ),
        in_specs=vmem_specs(11),
        out_specs=(hbm_specs(1)[0], *vmem_specs(2), hbm_specs(1)[0]),
        scratch_shapes=[
            pltpu.VMEM((width, half), BF16),
            pltpu.VMEM((half, q_width), BF16),
            pltpu.VMEM((half, q_width), BF16),
            pltpu.VMEM((rows, width), BF16),
            pltpu.VMEM((width, half), F32),
        ]
        + attention_scratch(kv_heads, half)
        + [dma((3,))],
        compiler_params=params(16),
        name="causal_upper",
    )(
        own_lower, other_lower, gain, key_held, value_held, query_held,
        branch_upper, normed_upper, pairs_upper, upper_causal, lower_causal,
    )
    causal_out = pl.pallas_call(
        causal_lower_kernel,
        out_shape=pltpu.HBM((rows, q_width), BF16),
        in_specs=vmem_specs(4) + hbm_specs(1),
        out_specs=hbm_specs(1)[0],
        scratch_shapes=[pltpu.VMEM((half, q_width), BF16)]
        + attention_scratch(kv_heads, rows)
        + [dma((q_width // (2 * LANES),))],
        input_output_aliases={4: 0},
        compiler_params=params(16),
        name="causal_lower",
    )(causal_queries, pairs_lower, in_vmem(earlier), lower_causal, causal_out)
    return (jnp.transpose(branch), causal_out)


def solution(mesh):
    placed = (
        P("ctx", "head"),
        P("ctx", "head"),
        P("ctx", "head"),
        P("head", None),
        P(),
        P(None, "head"),
        P(None, "head"),
        P(None, "head"),
        P(),
    )
    return jax.shard_map(
        local,
        mesh=mesh,
        in_specs=placed,
        out_specs=(P(("ctx", "head"), None), P("ctx", "head")),
        check_vma=False,
    )
```

```python
import functools

import jax
import jax.numpy as jnp
from jax import lax
from jax.experimental import pallas as pl
from jax.experimental.pallas import tpu as pltpu
from jax.sharding import PartitionSpec as P

HD = 64
WIN = 128
LANES = 128
NEG = -1e30
TAIL = 16

F32 = jnp.float32
BF16 = jnp.bfloat16
MIB = 1024 * 1024


def params(mib):
    return pltpu.CompilerParams(vmem_limit_bytes=mib * MIB)


def in_vmem(array):
    return pltpu.with_memory_space_constraint(array, pltpu.VMEM)


def in_hbm(array):
    return pltpu.with_memory_space_constraint(array, pltpu.HBM)


def hbm_specs(count):
    return [pl.BlockSpec(memory_space=pltpu.HBM)] * count


def vmem_specs(count):
    return [pl.BlockSpec(memory_space=pltpu.VMEM)] * count


def dot(a, b, dims):
    return lax.dot_general(a, b, (dims, ((), ())), preferred_element_type=F32)


def shifted(block, axis):
    size = lax.axis_size(axis)
    return lax.ppermute(block, axis, [(i, (i + 1) % size) for i in range(size)])


def swapped(block, axis):
    size = lax.axis_size(axis)
    return lax.ppermute(block, axis, [(i, size - 1 - i) for i in range(size)])


def lower_bias(lengths_ref, half, width):
    ctx = lax.axis_index("ctx")
    first = jnp.where(ctx == 0, half, 0)
    split = first + lengths_ref[2 * ctx]
    return bias_of(2 * half, half, half, first, split, width)


def upper_bias(lengths_ref, half, width):
    ctx = lax.axis_index("ctx")
    last = lengths_ref.shape[0] - 1
    split = lengths_ref[jnp.minimum(2 * ctx + 2, last)]
    split = jnp.where(ctx == lax.axis_size("ctx") - 1, 2 * half, split)
    return bias_of(half, half, 0, 0, split, width)


def bias_of(keys, rows, row_offset, first, split, width):
    key = lax.broadcasted_iota(jnp.int32, (keys, rows), 0)
    row = lax.broadcasted_iota(jnp.int32, (keys, rows), 1) + row_offset
    lowest = jnp.where(row >= split, split, first)
    if width is not None:
        lowest = jnp.maximum(lowest, row - (width - 1))
    return jnp.where((key >= lowest) & (key <= row), 0.0, NEG).astype(F32)


def stage_keys(keys, keys_ref):
    scaled = (keys.astype(F32) * HD ** (-0.5)).astype(BF16)
    lane = lax.broadcasted_iota(jnp.int32, (keys.shape[0], LANES), 1)
    zero = jnp.zeros((keys.shape[0], LANES), BF16)
    for pair in range(keys.shape[1] // LANES):
        tile = scaled[:, pair * LANES : (pair + 1) * LANES]
        turned = jnp.concatenate([tile[:, HD:], tile[:, :HD]], axis=1)
        keys_ref[2 * pair, 0] = jnp.where(lane < HD, tile, zero)
        keys_ref[2 * pair, 1] = jnp.where(lane < HD, zero, turned)
        keys_ref[2 * pair + 1, 0] = jnp.where(lane < HD, turned, zero)
        keys_ref[2 * pair + 1, 1] = jnp.where(lane < HD, zero, tile)


def stage_values(values, values_ref):
    count = values.shape[0]
    turned = jnp.transpose(values.astype(F32)).astype(BF16)
    for head in range(values.shape[1] // HD):
        values_ref[head, :HD, :] = turned[head * HD : (head + 1) * HD]
        values_ref[head, HD:, :] = jnp.ones((TAIL, count), BF16)


class Unit:
    def __init__(self, g, lane):
        self.g, self.lane = g, lane


def units_of(kv_heads, q_width):
    step = 2 * LANES
    group = q_width // kv_heads
    return [Unit(lane // group, lane) for lane in range(0, q_width, step)]


def unit_scores(queries, unit, keys_ref):
    stacked = jnp.concatenate([queries[:, :LANES], queries[:, LANES:]], axis=0)
    keys = jnp.concatenate([keys_ref[unit.g, 0], keys_ref[unit.g, 1]], axis=0)
    return dot(keys, stacked, ((1,), (1,)))


def unit_weighted(scores, unit, values_ref, bias):
    count = bias.shape[0]
    wide = jnp.concatenate([bias, bias], axis=1)
    patterns = []
    for side in range(2):
        masked = scores[side * count : (side + 1) * count] + wide
        highest = jnp.max(masked, axis=0, keepdims=True)
        patterns.append(jnp.exp((masked - highest).astype(BF16)))
    return dot(values_ref[unit.g], jnp.concatenate(patterns, axis=1), ((1,), (0,)))


def pipelined(units, queries_of, keys_ref, values_ref, bias, write):
    count = len(units)
    scores = [unit_scores(queries_of(unit), unit, keys_ref) for unit in units[:2]]

    def finish(unit, weighted):
        write(unit, weighted[:HD] * (1.0 / weighted[HD : HD + 1]))

    before = None
    for i, unit in enumerate(units):
        now = scores.pop(0)
        if i + 2 < count:
            scores.append(unit_scores(queries_of(units[i + 2]), units[i + 2], keys_ref))
        weighted = unit_weighted(now, unit, values_ref, bias)
        if before is not None:
            finish(*before)
        before = (unit, weighted)
    finish(*before)


def window_heads(queries_of, keys_ref, values_ref, bias_ref, out_ref, q_width):
    def write(unit, part):
        rows = part.shape[1] // 4
        rounded = part.astype(BF16)
        for side in range(2):
            for t in range(2):
                at = (side * 2 + t) * rows
                start = unit.lane + t * LANES + side * HD
                out_ref[start : start + HD, :] = rounded[:, at : at + rows]

    pipelined(units_of(keys_ref.shape[0], q_width), queries_of, keys_ref, values_ref, bias_ref[...], write)


def causal_heads(queries_of, keys_ref, values_ref, bias_ref, out_ref, q_width, ready):
    def write(unit, part):
        rows = part.shape[1] // 4
        for t in range(2):
            low = part[:, t * rows : (t + 1) * rows]
            high = part[:, (2 + t) * rows : (3 + t) * rows]
            lane = unit.lane + t * LANES
            out_ref[:, lane : lane + LANES] = jnp.transpose(
                jnp.concatenate([low, high], axis=0)
            ).astype(BF16)
        ready(unit)

    pipelined(units_of(keys_ref.shape[0], q_width), queries_of, keys_ref, values_ref, bias_ref[...], write)


def pack_kernel(k_ref, v_ref, out_ref, sems):
    half = out_ref.shape[0]
    kv_width = k_ref.shape[1]
    copies = [
        pltpu.make_async_copy(k_ref.at[pl.ds(half, half)], out_ref.at[:, pl.ds(0, kv_width)], sems.at[0]),
        pltpu.make_async_copy(
            v_ref.at[pl.ds(half, half)], out_ref.at[:, pl.ds(kv_width, kv_width)], sems.at[1]
        ),
    ]
    for copy in copies:
        copy.start()
    for copy in copies:
        copy.wait()


def window_upper_kernel(
    lengths_ref, q_ref, k_ref, v_ref, gain_ref,
    attn_ref, q_held, k_held, v_held, window_bias, upper_causal, lower_causal, gain_held,
    lengths_s, keys_s, values_s, bias_s, sems
):
    half = attn_ref.shape[1]
    upper, lower = pl.ds(half, half), pl.ds(0, half)
    first = [
        pltpu.make_async_copy(lengths_ref, lengths_s, sems.at[0]),
        pltpu.make_async_copy(k_ref.at[upper], k_held.at[upper], sems.at[1]),
        pltpu.make_async_copy(v_ref.at[upper], v_held.at[upper], sems.at[2]),
        pltpu.make_async_copy(q_ref.at[upper], q_held.at[upper], sems.at[3]),
    ]
    last = [
        pltpu.make_async_copy(k_ref.at[lower], k_held.at[lower], sems.at[4]),
        pltpu.make_async_copy(v_ref.at[lower], v_held.at[lower], sems.at[5]),
        pltpu.make_async_copy(q_ref.at[lower], q_held.at[lower], sems.at[6]),
        pltpu.make_async_copy(gain_ref, gain_held, sems.at[7]),
    ]
    for copy in first + last:
        copy.start()
    first[0].wait()
    bias_s[...] = upper_bias(lengths_s, half, WIN)
    window_bias[...] = lower_bias(lengths_s, half, WIN)
    upper_causal[...] = upper_bias(lengths_s, half, None)
    lower_causal[...] = lower_bias(lengths_s, half, None)
    first[1].wait()
    stage_keys(k_held[half:], keys_s)
    first[2].wait()
    stage_values(v_held[half:], values_s)
    first[3].wait()

    def queries_of(unit):
        return q_held[half:, unit.lane : unit.lane + 2 * LANES]

    window_heads(queries_of, keys_s, values_s, bias_s, attn_ref, q_held.shape[1])
    for copy in last:
        copy.wait()


def project(weight_ref, attn_ref, out_ref, chunk):
    for first in range(0, out_ref.shape[0], chunk):
        part = slice(first, first + chunk)
        out_ref[part, :] = dot(weight_ref[part, :], attn_ref[...], ((1,), (0,))).astype(BF16)


def project_upper_kernel(
    weight_ref, attn_ref, q_ref, k_ref, v_ref, bias_ref, out_ref, first_ref, keys_s, values_s, *, chunk
):
    half = attn_ref.shape[1]
    project(weight_ref, attn_ref, out_ref, chunk)

    @pl.when(lax.axis_index("ctx") == 0)
    def _():
        stage_keys(k_ref[:half], keys_s)
        stage_values(v_ref[:half], values_s)

        def queries_of(unit):
            return q_ref[:half, unit.lane : unit.lane + 2 * LANES]

        window_heads(queries_of, keys_s, values_s, bias_ref.at[pl.ds(half, half)], first_ref, q_ref.shape[1])


def window_lower_kernel(
    q_ref, k_ref, v_ref, halo_ref, weight_ref, bias_ref, first_ref,
    out_ref, attn_s, keys_s, values_s, *, chunk
):
    half = halo_ref.shape[0]
    kv_width = k_ref.shape[1]
    ctx = lax.axis_index("ctx")

    @pl.when(ctx == 0)
    def _():
        attn_s[...] = first_ref[...]

    @pl.when(ctx != 0)
    def _():
        stage_keys(jnp.concatenate([halo_ref[:, :kv_width], k_ref[:half]], axis=0), keys_s)
        stage_values(jnp.concatenate([halo_ref[:, kv_width:], v_ref[:half]], axis=0), values_s)

        def queries_of(unit):
            return q_ref[:half, unit.lane : unit.lane + 2 * LANES]

        window_heads(queries_of, keys_s, values_s, bias_ref, attn_s, q_ref.shape[1])

    project(weight_ref, attn_s, out_ref, chunk)


def add_and_norm(own_ref, other_ref, gain_ref, branch_ref, normed_ref, first_row, sum_s, keep_ref, chunk):
    width, rows = own_ref.shape
    head = lax.axis_index("head")

    def add(c, squares):
        part = pl.ds(pl.multiple_of(c * chunk, 16), chunk)
        total = own_ref[part, :].astype(F32) + other_ref[part, :].astype(F32)
        sum_s[part, :] = total
        rounded = total.astype(BF16)
        if keep_ref is not None:
            rounded = jnp.where(head == 0, rounded, keep_ref[part, :])
        branch_ref[part, :] = rounded
        return squares + jnp.sum(total * total, axis=0, keepdims=True)

    squares = lax.fori_loop(0, width // chunk, add, jnp.zeros((1, rows), F32))
    factor = lax.rsqrt(squares * (1.0 / width) + 1e-05)
    for first in range(0, width, LANES):
        last = min(first + LANES, width)
        piece = jnp.transpose(sum_s[first:last, :] * factor) * gain_ref[first:last][None, :]
        normed_ref[first_row : first_row + rows, first:last] = piece.astype(BF16)


def norm_upper_kernel(
    own_ref, other_ref, gain_ref, kw_ref, vw_ref, branch_ref, normed_ref, kv_ref, sum_s, *, chunk
):
    add_and_norm(own_ref, other_ref, gain_ref, branch_ref, normed_ref, 0, sum_s, None, chunk)
    kv_width = kw_ref.shape[1]
    kv_ref[:, :kv_width] = dot(normed_ref[...], kw_ref[...], ((1,), (0,))).astype(BF16)
    kv_ref[:, kv_width:] = dot(normed_ref[...], vw_ref[...], ((1,), (0,))).astype(BF16)


def causal_upper_kernel(
    own_ref, other_ref, gain_ref, kw_ref, vw_ref, qw_ref, kept_ref, normed_ref, kv_up_ref, bias_ref,
    lower_bias_ref, branch_ref, q_ref, kv_ref, out_ref,
    branch_s, out_s, upper_q_s, normed_s, sum_s, keys_s, values_s, sems, unit_sems, *, chunk
):
    half = own_ref.shape[1]
    kv_width = kw_ref.shape[1]
    q_width = qw_ref.shape[1]
    normed_s[half:, :] = normed_ref[...]
    add_and_norm(own_ref, other_ref, gain_ref, branch_s, normed_s, 0, sum_s, kept_ref, chunk)
    branch_out = pltpu.make_async_copy(branch_s, branch_ref, sems.at[0])
    branch_out.start()
    stage_keys(kv_up_ref[:, :kv_width], keys_s)
    stage_values(kv_up_ref[:, kv_width:], values_s)

    piece = q_width // 2
    for first in range(0, q_width, piece):
        columns = slice(first, first + piece)
        queries = dot(normed_s[...], qw_ref[:, columns], ((1,), (0,))).astype(BF16)
        q_ref[:, columns] = queries[:half]
        upper_q_s[:, columns] = queries[half:]

    def queries_of(unit):
        return upper_q_s[:, unit.lane : unit.lane + 2 * LANES]

    causal_heads(queries_of, keys_s, values_s, bias_ref, out_s, q_width, lambda unit: None)
    upper_out = pltpu.make_async_copy(out_s, out_ref.at[pl.ds(half, half)], sems.at[1])
    upper_out.start()
    kv_ref[:, :kv_width] = dot(normed_s[:half, :], kw_ref[...], ((1,), (0,))).astype(BF16)
    kv_ref[:, kv_width:] = dot(normed_s[:half, :], vw_ref[...], ((1,), (0,))).astype(BF16)
    branch_out.wait()
    upper_out.wait()

    @pl.when(lax.axis_index("ctx") == 0)
    def _():
        stage_keys(kv_ref[:, :kv_width], keys_s)
        stage_values(kv_ref[:, kv_width:], values_s)
        attend_lower(q_ref, keys_s, values_s, lower_bias_ref.at[pl.ds(half, half)], out_s, out_ref, unit_sems)


def attend_lower(q_ref, keys_s, values_s, bias_ref, out_s, out_ref, sems):
    half, q_width = q_ref.shape
    copies = []

    def queries_of(unit):
        return q_ref[:, unit.lane : unit.lane + 2 * LANES]

    def ready(unit):
        columns = pl.ds(unit.lane, 2 * LANES)
        copy = pltpu.make_async_copy(
            out_s.at[:, columns], out_ref.at[pl.ds(0, half), columns], sems.at[len(copies)]
        )
        copy.start()
        copies.append(copy)

    causal_heads(queries_of, keys_s, values_s, bias_ref, out_s, q_width, ready)
    for copy in copies:
        copy.wait()


def causal_lower_kernel(
    q_ref, kv_ref, halo_ref, bias_ref, given_ref, out_ref, out_s, keys_s, values_s, sems
):
    half, q_width = q_ref.shape
    kv_width = kv_ref.shape[1] // 2

    @pl.when(lax.axis_index("ctx") != 0)
    def _():
        stage_keys(jnp.concatenate([halo_ref[:, :kv_width], kv_ref[:, :kv_width]], axis=0), keys_s)
        stage_values(jnp.concatenate([halo_ref[:, kv_width:], kv_ref[:, kv_width:]], axis=0), values_s)
        attend_lower(q_ref, keys_s, values_s, bias_ref, out_s, out_ref, sems)


def attention_scratch(kv_heads, keys):
    return [
        pltpu.VMEM((kv_heads, 2, keys, LANES), BF16),
        pltpu.VMEM((kv_heads, HD + TAIL, keys), BF16),
    ]


def local(
    window_queries,
    window_keys,
    window_values,
    out_weight,
    norm_gain,
    query_weight,
    key_weight,
    value_weight,
    doc_lengths,
):
    rows, q_width = window_queries.shape
    kv_width = window_keys.shape[1]
    kv_heads = kv_width // HD
    width = out_weight.shape[1]
    half = rows // 2
    chunk = width // 2
    dma = pltpu.SemaphoreType.DMA
    lengths, queries, keys, values = [
        in_hbm(x) for x in (doc_lengths, window_queries, window_keys, window_values)
    ]

    packed = pl.pallas_call(
        pack_kernel,
        out_shape=jax.ShapeDtypeStruct((half, 2 * kv_width), BF16),
        in_specs=hbm_specs(2),
        out_specs=vmem_specs(1)[0],
        scratch_shapes=[dma((2,))],
        compiler_params=params(16),
        cost_estimate=pl.CostEstimate(flops=10**10, bytes_accessed=10**6, transcendentals=0),
        name="pack",
    )(keys, values)
    halo = shifted(packed, "ctx")
    attn_s = pltpu.VMEM((q_width, half), BF16)
    (
        attn_upper, q_held, k_held, v_held, window_bias, upper_causal, lower_causal, gain
    ) = pl.pallas_call(
        window_upper_kernel,
        out_shape=(
            attn_s,
            pltpu.VMEM((rows, q_width), BF16),
            pltpu.VMEM((rows, kv_width), BF16),
            pltpu.VMEM((rows, kv_width), BF16),
            pltpu.VMEM((rows, half), F32),
            pltpu.VMEM((half, half), F32),
            pltpu.VMEM((rows, half), F32),
            pltpu.VMEM((width,), F32),
        ),
        in_specs=hbm_specs(5),
        out_specs=tuple(vmem_specs(8)),
        scratch_shapes=[pltpu.SMEM(doc_lengths.shape, jnp.int32)]
        + attention_scratch(kv_heads, half)
        + [pltpu.VMEM((half, half), F32), dma((8,))],
        compiler_params=params(8),
        name="window_upper",
    )(lengths, queries, keys, values, in_hbm(norm_gain))
    held = in_vmem(jnp.transpose(out_weight))
    own_upper, attn_first = pl.pallas_call(
        functools.partial(project_upper_kernel, chunk=chunk),
        out_shape=(pltpu.VMEM((width, half), BF16), attn_s),
        in_specs=vmem_specs(6),
        out_specs=tuple(vmem_specs(2)),
        scratch_shapes=attention_scratch(kv_heads, half),
        compiler_params=params(8),
        name="project_upper",
    )(held, attn_upper, q_held, k_held, v_held, window_bias)
    key_held, value_held, query_held = [in_vmem(x) for x in (key_weight, value_weight, query_weight)]
    other_upper = swapped(own_upper, "head")
    own_lower = pl.pallas_call(
        functools.partial(window_lower_kernel, chunk=chunk),
        out_shape=pltpu.VMEM((width, half), BF16),
        in_specs=vmem_specs(7),
        out_specs=vmem_specs(1)[0],
        scratch_shapes=[attn_s] + attention_scratch(kv_heads, rows),
        compiler_params=params(16),
        name="window_lower",
    )(q_held, k_held, v_held, in_vmem(halo), held, window_bias, attn_first)
    other_lower = swapped(own_lower, "head")
    branch_upper, normed_upper, pairs_upper = pl.pallas_call(
        functools.partial(norm_upper_kernel, chunk=192),
        out_shape=(
            pltpu.VMEM((width, half), BF16),
            pltpu.VMEM((half, width), BF16),
            pltpu.VMEM((half, 2 * kv_width), BF16),
        ),
        in_specs=vmem_specs(5),
        out_specs=tuple(vmem_specs(3)),
        scratch_shapes=[pltpu.VMEM((width, half), F32)],
        compiler_params=params(16),
        name="norm_upper",
    )(own_upper, other_upper, gain, key_held, value_held)
    earlier = shifted(pairs_upper, "ctx")
    branch, causal_queries, pairs_lower, causal_out = pl.pallas_call(
        functools.partial(causal_upper_kernel, chunk=192),
        out_shape=(
            pltpu.HBM((width, half), BF16),
            pltpu.VMEM((half, q_width), BF16),
            pltpu.VMEM((half, 2 * kv_width), BF16),
            pltpu.HBM((rows, q_width), BF16),
        ),
        in_specs=vmem_specs(11),
        out_specs=(hbm_specs(1)[0], *vmem_specs(2), hbm_specs(1)[0]),
        scratch_shapes=[
            pltpu.VMEM((width, half), BF16),
            pltpu.VMEM((half, q_width), BF16),
            pltpu.VMEM((half, q_width), BF16),
            pltpu.VMEM((rows, width), BF16),
            pltpu.VMEM((width, half), F32),
        ]
        + attention_scratch(kv_heads, half)
        + [dma((2,)), dma((q_width // (2 * LANES),))],
        compiler_params=params(16),
        name="causal_upper",
    )(
        own_lower, other_lower, gain, key_held, value_held, query_held,
        branch_upper, normed_upper, pairs_upper, upper_causal, lower_causal,
    )
    causal_out = pl.pallas_call(
        causal_lower_kernel,
        out_shape=pltpu.HBM((rows, q_width), BF16),
        in_specs=vmem_specs(4) + hbm_specs(1),
        out_specs=hbm_specs(1)[0],
        scratch_shapes=[pltpu.VMEM((half, q_width), BF16)]
        + attention_scratch(kv_heads, rows)
        + [dma((q_width // (2 * LANES),))],
        input_output_aliases={4: 0},
        compiler_params=params(16),
        name="causal_lower",
    )(causal_queries, pairs_lower, in_vmem(earlier), lower_causal, causal_out)
    return (jnp.transpose(branch), causal_out)


def solution(mesh):
    placed = (
        P("ctx", "head"),
        P("ctx", "head"),
        P("ctx", "head"),
        P("head", None),
        P(),
        P(None, "head"),
        P(None, "head"),
        P(None, "head"),
        P(),
    )
    return jax.shard_map(
        local,
        mesh=mesh,
        in_specs=placed,
        out_specs=(P(("ctx", "head"), None), P("ctx", "head")),
        check_vma=False,
    )
```

```python
import functools

import jax
import jax.numpy as jnp
from jax import lax
from jax.experimental import pallas as pl
from jax.experimental.pallas import tpu as pltpu
from jax.sharding import PartitionSpec as P

HD = 64
WIN = 128
LANES = 128
NEG = -1e30
TAIL = 16

F32 = jnp.float32
BF16 = jnp.bfloat16
MIB = 1024 * 1024


def params(mib):
    return pltpu.CompilerParams(vmem_limit_bytes=mib * MIB)


def in_vmem(array):
    return pltpu.with_memory_space_constraint(array, pltpu.VMEM)


def in_hbm(array):
    return pltpu.with_memory_space_constraint(array, pltpu.HBM)


def hbm_specs(count):
    return [pl.BlockSpec(memory_space=pltpu.HBM)] * count


def vmem_specs(count):
    return [pl.BlockSpec(memory_space=pltpu.VMEM)] * count


def dot(a, b, dims):
    return lax.dot_general(a, b, (dims, ((), ())), preferred_element_type=F32)


def shifted(block, axis):
    size = lax.axis_size(axis)
    return lax.ppermute(block, axis, [(i, (i + 1) % size) for i in range(size)])


def swapped(block, axis):
    size = lax.axis_size(axis)
    return lax.ppermute(block, axis, [(i, size - 1 - i) for i in range(size)])


def lower_bias(lengths_ref, half, width):
    ctx = lax.axis_index("ctx")
    first = jnp.where(ctx == 0, half, 0)
    split = first + lengths_ref[2 * ctx]
    return bias_of(2 * half, half, half, first, split, width)


def upper_bias(lengths_ref, half, width):
    ctx = lax.axis_index("ctx")
    last = lengths_ref.shape[0] - 1
    split = lengths_ref[jnp.minimum(2 * ctx + 2, last)]
    split = jnp.where(ctx == lax.axis_size("ctx") - 1, 2 * half, split)
    return bias_of(half, half, 0, 0, split, width)


def bias_of(keys, rows, row_offset, first, split, width):
    key = lax.broadcasted_iota(jnp.int32, (keys, rows), 0)
    row = lax.broadcasted_iota(jnp.int32, (keys, rows), 1) + row_offset
    lowest = jnp.where(row >= split, split, first)
    if width is not None:
        lowest = jnp.maximum(lowest, row - (width - 1))
    return jnp.where((key >= lowest) & (key <= row), 0.0, NEG).astype(F32)


def stage_keys(keys, keys_ref):
    scaled = (keys.astype(F32) * HD ** (-0.5)).astype(BF16)
    lane = lax.broadcasted_iota(jnp.int32, (keys.shape[0], LANES), 1)
    zero = jnp.zeros((keys.shape[0], LANES), BF16)
    for pair in range(keys.shape[1] // LANES):
        tile = scaled[:, pair * LANES : (pair + 1) * LANES]
        turned = jnp.concatenate([tile[:, HD:], tile[:, :HD]], axis=1)
        keys_ref[2 * pair, 0] = jnp.where(lane < HD, tile, zero)
        keys_ref[2 * pair, 1] = jnp.where(lane < HD, zero, turned)
        keys_ref[2 * pair + 1, 0] = jnp.where(lane < HD, turned, zero)
        keys_ref[2 * pair + 1, 1] = jnp.where(lane < HD, zero, tile)


def stage_values(values, values_ref):
    count = values.shape[0]
    turned = jnp.transpose(values.astype(F32)).astype(BF16)
    for head in range(values.shape[1] // HD):
        values_ref[head, :HD, :] = turned[head * HD : (head + 1) * HD]
        values_ref[head, HD:, :] = jnp.ones((TAIL, count), BF16)


class Unit:
    def __init__(self, g, lane):
        self.g, self.lane = g, lane


def units_of(kv_heads, q_width):
    step = 2 * LANES
    group = q_width // kv_heads
    return [Unit(lane // group, lane) for lane in range(0, q_width, step)]


def unit_scores(queries, unit, keys_ref):
    stacked = jnp.concatenate([queries[:, :LANES], queries[:, LANES:]], axis=0)
    keys = jnp.concatenate([keys_ref[unit.g, 0], keys_ref[unit.g, 1]], axis=0)
    return dot(keys, stacked, ((1,), (1,)))


def unit_weighted(scores, unit, values_ref, bias):
    count = bias.shape[0]
    wide = jnp.concatenate([bias, bias], axis=1)
    patterns = []
    for side in range(2):
        masked = scores[side * count : (side + 1) * count] + wide
        highest = jnp.max(masked, axis=0, keepdims=True)
        patterns.append(jnp.exp((masked - highest).astype(BF16)))
    return dot(values_ref[unit.g], jnp.concatenate(patterns, axis=1), ((1,), (0,)))


def pipelined(units, queries_of, keys_ref, values_ref, bias, write):
    count = len(units)
    scores = [unit_scores(queries_of(unit), unit, keys_ref) for unit in units[:2]]

    def finish(unit, weighted):
        write(unit, weighted[:HD] * (1.0 / weighted[HD : HD + 1]))

    before = None
    for i, unit in enumerate(units):
        now = scores.pop(0)
        if i + 2 < count:
            scores.append(unit_scores(queries_of(units[i + 2]), units[i + 2], keys_ref))
        weighted = unit_weighted(now, unit, values_ref, bias)
        if before is not None:
            finish(*before)
        before = (unit, weighted)
    finish(*before)


def window_heads(queries_of, keys_ref, values_ref, bias_ref, out_ref, q_width):
    def write(unit, part):
        rows = part.shape[1] // 4
        rounded = part.astype(BF16)
        for side in range(2):
            for t in range(2):
                at = (side * 2 + t) * rows
                start = unit.lane + t * LANES + side * HD
                out_ref[start : start + HD, :] = rounded[:, at : at + rows]

    pipelined(units_of(keys_ref.shape[0], q_width), queries_of, keys_ref, values_ref, bias_ref[...], write)


def causal_heads(queries_of, keys_ref, values_ref, bias_ref, out_ref, q_width, ready):
    def write(unit, part):
        rows = part.shape[1] // 4
        for t in range(2):
            low = part[:, t * rows : (t + 1) * rows]
            high = part[:, (2 + t) * rows : (3 + t) * rows]
            lane = unit.lane + t * LANES
            out_ref[:, lane : lane + LANES] = jnp.transpose(
                jnp.concatenate([low, high], axis=0)
            ).astype(BF16)
        ready(unit)

    pipelined(units_of(keys_ref.shape[0], q_width), queries_of, keys_ref, values_ref, bias_ref[...], write)


def pack_kernel(k_ref, v_ref, out_ref, sems):
    half = out_ref.shape[0]
    kv_width = k_ref.shape[1]
    copies = [
        pltpu.make_async_copy(k_ref.at[pl.ds(half, half)], out_ref.at[:, pl.ds(0, kv_width)], sems.at[0]),
        pltpu.make_async_copy(
            v_ref.at[pl.ds(half, half)], out_ref.at[:, pl.ds(kv_width, kv_width)], sems.at[1]
        ),
    ]
    for copy in copies:
        copy.start()
    for copy in copies:
        copy.wait()


def window_upper_kernel(
    lengths_ref, q_ref, k_ref, v_ref, gain_ref,
    attn_ref, window_bias, upper_causal, lower_causal, gain_held,
    lengths_s, q_s, k_s, v_s, keys_s, values_s, bias_s, sems
):
    half = attn_ref.shape[1]
    upper = pl.ds(half, half)
    first = [
        pltpu.make_async_copy(lengths_ref, lengths_s, sems.at[0]),
        pltpu.make_async_copy(k_ref.at[upper], k_s, sems.at[1]),
        pltpu.make_async_copy(v_ref.at[upper], v_s, sems.at[2]),
        pltpu.make_async_copy(q_ref.at[upper], q_s, sems.at[3]),
    ]
    gain_in = pltpu.make_async_copy(gain_ref, gain_held, sems.at[4])
    for copy in first + [gain_in]:
        copy.start()
    first[0].wait()
    bias_s[...] = upper_bias(lengths_s, half, WIN)
    window_bias[...] = lower_bias(lengths_s, half, WIN)
    upper_causal[...] = upper_bias(lengths_s, half, None)
    lower_causal[...] = lower_bias(lengths_s, half, None)
    first[1].wait()
    stage_keys(k_s[...], keys_s)
    first[2].wait()
    stage_values(v_s[...], values_s)
    first[3].wait()

    def queries_of(unit):
        return q_s[:, unit.lane : unit.lane + 2 * LANES]

    window_heads(queries_of, keys_s, values_s, bias_s, attn_ref, q_s.shape[1])
    gain_in.wait()


def project(weight_ref, attn_ref, out_ref, chunk):
    for first in range(0, out_ref.shape[0], chunk):
        part = slice(first, first + chunk)
        out_ref[part, :] = dot(weight_ref[part, :], attn_ref[...], ((1,), (0,))).astype(BF16)


def project_upper_kernel(
    weight_ref, attn_ref, bias_ref, q_ref, k_ref, v_ref,
    out_ref, first_ref, q_held, k_held, v_held, keys_s, values_s, sems, *, chunk
):
    half = attn_ref.shape[1]
    lower = pl.ds(0, half)
    copies = [
        pltpu.make_async_copy(k_ref.at[lower], k_held, sems.at[0]),
        pltpu.make_async_copy(v_ref.at[lower], v_held, sems.at[1]),
        pltpu.make_async_copy(q_ref.at[lower], q_held, sems.at[2]),
    ]
    for copy in copies:
        copy.start()
    project(weight_ref, attn_ref, out_ref, chunk)
    for copy in copies:
        copy.wait()

    @pl.when(lax.axis_index("ctx") == 0)
    def _():
        stage_keys(k_held[...], keys_s)
        stage_values(v_held[...], values_s)

        def queries_of(unit):
            return q_held[:, unit.lane : unit.lane + 2 * LANES]

        window_heads(queries_of, keys_s, values_s, bias_ref.at[pl.ds(half, half)], first_ref, q_held.shape[1])


def window_lower_kernel(
    q_ref, k_ref, v_ref, halo_ref, weight_ref, bias_ref, first_ref,
    out_ref, attn_s, keys_s, values_s, *, chunk
):
    kv_width = k_ref.shape[1]
    ctx = lax.axis_index("ctx")

    @pl.when(ctx == 0)
    def _():
        attn_s[...] = first_ref[...]

    @pl.when(ctx != 0)
    def _():
        stage_keys(jnp.concatenate([halo_ref[:, :kv_width], k_ref[...]], axis=0), keys_s)
        stage_values(jnp.concatenate([halo_ref[:, kv_width:], v_ref[...]], axis=0), values_s)

        def queries_of(unit):
            return q_ref[:, unit.lane : unit.lane + 2 * LANES]

        window_heads(queries_of, keys_s, values_s, bias_ref, attn_s, q_ref.shape[1])

    project(weight_ref, attn_s, out_ref, chunk)


def add_and_norm(own_ref, other_ref, gain_ref, branch_ref, normed_ref, first_row, sum_s, keep_ref, chunk):
    width, rows = own_ref.shape
    head = lax.axis_index("head")

    def add(c, squares):
        part = pl.ds(pl.multiple_of(c * chunk, 16), chunk)
        total = own_ref[part, :].astype(F32) + other_ref[part, :].astype(F32)
        sum_s[part, :] = total
        rounded = total.astype(BF16)
        if keep_ref is not None:
            rounded = jnp.where(head == 0, rounded, keep_ref[part, :])
        branch_ref[part, :] = rounded
        return squares + jnp.sum(total * total, axis=0, keepdims=True)

    squares = lax.fori_loop(0, width // chunk, add, jnp.zeros((1, rows), F32))
    factor = lax.rsqrt(squares * (1.0 / width) + 1e-05)
    for first in range(0, width, LANES):
        last = min(first + LANES, width)
        piece = jnp.transpose(sum_s[first:last, :] * factor) * gain_ref[first:last][None, :]
        normed_ref[first_row : first_row + rows, first:last] = piece.astype(BF16)


def norm_upper_kernel(
    own_ref, other_ref, gain_ref, kw_ref, vw_ref, branch_ref, normed_ref, kv_ref, sum_s, *, chunk
):
    add_and_norm(own_ref, other_ref, gain_ref, branch_ref, normed_ref, 0, sum_s, None, chunk)
    kv_width = kw_ref.shape[1]
    kv_ref[:, :kv_width] = dot(normed_ref[...], kw_ref[...], ((1,), (0,))).astype(BF16)
    kv_ref[:, kv_width:] = dot(normed_ref[...], vw_ref[...], ((1,), (0,))).astype(BF16)


def causal_upper_kernel(
    own_ref, other_ref, gain_ref, kw_ref, vw_ref, qw_ref, kept_ref, normed_ref, kv_up_ref, bias_ref,
    lower_bias_ref, branch_ref, q_ref, kv_ref, out_ref,
    branch_s, out_s, normed_s, sum_s, keys_s, values_s, sems, unit_sems, *, chunk
):
    half = own_ref.shape[1]
    kv_width = kw_ref.shape[1]
    q_width = qw_ref.shape[1]
    normed_s[half:, :] = normed_ref[...]
    add_and_norm(own_ref, other_ref, gain_ref, branch_s, normed_s, 0, sum_s, kept_ref, chunk)
    branch_out = pltpu.make_async_copy(branch_s, branch_ref, sems.at[0])
    branch_out.start()
    stage_keys(kv_up_ref[:, :kv_width], keys_s)
    stage_values(kv_up_ref[:, kv_width:], values_s)

    piece = 4 * LANES
    pieces = {}

    def queries_of(unit):
        first = unit.lane // piece * piece
        if first not in pieces:
            columns = slice(first, first + piece)
            queries = dot(normed_s[...], qw_ref[:, columns], ((1,), (0,))).astype(BF16)
            q_ref[:, columns] = queries[:half]
            pieces[first] = queries[half:]
        return pieces[first][:, unit.lane - first : unit.lane - first + 2 * LANES]

    causal_heads(queries_of, keys_s, values_s, bias_ref, out_s, q_width, lambda unit: None)
    upper_out = pltpu.make_async_copy(out_s, out_ref.at[pl.ds(half, half)], sems.at[1])
    upper_out.start()
    kv_ref[:, :kv_width] = dot(normed_s[:half, :], kw_ref[...], ((1,), (0,))).astype(BF16)
    kv_ref[:, kv_width:] = dot(normed_s[:half, :], vw_ref[...], ((1,), (0,))).astype(BF16)
    branch_out.wait()
    upper_out.wait()

    @pl.when(lax.axis_index("ctx") == 0)
    def _():
        stage_keys(kv_ref[:, :kv_width], keys_s)
        stage_values(kv_ref[:, kv_width:], values_s)
        attend_lower(q_ref, keys_s, values_s, lower_bias_ref.at[pl.ds(half, half)], out_s, out_ref, unit_sems)


def attend_lower(q_ref, keys_s, values_s, bias_ref, out_s, out_ref, sems):
    half, q_width = q_ref.shape
    copies = []

    def queries_of(unit):
        return q_ref[:, unit.lane : unit.lane + 2 * LANES]

    def ready(unit):
        columns = pl.ds(unit.lane, 2 * LANES)
        copy = pltpu.make_async_copy(
            out_s.at[:, columns], out_ref.at[pl.ds(0, half), columns], sems.at[len(copies)]
        )
        copy.start()
        copies.append(copy)

    causal_heads(queries_of, keys_s, values_s, bias_ref, out_s, q_width, ready)
    for copy in copies:
        copy.wait()


def causal_lower_kernel(
    q_ref, kv_ref, halo_ref, bias_ref, given_ref, out_ref, out_s, keys_s, values_s, sems
):
    half, q_width = q_ref.shape
    kv_width = kv_ref.shape[1] // 2

    @pl.when(lax.axis_index("ctx") != 0)
    def _():
        stage_keys(jnp.concatenate([halo_ref[:, :kv_width], kv_ref[:, :kv_width]], axis=0), keys_s)
        stage_values(jnp.concatenate([halo_ref[:, kv_width:], kv_ref[:, kv_width:]], axis=0), values_s)
        attend_lower(q_ref, keys_s, values_s, bias_ref, out_s, out_ref, sems)


def attention_scratch(kv_heads, keys):
    return [
        pltpu.VMEM((kv_heads, 2, keys, LANES), BF16),
        pltpu.VMEM((kv_heads, HD + TAIL, keys), BF16),
    ]


def local(
    window_queries,
    window_keys,
    window_values,
    out_weight,
    norm_gain,
    query_weight,
    key_weight,
    value_weight,
    doc_lengths,
):
    rows, q_width = window_queries.shape
    kv_width = window_keys.shape[1]
    kv_heads = kv_width // HD
    width = out_weight.shape[1]
    half = rows // 2
    chunk = width // 2
    dma = pltpu.SemaphoreType.DMA
    lengths, queries, keys, values = [
        in_hbm(x) for x in (doc_lengths, window_queries, window_keys, window_values)
    ]

    packed = pl.pallas_call(
        pack_kernel,
        out_shape=jax.ShapeDtypeStruct((half, 2 * kv_width), BF16),
        in_specs=hbm_specs(2),
        out_specs=vmem_specs(1)[0],
        scratch_shapes=[dma((2,))],
        compiler_params=params(16),
        cost_estimate=pl.CostEstimate(flops=10**10, bytes_accessed=10**6, transcendentals=0),
        name="pack",
    )(keys, values)
    halo = shifted(packed, "ctx")
    attn_s = pltpu.VMEM((q_width, half), BF16)
    inputs_s = [
        pltpu.VMEM((half, q_width), BF16),
        pltpu.VMEM((half, kv_width), BF16),
        pltpu.VMEM((half, kv_width), BF16),
    ]
    attn_upper, window_bias, upper_causal, lower_causal, gain = pl.pallas_call(
        window_upper_kernel,
        out_shape=(
            attn_s,
            pltpu.VMEM((rows, half), F32),
            pltpu.VMEM((half, half), F32),
            pltpu.VMEM((rows, half), F32),
            pltpu.VMEM((width,), F32),
        ),
        in_specs=hbm_specs(5),
        out_specs=tuple(vmem_specs(5)),
        scratch_shapes=[pltpu.SMEM(doc_lengths.shape, jnp.int32)]
        + inputs_s
        + attention_scratch(kv_heads, half)
        + [pltpu.VMEM((half, half), F32), dma((5,))],
        compiler_params=params(8),
        name="window_upper",
    )(lengths, queries, keys, values, in_hbm(norm_gain))
    held = in_vmem(jnp.transpose(out_weight))
    own_upper, attn_first, q_held, k_held, v_held = pl.pallas_call(
        functools.partial(project_upper_kernel, chunk=chunk),
        out_shape=(pltpu.VMEM((width, half), BF16), attn_s, *inputs_s),
        in_specs=vmem_specs(3) + hbm_specs(3),
        out_specs=tuple(vmem_specs(5)),
        scratch_shapes=attention_scratch(kv_heads, half) + [dma((3,))],
        compiler_params=params(8),
        name="project_upper",
    )(held, attn_upper, window_bias, queries, keys, values)
    key_held, value_held, query_held = [in_vmem(x) for x in (key_weight, value_weight, query_weight)]
    other_upper = swapped(own_upper, "head")
    own_lower = pl.pallas_call(
        functools.partial(window_lower_kernel, chunk=chunk),
        out_shape=pltpu.VMEM((width, half), BF16),
        in_specs=vmem_specs(7),
        out_specs=vmem_specs(1)[0],
        scratch_shapes=[attn_s] + attention_scratch(kv_heads, rows),
        compiler_params=params(16),
        name="window_lower",
    )(q_held, k_held, v_held, in_vmem(halo), held, window_bias, attn_first)
    other_lower = swapped(own_lower, "head")
    branch_upper, normed_upper, pairs_upper = pl.pallas_call(
        functools.partial(norm_upper_kernel, chunk=192),
        out_shape=(
            pltpu.VMEM((width, half), BF16),
            pltpu.VMEM((half, width), BF16),
            pltpu.VMEM((half, 2 * kv_width), BF16),
        ),
        in_specs=vmem_specs(5),
        out_specs=tuple(vmem_specs(3)),
        scratch_shapes=[pltpu.VMEM((width, half), F32)],
        compiler_params=params(16),
        name="norm_upper",
    )(own_upper, other_upper, gain, key_held, value_held)
    earlier = shifted(pairs_upper, "ctx")
    branch, causal_queries, pairs_lower, causal_out = pl.pallas_call(
        functools.partial(causal_upper_kernel, chunk=192),
        out_shape=(
            pltpu.HBM((width, half), BF16),
            pltpu.VMEM((half, q_width), BF16),
            pltpu.VMEM((half, 2 * kv_width), BF16),
            pltpu.HBM((rows, q_width), BF16),
        ),
        in_specs=vmem_specs(11),
        out_specs=(hbm_specs(1)[0], *vmem_specs(2), hbm_specs(1)[0]),
        scratch_shapes=[
            pltpu.VMEM((width, half), BF16),
            pltpu.VMEM((half, q_width), BF16),
            pltpu.VMEM((rows, width), BF16),
            pltpu.VMEM((width, half), F32),
        ]
        + attention_scratch(kv_heads, half)
        + [dma((2,)), dma((q_width // (2 * LANES),))],
        compiler_params=params(16),
        name="causal_upper",
    )(
        own_lower, other_lower, gain, key_held, value_held, query_held,
        branch_upper, normed_upper, pairs_upper, upper_causal, lower_causal,
    )
    causal_out = pl.pallas_call(
        causal_lower_kernel,
        out_shape=pltpu.HBM((rows, q_width), BF16),
        in_specs=vmem_specs(4) + hbm_specs(1),
        out_specs=hbm_specs(1)[0],
        scratch_shapes=[pltpu.VMEM((half, q_width), BF16)]
        + attention_scratch(kv_heads, rows)
        + [dma((q_width // (2 * LANES),))],
        input_output_aliases={4: 0},
        compiler_params=params(16),
        name="causal_lower",
    )(causal_queries, pairs_lower, in_vmem(earlier), lower_causal, causal_out)
    return (jnp.transpose(branch), causal_out)


def solution(mesh):
    placed = (
        P("ctx", "head"),
        P("ctx", "head"),
        P("ctx", "head"),
        P("head", None),
        P(),
        P(None, "head"),
        P(None, "head"),
        P(None, "head"),
        P(),
    )
    return jax.shard_map(
        local,
        mesh=mesh,
        in_specs=placed,
        out_specs=(P(("ctx", "head"), None), P("ctx", "head")),
        check_vma=False,
    )
```

```python
import functools

import jax
import jax.numpy as jnp
from jax import lax
from jax.experimental import pallas as pl
from jax.experimental.pallas import tpu as pltpu
from jax.sharding import PartitionSpec as P

HD = 64
WIN = 128
LANES = 128
NEG = -1e30
TAIL = 16

F32 = jnp.float32
BF16 = jnp.bfloat16
MIB = 1024 * 1024


def params(mib):
    return pltpu.CompilerParams(vmem_limit_bytes=mib * MIB)


def in_vmem(array):
    return pltpu.with_memory_space_constraint(array, pltpu.VMEM)


def in_hbm(array):
    return pltpu.with_memory_space_constraint(array, pltpu.HBM)


def hbm_specs(count):
    return [pl.BlockSpec(memory_space=pltpu.HBM)] * count


def vmem_specs(count):
    return [pl.BlockSpec(memory_space=pltpu.VMEM)] * count


def dot(a, b, dims):
    return lax.dot_general(a, b, (dims, ((), ())), preferred_element_type=F32)


def shifted(block, axis):
    size = lax.axis_size(axis)
    return lax.ppermute(block, axis, [(i, (i + 1) % size) for i in range(size)])


def swapped(block, axis):
    size = lax.axis_size(axis)
    return lax.ppermute(block, axis, [(i, size - 1 - i) for i in range(size)])


def lower_bias(lengths_ref, half, width):
    ctx = lax.axis_index("ctx")
    first = jnp.where(ctx == 0, half, 0)
    split = first + lengths_ref[2 * ctx]
    return bias_of(2 * half, half, half, first, split, width)


def upper_bias(lengths_ref, half, width):
    ctx = lax.axis_index("ctx")
    last = lengths_ref.shape[0] - 1
    split = lengths_ref[jnp.minimum(2 * ctx + 2, last)]
    split = jnp.where(ctx == lax.axis_size("ctx") - 1, 2 * half, split)
    return bias_of(half, half, 0, 0, split, width)


def bias_of(keys, rows, row_offset, first, split, width):
    key = lax.broadcasted_iota(jnp.int32, (keys, rows), 0)
    row = lax.broadcasted_iota(jnp.int32, (keys, rows), 1) + row_offset
    lowest = jnp.where(row >= split, split, first)
    if width is not None:
        lowest = jnp.maximum(lowest, row - (width - 1))
    return jnp.where((key >= lowest) & (key <= row), 0.0, NEG).astype(F32)


def stage_keys(keys, keys_ref):
    scaled = (keys.astype(F32) * HD ** (-0.5)).astype(BF16)
    lane = lax.broadcasted_iota(jnp.int32, (keys.shape[0], LANES), 1)
    zero = jnp.zeros((keys.shape[0], LANES), BF16)
    for pair in range(keys.shape[1] // LANES):
        tile = scaled[:, pair * LANES : (pair + 1) * LANES]
        turned = jnp.concatenate([tile[:, HD:], tile[:, :HD]], axis=1)
        keys_ref[2 * pair, 0] = jnp.where(lane < HD, tile, zero)
        keys_ref[2 * pair, 1] = jnp.where(lane < HD, zero, turned)
        keys_ref[2 * pair + 1, 0] = jnp.where(lane < HD, turned, zero)
        keys_ref[2 * pair + 1, 1] = jnp.where(lane < HD, zero, tile)


def stage_values(values, values_ref):
    count = values.shape[0]
    turned = jnp.transpose(values.astype(F32)).astype(BF16)
    for head in range(values.shape[1] // HD):
        values_ref[head, :HD, :] = turned[head * HD : (head + 1) * HD]
        values_ref[head, HD:, :] = jnp.ones((TAIL, count), BF16)


class Unit:
    def __init__(self, g, lane):
        self.g, self.lane = g, lane


def units_of(kv_heads, q_width):
    step = 2 * LANES
    group = q_width // kv_heads
    return [Unit(lane // group, lane) for lane in range(0, q_width, step)]


def unit_scores(queries, unit, keys_ref):
    stacked = jnp.concatenate([queries[:, :LANES], queries[:, LANES:]], axis=0)
    keys = jnp.concatenate([keys_ref[unit.g, 0], keys_ref[unit.g, 1]], axis=0)
    return dot(keys, stacked, ((1,), (1,)))


def unit_weighted(scores, unit, values_ref, bias):
    count = bias.shape[0]
    wide = jnp.concatenate([bias, bias], axis=1)
    patterns = []
    for side in range(2):
        masked = scores[side * count : (side + 1) * count] + wide
        highest = jnp.max(masked, axis=0, keepdims=True)
        patterns.append(jnp.exp((masked - highest).astype(BF16)))
    return dot(values_ref[unit.g], jnp.concatenate(patterns, axis=1), ((1,), (0,)))


def pipelined(units, queries_of, keys_ref, values_ref, bias, write):
    count = len(units)
    scores = [unit_scores(queries_of(unit), unit, keys_ref) for unit in units[:2]]

    def finish(unit, weighted):
        write(unit, weighted[:HD] * (1.0 / weighted[HD : HD + 1]))

    before = None
    for i, unit in enumerate(units):
        now = scores.pop(0)
        if i + 2 < count:
            scores.append(unit_scores(queries_of(units[i + 2]), units[i + 2], keys_ref))
        weighted = unit_weighted(now, unit, values_ref, bias)
        if before is not None:
            finish(*before)
        before = (unit, weighted)
    finish(*before)


def window_heads(queries_of, keys_ref, values_ref, bias_ref, out_ref, q_width):
    def write(unit, part):
        rows = part.shape[1] // 4
        rounded = part.astype(BF16)
        for side in range(2):
            for t in range(2):
                at = (side * 2 + t) * rows
                start = unit.lane + t * LANES + side * HD
                out_ref[start : start + HD, :] = rounded[:, at : at + rows]

    pipelined(units_of(keys_ref.shape[0], q_width), queries_of, keys_ref, values_ref, bias_ref[...], write)


def causal_heads(queries_of, keys_ref, values_ref, bias_ref, out_ref, q_width, ready):
    def write(unit, part):
        rows = part.shape[1] // 4
        for t in range(2):
            low = part[:, t * rows : (t + 1) * rows]
            high = part[:, (2 + t) * rows : (3 + t) * rows]
            lane = unit.lane + t * LANES
            out_ref[:, lane : lane + LANES] = jnp.transpose(
                jnp.concatenate([low, high], axis=0)
            ).astype(BF16)
        ready(unit)

    pipelined(units_of(keys_ref.shape[0], q_width), queries_of, keys_ref, values_ref, bias_ref[...], write)


def pack_kernel(k_ref, v_ref, out_ref, sems):
    half = out_ref.shape[0]
    kv_width = k_ref.shape[1]
    copies = [
        pltpu.make_async_copy(k_ref.at[pl.ds(half, half)], out_ref.at[:, pl.ds(0, kv_width)], sems.at[0]),
        pltpu.make_async_copy(
            v_ref.at[pl.ds(half, half)], out_ref.at[:, pl.ds(kv_width, kv_width)], sems.at[1]
        ),
    ]
    for copy in copies:
        copy.start()
    for copy in copies:
        copy.wait()


def window_upper_kernel(
    lengths_ref, q_ref, k_ref, v_ref, weight_ref, gain_ref,
    out_ref, held_ref, first_ref, q_held, k_held, v_held, window_bias, upper_causal, lower_causal, gain_held,
    lengths_s, attn_s, keys_s, values_s, bias_s, sems, weight_sems
):
    half = out_ref.shape[1]
    count = weight_sems.shape[0]
    chunk = held_ref.shape[0] // count
    upper, lower = pl.ds(half, half), pl.ds(0, half)
    first = [
        pltpu.make_async_copy(lengths_ref, lengths_s, sems.at[0]),
        pltpu.make_async_copy(k_ref.at[upper], k_held.at[upper], sems.at[1]),
        pltpu.make_async_copy(v_ref.at[upper], v_held.at[upper], sems.at[2]),
        pltpu.make_async_copy(q_ref.at[upper], q_held.at[upper], sems.at[3]),
    ]
    last = [
        pltpu.make_async_copy(k_ref.at[lower], k_held.at[lower], sems.at[4]),
        pltpu.make_async_copy(v_ref.at[lower], v_held.at[lower], sems.at[5]),
        pltpu.make_async_copy(q_ref.at[lower], q_held.at[lower], sems.at[6]),
        pltpu.make_async_copy(gain_ref, gain_held, sems.at[7]),
    ]
    weights = [
        pltpu.make_async_copy(
            weight_ref.at[pl.ds(c * chunk, chunk)], held_ref.at[pl.ds(c * chunk, chunk)], weight_sems.at[c]
        )
        for c in range(count)
    ]
    early = count // 2
    for copy in first + weights[:2]:
        copy.start()
    first[0].wait()
    bias_s[...] = upper_bias(lengths_s, half, WIN)
    window_bias[...] = lower_bias(lengths_s, half, WIN)
    upper_causal[...] = upper_bias(lengths_s, half, None)
    lower_causal[...] = lower_bias(lengths_s, half, None)
    first[1].wait()
    stage_keys(k_held[half:], keys_s)
    first[2].wait()
    stage_values(v_held[half:], values_s)
    first[3].wait()
    for copy in weights[2:early] + last:
        copy.start()

    def queries_of(unit):
        return q_held[half:, unit.lane : unit.lane + 2 * LANES]

    window_heads(queries_of, keys_s, values_s, bias_s, attn_s, q_held.shape[1])
    for copy in weights[early : early + 3]:
        copy.start()
    for copy in weights[:early] + last:
        copy.wait()
    for c in range(count):
        if early <= c + 2 < count:
            weights[c + 2].wait()
            if c + 5 < count:
                weights[c + 5].start()
        part = slice(c * chunk, (c + 1) * chunk)
        out_ref[part, :] = dot(held_ref[part, :], attn_s[...], ((1,), (0,))).astype(BF16)

    @pl.when(lax.axis_index("ctx") == 0)
    def _():
        stage_keys(k_held[:half], keys_s)
        stage_values(v_held[:half], values_s)

        def lower_queries_of(unit):
            return q_held[:half, unit.lane : unit.lane + 2 * LANES]

        window_heads(
            lower_queries_of, keys_s, values_s, window_bias.at[pl.ds(half, half)], first_ref, q_held.shape[1]
        )


def project(weight_ref, attn_ref, out_ref, chunk):
    for first in range(0, out_ref.shape[0], chunk):
        part = slice(first, first + chunk)
        out_ref[part, :] = dot(weight_ref[part, :], attn_ref[...], ((1,), (0,))).astype(BF16)


def window_lower_kernel(
    q_ref, k_ref, v_ref, halo_ref, weight_ref, bias_ref, first_ref, kw_ref, vw_ref, qw_ref,
    out_ref, key_held, value_held, query_held, attn_s, keys_s, values_s, sems, *, chunk
):
    copies = [
        pltpu.make_async_copy(kw_ref, key_held, sems.at[0]),
        pltpu.make_async_copy(vw_ref, value_held, sems.at[1]),
        pltpu.make_async_copy(qw_ref.at[:, pl.ds(0, query_held.shape[1])], query_held, sems.at[2]),
    ]
    for copy in copies:
        copy.start()
    half = halo_ref.shape[0]
    kv_width = k_ref.shape[1]
    ctx = lax.axis_index("ctx")

    @pl.when(ctx == 0)
    def _():
        attn_s[...] = first_ref[...]

    @pl.when(ctx != 0)
    def _():
        stage_keys(jnp.concatenate([halo_ref[:, :kv_width], k_ref[:half]], axis=0), keys_s)
        stage_values(jnp.concatenate([halo_ref[:, kv_width:], v_ref[:half]], axis=0), values_s)

        def queries_of(unit):
            return q_ref[:half, unit.lane : unit.lane + 2 * LANES]

        window_heads(queries_of, keys_s, values_s, bias_ref, attn_s, q_ref.shape[1])

    project(weight_ref, attn_s, out_ref, chunk)
    for copy in copies:
        copy.wait()


def add_and_norm(own_ref, other_ref, gain_ref, branch_ref, normed_ref, first_row, sum_s, keep_ref, chunk):
    width, rows = own_ref.shape
    head = lax.axis_index("head")

    def add(c, squares):
        part = pl.ds(pl.multiple_of(c * chunk, 16), chunk)
        total = own_ref[part, :].astype(F32) + other_ref[part, :].astype(F32)
        sum_s[part, :] = total
        rounded = total.astype(BF16)
        if keep_ref is not None:
            rounded = jnp.where(head == 0, rounded, keep_ref[part, :])
        branch_ref[part, :] = rounded
        return squares + jnp.sum(total * total, axis=0, keepdims=True)

    squares = lax.fori_loop(0, width // chunk, add, jnp.zeros((1, rows), F32))
    factor = lax.rsqrt(squares * (1.0 / width) + 1e-05)
    for first in range(0, width, LANES):
        last = min(first + LANES, width)
        piece = jnp.transpose(sum_s[first:last, :] * factor) * gain_ref[first:last][None, :]
        normed_ref[first_row : first_row + rows, first:last] = piece.astype(BF16)


def norm_upper_kernel(
    own_ref, other_ref, gain_ref, kw_ref, vw_ref, branch_ref, normed_ref, kv_ref, sum_s, *, chunk
):
    add_and_norm(own_ref, other_ref, gain_ref, branch_ref, normed_ref, 0, sum_s, None, chunk)
    kv_width = kw_ref.shape[1]
    kv_ref[:, :kv_width] = dot(normed_ref[...], kw_ref[...], ((1,), (0,))).astype(BF16)
    kv_ref[:, kv_width:] = dot(normed_ref[...], vw_ref[...], ((1,), (0,))).astype(BF16)


def causal_upper_kernel(
    own_ref, other_ref, gain_ref, kw_ref, vw_ref, query_held, kept_ref, normed_ref, kv_up_ref, bias_ref,
    lower_bias_ref, qw_ref, branch_ref, q_ref, kv_ref, out_ref,
    rest_s, branch_s, out_s, upper_q_s, normed_s, sum_s, keys_s, values_s, sems, unit_sems, *, chunk
):
    half = own_ref.shape[1]
    kv_width = kw_ref.shape[1]
    q_width = qw_ref.shape[1]
    piece = query_held.shape[1]
    rest_in = pltpu.make_async_copy(qw_ref.at[:, pl.ds(piece, q_width - piece)], rest_s, sems.at[2])
    rest_in.start()
    normed_s[half:, :] = normed_ref[...]
    add_and_norm(own_ref, other_ref, gain_ref, branch_s, normed_s, 0, sum_s, kept_ref, chunk)
    branch_out = pltpu.make_async_copy(branch_s, branch_ref, sems.at[0])
    branch_out.start()
    stage_keys(kv_up_ref[:, :kv_width], keys_s)
    stage_values(kv_up_ref[:, kv_width:], values_s)

    for first, weight_ref in ((0, query_held), (piece, rest_s)):
        if first > 0:
            rest_in.wait()
        columns = slice(first, first + piece)
        queries = dot(normed_s[...], weight_ref[...], ((1,), (0,))).astype(BF16)
        q_ref[:, columns] = queries[:half]
        upper_q_s[:, columns] = queries[half:]

    def queries_of(unit):
        return upper_q_s[:, unit.lane : unit.lane + 2 * LANES]

    causal_heads(queries_of, keys_s, values_s, bias_ref, out_s, q_width, lambda unit: None)
    upper_out = pltpu.make_async_copy(out_s, out_ref.at[pl.ds(half, half)], sems.at[1])
    upper_out.start()
    kv_ref[:, :kv_width] = dot(normed_s[:half, :], kw_ref[...], ((1,), (0,))).astype(BF16)
    kv_ref[:, kv_width:] = dot(normed_s[:half, :], vw_ref[...], ((1,), (0,))).astype(BF16)
    branch_out.wait()
    upper_out.wait()

    @pl.when(lax.axis_index("ctx") == 0)
    def _():
        stage_keys(kv_ref[:, :kv_width], keys_s)
        stage_values(kv_ref[:, kv_width:], values_s)
        attend_lower(q_ref, keys_s, values_s, lower_bias_ref.at[pl.ds(half, half)], out_s, out_ref, unit_sems)


def attend_lower(q_ref, keys_s, values_s, bias_ref, out_s, out_ref, sems):
    half, q_width = q_ref.shape
    copies = []

    def queries_of(unit):
        return q_ref[:, unit.lane : unit.lane + 2 * LANES]

    def ready(unit):
        columns = pl.ds(unit.lane, 2 * LANES)
        copy = pltpu.make_async_copy(
            out_s.at[:, columns], out_ref.at[pl.ds(0, half), columns], sems.at[len(copies)]
        )
        copy.start()
        copies.append(copy)

    causal_heads(queries_of, keys_s, values_s, bias_ref, out_s, q_width, ready)
    for copy in copies:
        copy.wait()


def causal_lower_kernel(
    q_ref, kv_ref, halo_ref, bias_ref, given_ref, out_ref, out_s, keys_s, values_s, sems
):
    half, q_width = q_ref.shape
    kv_width = kv_ref.shape[1] // 2

    @pl.when(lax.axis_index("ctx") != 0)
    def _():
        stage_keys(jnp.concatenate([halo_ref[:, :kv_width], kv_ref[:, :kv_width]], axis=0), keys_s)
        stage_values(jnp.concatenate([halo_ref[:, kv_width:], kv_ref[:, kv_width:]], axis=0), values_s)
        attend_lower(q_ref, keys_s, values_s, bias_ref, out_s, out_ref, sems)


def attention_scratch(kv_heads, keys):
    return [
        pltpu.VMEM((kv_heads, 2, keys, LANES), BF16),
        pltpu.VMEM((kv_heads, HD + TAIL, keys), BF16),
    ]


def local(
    window_queries,
    window_keys,
    window_values,
    out_weight,
    norm_gain,
    query_weight,
    key_weight,
    value_weight,
    doc_lengths,
):
    rows, q_width = window_queries.shape
    kv_width = window_keys.shape[1]
    kv_heads = kv_width // HD
    width = out_weight.shape[1]
    half = rows // 2
    chunk = width // 2
    dma = pltpu.SemaphoreType.DMA
    lengths, queries, keys, values = [
        in_hbm(x) for x in (doc_lengths, window_queries, window_keys, window_values)
    ]

    packed = pl.pallas_call(
        pack_kernel,
        out_shape=jax.ShapeDtypeStruct((half, 2 * kv_width), BF16),
        in_specs=hbm_specs(2),
        out_specs=vmem_specs(1)[0],
        scratch_shapes=[dma((2,))],
        compiler_params=params(16),
        name="pack",
    )(keys, values)
    halo = shifted(packed, "ctx")
    attn_s = pltpu.VMEM((q_width, half), BF16)
    (
        own_upper, held, attn_first, q_held, k_held, v_held, window_bias, upper_causal, lower_causal, gain
    ) = pl.pallas_call(
        window_upper_kernel,
        out_shape=(
            pltpu.VMEM((width, half), BF16),
            pltpu.VMEM((width, q_width), BF16),
            attn_s,
            pltpu.VMEM((rows, q_width), BF16),
            pltpu.VMEM((rows, kv_width), BF16),
            pltpu.VMEM((rows, kv_width), BF16),
            pltpu.VMEM((rows, half), F32),
            pltpu.VMEM((half, half), F32),
            pltpu.VMEM((rows, half), F32),
            pltpu.VMEM((width,), F32),
        ),
        in_specs=hbm_specs(6),
        out_specs=tuple(vmem_specs(10)),
        scratch_shapes=[pltpu.SMEM(doc_lengths.shape, jnp.int32), attn_s]
        + attention_scratch(kv_heads, half)
        + [pltpu.VMEM((half, half), F32), dma((8,)), dma((10,))],
        compiler_params=params(12),
        name="window_upper",
    )(lengths, queries, keys, values, in_hbm(jnp.transpose(out_weight)), in_hbm(norm_gain))
    key_weight, value_weight, query_weight = [
        in_hbm(x) for x in (key_weight, value_weight, query_weight)
    ]
    other_upper = swapped(own_upper, "head")
    own_lower, key_held, value_held, query_held = pl.pallas_call(
        functools.partial(window_lower_kernel, chunk=chunk),
        out_shape=(
            pltpu.VMEM((width, half), BF16),
            pltpu.VMEM((width, kv_width), BF16),
            pltpu.VMEM((width, kv_width), BF16),
            pltpu.VMEM((width, q_width // 2), BF16),
        ),
        in_specs=vmem_specs(7) + hbm_specs(3),
        out_specs=tuple(vmem_specs(4)),
        scratch_shapes=[attn_s] + attention_scratch(kv_heads, rows) + [dma((3,))],
        compiler_params=params(16),
        name="window_lower",
    )(
        q_held, k_held, v_held, in_vmem(halo), held, window_bias, attn_first,
        key_weight, value_weight, query_weight,
    )
    other_lower = swapped(own_lower, "head")
    branch_upper, normed_upper, pairs_upper = pl.pallas_call(
        functools.partial(norm_upper_kernel, chunk=192),
        out_shape=(
            pltpu.VMEM((width, half), BF16),
            pltpu.VMEM((half, width), BF16),
            pltpu.VMEM((half, 2 * kv_width), BF16),
        ),
        in_specs=vmem_specs(5),
        out_specs=tuple(vmem_specs(3)),
        scratch_shapes=[pltpu.VMEM((width, half), F32)],
        compiler_params=params(16),
        name="norm_upper",
    )(own_upper, other_upper, gain, key_held, value_held)
    earlier = shifted(pairs_upper, "ctx")
    branch, causal_queries, pairs_lower, causal_out = pl.pallas_call(
        functools.partial(causal_upper_kernel, chunk=192),
        out_shape=(
            pltpu.HBM((width, half), BF16),
            pltpu.VMEM((half, q_width), BF16),
            pltpu.VMEM((half, 2 * kv_width), BF16),
            pltpu.HBM((rows, q_width), BF16),
        ),
        in_specs=vmem_specs(11) + hbm_specs(1),
        out_specs=(hbm_specs(1)[0], *vmem_specs(2), hbm_specs(1)[0]),
        scratch_shapes=[
            pltpu.VMEM((width, q_width // 2), BF16),
            pltpu.VMEM((width, half), BF16),
            pltpu.VMEM((half, q_width), BF16),
            pltpu.VMEM((half, q_width), BF16),
            pltpu.VMEM((rows, width), BF16),
            pltpu.VMEM((width, half), F32),
        ]
        + attention_scratch(kv_heads, half)
        + [dma((3,)), dma((q_width // (2 * LANES),))],
        compiler_params=params(22),
        name="causal_upper",
    )(
        own_lower, other_lower, gain, key_held, value_held, query_held,
        branch_upper, normed_upper, pairs_upper, upper_causal, lower_causal,
        query_weight,
    )
    causal_out = pl.pallas_call(
        causal_lower_kernel,
        out_shape=pltpu.HBM((rows, q_width), BF16),
        in_specs=vmem_specs(4) + hbm_specs(1),
        out_specs=hbm_specs(1)[0],
        scratch_shapes=[pltpu.VMEM((half, q_width), BF16)]
        + attention_scratch(kv_heads, rows)
        + [dma((q_width // (2 * LANES),))],
        input_output_aliases={4: 0},
        compiler_params=params(16),
        name="causal_lower",
    )(causal_queries, pairs_lower, in_vmem(earlier), lower_causal, causal_out)
    return (jnp.transpose(branch), causal_out)


def solution(mesh):
    placed = (
        P("ctx", "head"),
        P("ctx", "head"),
        P("ctx", "head"),
        P("head", None),
        P(),
        P(None, "head"),
        P(None, "head"),
        P(None, "head"),
        P(),
    )
    return jax.shard_map(
        local,
        mesh=mesh,
        in_specs=placed,
        out_specs=(P(("ctx", "head"), None), P("ctx", "head")),
        check_vma=False,
    )
```

```python
import functools

import jax
import jax.numpy as jnp
from jax import lax
from jax.experimental import pallas as pl
from jax.experimental.pallas import tpu as pltpu
from jax.sharding import PartitionSpec as P

HD = 64
WIN = 128
LANES = 128
NEG = -1e30
TAIL = 16

F32 = jnp.float32
BF16 = jnp.bfloat16
MIB = 1024 * 1024


def params(mib):
    return pltpu.CompilerParams(vmem_limit_bytes=mib * MIB)


def in_vmem(array):
    return pltpu.with_memory_space_constraint(array, pltpu.VMEM)


def in_hbm(array):
    return pltpu.with_memory_space_constraint(array, pltpu.HBM)


def hbm_specs(count):
    return [pl.BlockSpec(memory_space=pltpu.HBM)] * count


def vmem_specs(count):
    return [pl.BlockSpec(memory_space=pltpu.VMEM)] * count


def dot(a, b, dims):
    return lax.dot_general(a, b, (dims, ((), ())), preferred_element_type=F32)


def shifted(block, axis):
    size = lax.axis_size(axis)
    return lax.ppermute(block, axis, [(i, (i + 1) % size) for i in range(size)])


def swapped(block, axis):
    size = lax.axis_size(axis)
    return lax.ppermute(block, axis, [(i, size - 1 - i) for i in range(size)])


def lower_bias(lengths_ref, half, width):
    ctx = lax.axis_index("ctx")
    first = jnp.where(ctx == 0, half, 0)
    split = first + lengths_ref[2 * ctx]
    return bias_of(2 * half, half, half, first, split, width)


def upper_bias(lengths_ref, half, width):
    ctx = lax.axis_index("ctx")
    last = lengths_ref.shape[0] - 1
    split = lengths_ref[jnp.minimum(2 * ctx + 2, last)]
    split = jnp.where(ctx == lax.axis_size("ctx") - 1, 2 * half, split)
    return bias_of(half, half, 0, 0, split, width)


def bias_of(keys, rows, row_offset, first, split, width):
    key = lax.broadcasted_iota(jnp.int32, (keys, rows), 0)
    row = lax.broadcasted_iota(jnp.int32, (keys, rows), 1) + row_offset
    lowest = jnp.where(row >= split, split, first)
    if width is not None:
        lowest = jnp.maximum(lowest, row - (width - 1))
    return jnp.where((key >= lowest) & (key <= row), 0.0, NEG).astype(F32)


def stage_keys(keys, keys_ref):
    scaled = (keys.astype(F32) * HD ** (-0.5)).astype(BF16)
    lane = lax.broadcasted_iota(jnp.int32, (keys.shape[0], LANES), 1)
    zero = jnp.zeros((keys.shape[0], LANES), BF16)
    for pair in range(keys.shape[1] // LANES):
        tile = scaled[:, pair * LANES : (pair + 1) * LANES]
        turned = jnp.concatenate([tile[:, HD:], tile[:, :HD]], axis=1)
        keys_ref[2 * pair, 0] = jnp.where(lane < HD, tile, zero)
        keys_ref[2 * pair, 1] = jnp.where(lane < HD, zero, turned)
        keys_ref[2 * pair + 1, 0] = jnp.where(lane < HD, turned, zero)
        keys_ref[2 * pair + 1, 1] = jnp.where(lane < HD, zero, tile)


def stage_values(values, values_ref):
    count = values.shape[0]
    turned = jnp.transpose(values.astype(F32)).astype(BF16)
    for head in range(values.shape[1] // HD):
        values_ref[head, :HD, :] = turned[head * HD : (head + 1) * HD]
        values_ref[head, HD:, :] = jnp.ones((TAIL, count), BF16)


class Unit:
    def __init__(self, g, lane):
        self.g, self.lane = g, lane


def units_of(kv_heads, q_width):
    step = 2 * LANES
    group = q_width // kv_heads
    return [Unit(lane // group, lane) for lane in range(0, q_width, step)]


def unit_scores(queries, unit, keys_ref):
    stacked = jnp.concatenate([queries[:, :LANES], queries[:, LANES:]], axis=0)
    keys = jnp.concatenate([keys_ref[unit.g, 0], keys_ref[unit.g, 1]], axis=0)
    return dot(keys, stacked, ((1,), (1,)))


def unit_weighted(scores, unit, values_ref, bias):
    count = bias.shape[0]
    wide = jnp.concatenate([bias, bias], axis=1)
    patterns = []
    for side in range(2):
        masked = scores[side * count : (side + 1) * count] + wide
        highest = jnp.max(masked, axis=0, keepdims=True)
        patterns.append(jnp.exp((masked - highest).astype(BF16)))
    return dot(values_ref[unit.g], jnp.concatenate(patterns, axis=1), ((1,), (0,)))


def pipelined(units, queries_of, keys_ref, values_ref, bias, write):
    count = len(units)
    scores = [unit_scores(queries_of(unit), unit, keys_ref) for unit in units[:2]]

    def finish(unit, weighted):
        write(unit, weighted[:HD] * (1.0 / weighted[HD : HD + 1]))

    before = None
    for i, unit in enumerate(units):
        now = scores.pop(0)
        if i + 2 < count:
            scores.append(unit_scores(queries_of(units[i + 2]), units[i + 2], keys_ref))
        weighted = unit_weighted(now, unit, values_ref, bias)
        if before is not None:
            finish(*before)
        before = (unit, weighted)
    finish(*before)


def window_heads(queries_of, keys_ref, values_ref, bias_ref, out_ref, q_width):
    def write(unit, part):
        rows = part.shape[1] // 4
        rounded = part.astype(BF16)
        for side in range(2):
            for t in range(2):
                at = (side * 2 + t) * rows
                start = unit.lane + t * LANES + side * HD
                out_ref[start : start + HD, :] = rounded[:, at : at + rows]

    pipelined(units_of(keys_ref.shape[0], q_width), queries_of, keys_ref, values_ref, bias_ref[...], write)


def causal_heads(queries_of, keys_ref, values_ref, bias_ref, out_ref, q_width, ready):
    def write(unit, part):
        rows = part.shape[1] // 4
        for t in range(2):
            low = part[:, t * rows : (t + 1) * rows]
            high = part[:, (2 + t) * rows : (3 + t) * rows]
            lane = unit.lane + t * LANES
            out_ref[:, lane : lane + LANES] = jnp.transpose(
                jnp.concatenate([low, high], axis=0)
            ).astype(BF16)
        ready(unit)

    pipelined(units_of(keys_ref.shape[0], q_width), queries_of, keys_ref, values_ref, bias_ref[...], write)


def pack_kernel(k_ref, v_ref, out_ref, sems):
    half = out_ref.shape[0]
    kv_width = k_ref.shape[1]
    copies = [
        pltpu.make_async_copy(k_ref.at[pl.ds(half, half)], out_ref.at[:, pl.ds(0, kv_width)], sems.at[0]),
        pltpu.make_async_copy(
            v_ref.at[pl.ds(half, half)], out_ref.at[:, pl.ds(kv_width, kv_width)], sems.at[1]
        ),
    ]
    for copy in copies:
        copy.start()
    for copy in copies:
        copy.wait()


def window_upper_kernel(
    lengths_ref, q_ref, k_ref, v_ref, gain_ref,
    attn_ref, q_held, k_held, v_held, window_bias, upper_causal, lower_causal, gain_held,
    lengths_s, keys_s, values_s, bias_s, sems
):
    half = attn_ref.shape[1]
    upper, lower = pl.ds(half, half), pl.ds(0, half)
    first = [
        pltpu.make_async_copy(lengths_ref, lengths_s, sems.at[0]),
        pltpu.make_async_copy(k_ref.at[upper], k_held.at[upper], sems.at[1]),
        pltpu.make_async_copy(v_ref.at[upper], v_held.at[upper], sems.at[2]),
        pltpu.make_async_copy(q_ref.at[upper], q_held.at[upper], sems.at[3]),
    ]
    last = [
        pltpu.make_async_copy(k_ref.at[lower], k_held.at[lower], sems.at[4]),
        pltpu.make_async_copy(v_ref.at[lower], v_held.at[lower], sems.at[5]),
        pltpu.make_async_copy(q_ref.at[lower], q_held.at[lower], sems.at[6]),
        pltpu.make_async_copy(gain_ref, gain_held, sems.at[7]),
    ]
    for copy in first + last:
        copy.start()
    first[0].wait()
    bias_s[...] = upper_bias(lengths_s, half, WIN)
    window_bias[...] = lower_bias(lengths_s, half, WIN)
    upper_causal[...] = upper_bias(lengths_s, half, None)
    lower_causal[...] = lower_bias(lengths_s, half, None)
    first[1].wait()
    stage_keys(k_held[half:], keys_s)
    first[2].wait()
    stage_values(v_held[half:], values_s)
    first[3].wait()

    def queries_of(unit):
        return q_held[half:, unit.lane : unit.lane + 2 * LANES]

    window_heads(queries_of, keys_s, values_s, bias_s, attn_ref, q_held.shape[1])
    for copy in last:
        copy.wait()


def project(weight_ref, attn_ref, out_ref, chunk):
    for first in range(0, out_ref.shape[0], chunk):
        part = slice(first, first + chunk)
        out_ref[part, :] = dot(weight_ref[part, :], attn_ref[...], ((1,), (0,))).astype(BF16)


def project_upper_kernel(
    weight_ref, attn_ref, q_ref, k_ref, v_ref, bias_ref, out_ref, first_ref, keys_s, values_s, *, chunk
):
    half = attn_ref.shape[1]
    project(weight_ref, attn_ref, out_ref, chunk)

    @pl.when(lax.axis_index("ctx") == 0)
    def _():
        stage_keys(k_ref[:half], keys_s)
        stage_values(v_ref[:half], values_s)

        def queries_of(unit):
            return q_ref[:half, unit.lane : unit.lane + 2 * LANES]

        window_heads(queries_of, keys_s, values_s, bias_ref.at[pl.ds(half, half)], first_ref, q_ref.shape[1])


def window_lower_kernel(
    q_ref, k_ref, v_ref, halo_ref, weight_ref, bias_ref, first_ref, kw_ref, vw_ref,
    out_ref, pair_held, attn_s, keys_s, values_s, sems, *, chunk
):
    width = kw_ref.shape[1]
    copies = [
        pltpu.make_async_copy(kw_ref, pair_held.at[:, pl.ds(0, width)], sems.at[0]),
        pltpu.make_async_copy(vw_ref, pair_held.at[:, pl.ds(width, width)], sems.at[1]),
    ]
    for copy in copies:
        copy.start()
    half = halo_ref.shape[0]
    kv_width = k_ref.shape[1]
    ctx = lax.axis_index("ctx")

    @pl.when(ctx == 0)
    def _():
        attn_s[...] = first_ref[...]

    @pl.when(ctx != 0)
    def _():
        stage_keys(jnp.concatenate([halo_ref[:, :kv_width], k_ref[:half]], axis=0), keys_s)
        stage_values(jnp.concatenate([halo_ref[:, kv_width:], v_ref[:half]], axis=0), values_s)

        def queries_of(unit):
            return q_ref[:half, unit.lane : unit.lane + 2 * LANES]

        window_heads(queries_of, keys_s, values_s, bias_ref, attn_s, q_ref.shape[1])

    project(weight_ref, attn_s, out_ref, chunk)
    for copy in copies:
        copy.wait()


def add_and_norm(own_ref, other_ref, gain_ref, branch_ref, normed_ref, first_row, sum_s, keep_ref, chunk):
    width, rows = own_ref.shape
    head = lax.axis_index("head")

    def add(c, squares):
        part = pl.ds(pl.multiple_of(c * chunk, 16), chunk)
        total = own_ref[part, :].astype(F32) + other_ref[part, :].astype(F32)
        sum_s[part, :] = total
        rounded = total.astype(BF16)
        if keep_ref is not None:
            rounded = jnp.where(head == 0, rounded, keep_ref[part, :])
        branch_ref[part, :] = rounded
        return squares + jnp.sum(total * total, axis=0, keepdims=True)

    squares = lax.fori_loop(0, width // chunk, add, jnp.zeros((1, rows), F32))
    factor = lax.rsqrt(squares * (1.0 / width) + 1e-05)
    for first in range(0, width, LANES):
        last = min(first + LANES, width)
        piece = jnp.transpose(sum_s[first:last, :] * factor) * gain_ref[first:last][None, :]
        normed_ref[first_row : first_row + rows, first:last] = piece.astype(BF16)


def norm_upper_kernel(
    own_ref, other_ref, gain_ref, pair_ref, branch_ref, normed_ref, kv_ref, sum_s, *, chunk
):
    add_and_norm(own_ref, other_ref, gain_ref, branch_ref, normed_ref, 0, sum_s, None, chunk)
    kv_ref[...] = dot(normed_ref[...], pair_ref[...], ((1,), (0,))).astype(BF16)


def causal_upper_kernel(
    own_ref, other_ref, gain_ref, pair_ref, qw_ref, kept_ref, normed_ref, kv_up_ref, bias_ref,
    lower_bias_ref, branch_ref, q_ref, kv_ref, out_ref,
    branch_s, out_s, upper_q_s, normed_s, sum_s, keys_s, values_s, sems, unit_sems, *, chunk
):
    half = own_ref.shape[1]
    kv_width = kv_ref.shape[1] // 2
    q_width = qw_ref.shape[1]
    normed_s[half:, :] = normed_ref[...]
    add_and_norm(own_ref, other_ref, gain_ref, branch_s, normed_s, 0, sum_s, kept_ref, chunk)
    branch_out = pltpu.make_async_copy(branch_s, branch_ref, sems.at[0])
    branch_out.start()
    stage_keys(kv_up_ref[:, :kv_width], keys_s)
    stage_values(kv_up_ref[:, kv_width:], values_s)

    queries = dot(normed_s[...], qw_ref[...], ((1,), (0,))).astype(BF16)
    q_ref[...] = queries[:half]
    upper_q_s[...] = queries[half:]

    def queries_of(unit):
        return upper_q_s[:, unit.lane : unit.lane + 2 * LANES]

    causal_heads(queries_of, keys_s, values_s, bias_ref, out_s, q_width, lambda unit: None)
    upper_out = pltpu.make_async_copy(out_s, out_ref.at[pl.ds(half, half)], sems.at[1])
    upper_out.start()
    kv_ref[...] = dot(normed_s[:half, :], pair_ref[...], ((1,), (0,))).astype(BF16)
    branch_out.wait()
    upper_out.wait()

    @pl.when(lax.axis_index("ctx") == 0)
    def _():
        stage_keys(kv_ref[:, :kv_width], keys_s)
        stage_values(kv_ref[:, kv_width:], values_s)
        attend_lower(q_ref, keys_s, values_s, lower_bias_ref.at[pl.ds(half, half)], out_s, out_ref, unit_sems)


def attend_lower(q_ref, keys_s, values_s, bias_ref, out_s, out_ref, sems):
    half, q_width = q_ref.shape
    copies = []

    def queries_of(unit):
        return q_ref[:, unit.lane : unit.lane + 2 * LANES]

    def ready(unit):
        columns = pl.ds(unit.lane, 2 * LANES)
        copy = pltpu.make_async_copy(
            out_s.at[:, columns], out_ref.at[pl.ds(0, half), columns], sems.at[len(copies)]
        )
        copy.start()
        copies.append(copy)

    causal_heads(queries_of, keys_s, values_s, bias_ref, out_s, q_width, ready)
    for copy in copies:
        copy.wait()


def causal_lower_kernel(
    q_ref, kv_ref, halo_ref, bias_ref, given_ref, out_ref, out_s, keys_s, values_s, sems
):
    half, q_width = q_ref.shape
    kv_width = kv_ref.shape[1] // 2

    @pl.when(lax.axis_index("ctx") != 0)
    def _():
        stage_keys(jnp.concatenate([halo_ref[:, :kv_width], kv_ref[:, :kv_width]], axis=0), keys_s)
        stage_values(jnp.concatenate([halo_ref[:, kv_width:], kv_ref[:, kv_width:]], axis=0), values_s)
        attend_lower(q_ref, keys_s, values_s, bias_ref, out_s, out_ref, sems)


def attention_scratch(kv_heads, keys):
    return [
        pltpu.VMEM((kv_heads, 2, keys, LANES), BF16),
        pltpu.VMEM((kv_heads, HD + TAIL, keys), BF16),
    ]


def local(
    window_queries,
    window_keys,
    window_values,
    out_weight,
    norm_gain,
    query_weight,
    key_weight,
    value_weight,
    doc_lengths,
):
    rows, q_width = window_queries.shape
    kv_width = window_keys.shape[1]
    kv_heads = kv_width // HD
    width = out_weight.shape[1]
    half = rows // 2
    chunk = width // 2
    dma = pltpu.SemaphoreType.DMA
    lengths, queries, keys, values = [
        in_hbm(x) for x in (doc_lengths, window_queries, window_keys, window_values)
    ]

    packed = pl.pallas_call(
        pack_kernel,
        out_shape=jax.ShapeDtypeStruct((half, 2 * kv_width), BF16),
        in_specs=hbm_specs(2),
        out_specs=vmem_specs(1)[0],
        scratch_shapes=[dma((2,))],
        compiler_params=params(16),
        cost_estimate=pl.CostEstimate(flops=10**10, bytes_accessed=10**6, transcendentals=0),
        name="pack",
    )(keys, values)
    halo = shifted(packed, "ctx")
    attn_s = pltpu.VMEM((q_width, half), BF16)
    (
        attn_upper, q_held, k_held, v_held, window_bias, upper_causal, lower_causal, gain
    ) = pl.pallas_call(
        window_upper_kernel,
        out_shape=(
            attn_s,
            pltpu.VMEM((rows, q_width), BF16),
            pltpu.VMEM((rows, kv_width), BF16),
            pltpu.VMEM((rows, kv_width), BF16),
            pltpu.VMEM((rows, half), F32),
            pltpu.VMEM((half, half), F32),
            pltpu.VMEM((rows, half), F32),
            pltpu.VMEM((width,), F32),
        ),
        in_specs=hbm_specs(5),
        out_specs=tuple(vmem_specs(8)),
        scratch_shapes=[pltpu.SMEM(doc_lengths.shape, jnp.int32)]
        + attention_scratch(kv_heads, half)
        + [pltpu.VMEM((half, half), F32), dma((8,))],
        compiler_params=params(8),
        name="window_upper",
    )(lengths, queries, keys, values, in_hbm(norm_gain))
    held = in_vmem(jnp.transpose(out_weight))
    own_upper, attn_first = pl.pallas_call(
        functools.partial(project_upper_kernel, chunk=chunk),
        out_shape=(pltpu.VMEM((width, half), BF16), attn_s),
        in_specs=vmem_specs(6),
        out_specs=tuple(vmem_specs(2)),
        scratch_shapes=attention_scratch(kv_heads, half),
        compiler_params=params(8),
        name="project_upper",
    )(held, attn_upper, q_held, k_held, v_held, window_bias)
    query_held = in_vmem(query_weight)
    other_upper = swapped(own_upper, "head")
    own_lower, pair_held = pl.pallas_call(
        functools.partial(window_lower_kernel, chunk=chunk),
        out_shape=(pltpu.VMEM((width, half), BF16), pltpu.VMEM((width, 2 * kv_width), BF16)),
        in_specs=vmem_specs(7) + hbm_specs(2),
        out_specs=tuple(vmem_specs(2)),
        scratch_shapes=[attn_s] + attention_scratch(kv_heads, rows) + [dma((2,))],
        compiler_params=params(16),
        name="window_lower",
    )(q_held, k_held, v_held, in_vmem(halo), held, window_bias, attn_first, in_hbm(key_weight), in_hbm(value_weight))
    other_lower = swapped(own_lower, "head")
    branch_upper, normed_upper, pairs_upper = pl.pallas_call(
        functools.partial(norm_upper_kernel, chunk=192),
        out_shape=(
            pltpu.VMEM((width, half), BF16),
            pltpu.VMEM((half, width), BF16),
            pltpu.VMEM((half, 2 * kv_width), BF16),
        ),
        in_specs=vmem_specs(4),
        out_specs=tuple(vmem_specs(3)),
        scratch_shapes=[pltpu.VMEM((width, half), F32)],
        compiler_params=params(16),
        name="norm_upper",
    )(own_upper, other_upper, gain, pair_held)
    earlier = shifted(pairs_upper, "ctx")
    branch, causal_queries, pairs_lower, causal_out = pl.pallas_call(
        functools.partial(causal_upper_kernel, chunk=192),
        out_shape=(
            pltpu.HBM((width, half), BF16),
            pltpu.VMEM((half, q_width), BF16),
            pltpu.VMEM((half, 2 * kv_width), BF16),
            pltpu.HBM((rows, q_width), BF16),
        ),
        in_specs=vmem_specs(10),
        out_specs=(hbm_specs(1)[0], *vmem_specs(2), hbm_specs(1)[0]),
        scratch_shapes=[
            pltpu.VMEM((width, half), BF16),
            pltpu.VMEM((half, q_width), BF16),
            pltpu.VMEM((half, q_width), BF16),
            pltpu.VMEM((rows, width), BF16),
            pltpu.VMEM((width, half), F32),
        ]
        + attention_scratch(kv_heads, half)
        + [dma((2,)), dma((q_width // (2 * LANES),))],
        compiler_params=params(16),
        name="causal_upper",
    )(
        own_lower, other_lower, gain, pair_held, query_held,
        branch_upper, normed_upper, pairs_upper, upper_causal, lower_causal,
    )
    causal_out = pl.pallas_call(
        causal_lower_kernel,
        out_shape=pltpu.HBM((rows, q_width), BF16),
        in_specs=vmem_specs(4) + hbm_specs(1),
        out_specs=hbm_specs(1)[0],
        scratch_shapes=[pltpu.VMEM((half, q_width), BF16)]
        + attention_scratch(kv_heads, rows)
        + [dma((q_width // (2 * LANES),))],
        input_output_aliases={4: 0},
        compiler_params=params(16),
        name="causal_lower",
    )(causal_queries, pairs_lower, in_vmem(earlier), lower_causal, causal_out)
    return (jnp.transpose(branch), causal_out)


def solution(mesh):
    placed = (
        P("ctx", "head"),
        P("ctx", "head"),
        P("ctx", "head"),
        P("head", None),
        P(),
        P(None, "head"),
        P(None, "head"),
        P(None, "head"),
        P(),
    )
    return jax.shard_map(
        local,
        mesh=mesh,
        in_specs=placed,
        out_specs=(P(("ctx", "head"), None), P("ctx", "head")),
        check_vma=False,
    )
```

```python
import functools

import jax
import jax.numpy as jnp
from jax import lax
from jax.experimental import pallas as pl
from jax.experimental.pallas import tpu as pltpu
from jax.sharding import PartitionSpec as P

HD = 64
WIN = 128
LANES = 128
NEG = -1e30
TAIL = 16

F32 = jnp.float32
BF16 = jnp.bfloat16
MIB = 1024 * 1024


def params(mib):
    return pltpu.CompilerParams(vmem_limit_bytes=mib * MIB)


def in_vmem(array):
    return pltpu.with_memory_space_constraint(array, pltpu.VMEM)


def in_hbm(array):
    return pltpu.with_memory_space_constraint(array, pltpu.HBM)


def hbm_specs(count):
    return [pl.BlockSpec(memory_space=pltpu.HBM)] * count


def vmem_specs(count):
    return [pl.BlockSpec(memory_space=pltpu.VMEM)] * count


def dot(a, b, dims):
    return lax.dot_general(a, b, (dims, ((), ())), preferred_element_type=F32)


def shifted(block, axis):
    size = lax.axis_size(axis)
    return lax.ppermute(block, axis, [(i, (i + 1) % size) for i in range(size)])


def swapped(block, axis):
    size = lax.axis_size(axis)
    return lax.ppermute(block, axis, [(i, size - 1 - i) for i in range(size)])


def lower_bias(lengths_ref, half, width):
    ctx = lax.axis_index("ctx")
    first = jnp.where(ctx == 0, half, 0)
    split = first + lengths_ref[2 * ctx]
    return bias_of(2 * half, half, half, first, split, width)


def upper_bias(lengths_ref, half, width):
    ctx = lax.axis_index("ctx")
    last = lengths_ref.shape[0] - 1
    split = lengths_ref[jnp.minimum(2 * ctx + 2, last)]
    split = jnp.where(ctx == lax.axis_size("ctx") - 1, 2 * half, split)
    return bias_of(half, half, 0, 0, split, width)


def bias_of(keys, rows, row_offset, first, split, width):
    key = lax.broadcasted_iota(jnp.int32, (keys, rows), 0)
    row = lax.broadcasted_iota(jnp.int32, (keys, rows), 1) + row_offset
    lowest = jnp.where(row >= split, split, first)
    if width is not None:
        lowest = jnp.maximum(lowest, row - (width - 1))
    return jnp.where((key >= lowest) & (key <= row), 0.0, NEG).astype(F32)


def stage_keys(keys, keys_ref):
    scaled = (keys.astype(F32) * HD ** (-0.5)).astype(BF16)
    lane = lax.broadcasted_iota(jnp.int32, (keys.shape[0], LANES), 1)
    zero = jnp.zeros((keys.shape[0], LANES), BF16)
    for pair in range(keys.shape[1] // LANES):
        tile = scaled[:, pair * LANES : (pair + 1) * LANES]
        turned = jnp.concatenate([tile[:, HD:], tile[:, :HD]], axis=1)
        keys_ref[2 * pair, 0] = jnp.where(lane < HD, tile, zero)
        keys_ref[2 * pair, 1] = jnp.where(lane < HD, zero, turned)
        keys_ref[2 * pair + 1, 0] = jnp.where(lane < HD, turned, zero)
        keys_ref[2 * pair + 1, 1] = jnp.where(lane < HD, zero, tile)


def stage_values(values, values_ref):
    count = values.shape[0]
    turned = jnp.transpose(values)
    for head in range(values.shape[1] // HD):
        values_ref[head, :HD, :] = turned[head * HD : (head + 1) * HD]
        values_ref[head, HD:, :] = jnp.ones((TAIL, count), BF16)


class Unit:
    def __init__(self, g, lane):
        self.g, self.lane = g, lane


def units_of(kv_heads, q_width):
    step = 2 * LANES
    group = q_width // kv_heads
    return [Unit(lane // group, lane) for lane in range(0, q_width, step)]


def unit_scores(queries, unit, keys_ref):
    stacked = jnp.concatenate([queries[:, :LANES], queries[:, LANES:]], axis=0)
    keys = jnp.concatenate([keys_ref[unit.g, 0], keys_ref[unit.g, 1]], axis=0)
    return dot(keys, stacked, ((1,), (1,)))


def unit_weighted(scores, unit, values_ref, bias):
    count = bias.shape[0]
    wide = jnp.concatenate([bias, bias], axis=1)
    patterns = []
    for side in range(2):
        masked = scores[side * count : (side + 1) * count] + wide
        highest = jnp.max(masked, axis=0, keepdims=True)
        patterns.append(jnp.exp((masked - highest).astype(BF16)))
    return dot(values_ref[unit.g], jnp.concatenate(patterns, axis=1), ((1,), (0,)))


def pipelined(units, queries_of, keys_ref, values_ref, bias, write):
    count = len(units)
    scores = [unit_scores(queries_of(unit), unit, keys_ref) for unit in units[:2]]

    def finish(unit, weighted):
        write(unit, weighted[:HD] * (1.0 / weighted[HD : HD + 1]))

    before = None
    for i, unit in enumerate(units):
        now = scores.pop(0)
        if i + 2 < count:
            scores.append(unit_scores(queries_of(units[i + 2]), units[i + 2], keys_ref))
        weighted = unit_weighted(now, unit, values_ref, bias)
        if before is not None:
            finish(*before)
        before = (unit, weighted)
    finish(*before)


def window_heads(queries_of, keys_ref, values_ref, bias_ref, out_ref, q_width):
    def write(unit, part):
        rows = part.shape[1] // 4
        rounded = part.astype(BF16)
        for side in range(2):
            for t in range(2):
                at = (side * 2 + t) * rows
                start = unit.lane + t * LANES + side * HD
                out_ref[start : start + HD, :] = rounded[:, at : at + rows]

    pipelined(units_of(keys_ref.shape[0], q_width), queries_of, keys_ref, values_ref, bias_ref[...], write)


def causal_heads(queries_of, keys_ref, values_ref, bias_ref, out_ref, q_width, ready):
    def write(unit, part):
        rows = part.shape[1] // 4
        for t in range(2):
            low = part[:, t * rows : (t + 1) * rows]
            high = part[:, (2 + t) * rows : (3 + t) * rows]
            lane = unit.lane + t * LANES
            out_ref[:, lane : lane + LANES] = jnp.transpose(
                jnp.concatenate([low, high], axis=0).astype(BF16)
            )
        ready(unit)

    pipelined(units_of(keys_ref.shape[0], q_width), queries_of, keys_ref, values_ref, bias_ref[...], write)


def pack_kernel(k_ref, v_ref, out_ref, sems):
    half = out_ref.shape[0]
    kv_width = k_ref.shape[1]
    copies = [
        pltpu.make_async_copy(k_ref.at[pl.ds(half, half)], out_ref.at[:, pl.ds(0, kv_width)], sems.at[0]),
        pltpu.make_async_copy(
            v_ref.at[pl.ds(half, half)], out_ref.at[:, pl.ds(kv_width, kv_width)], sems.at[1]
        ),
    ]
    for copy in copies:
        copy.start()
    for copy in copies:
        copy.wait()


def window_upper_kernel(
    lengths_ref, q_ref, k_ref, v_ref, gain_ref,
    attn_ref, q_held, k_held, v_held, window_bias, upper_causal, lower_causal, gain_held,
    lengths_s, keys_s, values_s, bias_s, sems
):
    half = attn_ref.shape[1]
    upper, lower = pl.ds(half, half), pl.ds(0, half)
    first = [
        pltpu.make_async_copy(lengths_ref, lengths_s, sems.at[0]),
        pltpu.make_async_copy(k_ref.at[upper], k_held.at[upper], sems.at[1]),
        pltpu.make_async_copy(v_ref.at[upper], v_held.at[upper], sems.at[2]),
        pltpu.make_async_copy(q_ref.at[upper], q_held.at[upper], sems.at[3]),
    ]
    last = [
        pltpu.make_async_copy(k_ref.at[lower], k_held.at[lower], sems.at[4]),
        pltpu.make_async_copy(v_ref.at[lower], v_held.at[lower], sems.at[5]),
        pltpu.make_async_copy(q_ref.at[lower], q_held.at[lower], sems.at[6]),
        pltpu.make_async_copy(gain_ref, gain_held, sems.at[7]),
    ]
    for copy in first + last:
        copy.start()
    first[0].wait()
    bias_s[...] = upper_bias(lengths_s, half, WIN)
    window_bias[...] = lower_bias(lengths_s, half, WIN)
    upper_causal[...] = upper_bias(lengths_s, half, None)
    lower_causal[...] = lower_bias(lengths_s, half, None)
    first[1].wait()
    stage_keys(k_held[half:], keys_s)
    first[2].wait()
    stage_values(v_held[half:], values_s)
    first[3].wait()

    def queries_of(unit):
        return q_held[half:, unit.lane : unit.lane + 2 * LANES]

    window_heads(queries_of, keys_s, values_s, bias_s, attn_ref, q_held.shape[1])
    for copy in last:
        copy.wait()


def project(weight_ref, attn_ref, out_ref, chunk):
    for first in range(0, out_ref.shape[0], chunk):
        part = slice(first, first + chunk)
        out_ref[part, :] = dot(weight_ref[part, :], attn_ref[...], ((1,), (0,))).astype(BF16)


def project_upper_kernel(
    weight_ref, attn_ref, q_ref, k_ref, v_ref, bias_ref, out_ref, first_ref, keys_s, values_s, *, chunk
):
    half = attn_ref.shape[1]
    project(weight_ref, attn_ref, out_ref, chunk)

    @pl.when(lax.axis_index("ctx") == 0)
    def _():
        stage_keys(k_ref[:half], keys_s)
        stage_values(v_ref[:half], values_s)

        def queries_of(unit):
            return q_ref[:half, unit.lane : unit.lane + 2 * LANES]

        window_heads(queries_of, keys_s, values_s, bias_ref.at[pl.ds(half, half)], first_ref, q_ref.shape[1])


def window_lower_kernel(
    q_ref, k_ref, v_ref, halo_ref, weight_ref, bias_ref, first_ref, kw_ref, vw_ref,
    out_ref, pair_held, attn_s, keys_s, values_s, sems, *, chunk
):
    width = kw_ref.shape[1]
    copies = [
        pltpu.make_async_copy(kw_ref, pair_held.at[:, pl.ds(0, width)], sems.at[0]),
        pltpu.make_async_copy(vw_ref, pair_held.at[:, pl.ds(width, width)], sems.at[1]),
    ]
    for copy in copies:
        copy.start()
    half = halo_ref.shape[0]
    kv_width = k_ref.shape[1]
    ctx = lax.axis_index("ctx")

    @pl.when(ctx == 0)
    def _():
        attn_s[...] = first_ref[...]

    @pl.when(ctx != 0)
    def _():
        stage_keys(jnp.concatenate([halo_ref[:, :kv_width], k_ref[:half]], axis=0), keys_s)
        stage_values(jnp.concatenate([halo_ref[:, kv_width:], v_ref[:half]], axis=0), values_s)

        def queries_of(unit):
            return q_ref[:half, unit.lane : unit.lane + 2 * LANES]

        window_heads(queries_of, keys_s, values_s, bias_ref, attn_s, q_ref.shape[1])

    project(weight_ref, attn_s, out_ref, chunk)
    for copy in copies:
        copy.wait()


def add_and_norm(own_ref, other_ref, gain_ref, branch_ref, normed_ref, first_row, sum_s, keep_ref, chunk):
    width, rows = own_ref.shape
    head = lax.axis_index("head")

    def add(c, squares):
        part = pl.ds(pl.multiple_of(c * chunk, 16), chunk)
        total = own_ref[part, :].astype(F32) + other_ref[part, :].astype(F32)
        sum_s[part, :] = total
        rounded = total.astype(BF16)
        if keep_ref is not None:
            rounded = jnp.where(head == 0, rounded, keep_ref[part, :])
        branch_ref[part, :] = rounded
        return squares + jnp.sum(total * total, axis=0, keepdims=True)

    squares = lax.fori_loop(0, width // chunk, add, jnp.zeros((1, rows), F32))
    factor = lax.rsqrt(squares * (1.0 / width) + 1e-05)
    for first in range(0, width, LANES):
        last = min(first + LANES, width)
        piece = jnp.transpose(sum_s[first:last, :] * factor) * gain_ref[first:last][None, :]
        normed_ref[first_row : first_row + rows, first:last] = piece.astype(BF16)


def norm_upper_kernel(
    own_ref, other_ref, gain_ref, pair_ref, branch_ref, normed_ref, kv_ref, sum_s, *, chunk
):
    add_and_norm(own_ref, other_ref, gain_ref, branch_ref, normed_ref, 0, sum_s, None, chunk)
    kv_ref[...] = dot(normed_ref[...], pair_ref[...], ((1,), (0,))).astype(BF16)


def causal_upper_kernel(
    own_ref, other_ref, gain_ref, pair_ref, qw_ref, kept_ref, normed_ref, kv_up_ref, bias_ref,
    lower_bias_ref, branch_ref, q_ref, kv_ref, out_ref,
    branch_s, out_s, upper_q_s, normed_s, sum_s, keys_s, values_s, sems, unit_sems, *, chunk
):
    half = own_ref.shape[1]
    kv_width = kv_ref.shape[1] // 2
    q_width = qw_ref.shape[1]
    normed_s[half:, :] = normed_ref[...]
    add_and_norm(own_ref, other_ref, gain_ref, branch_s, normed_s, 0, sum_s, kept_ref, chunk)
    branch_out = pltpu.make_async_copy(branch_s, branch_ref, sems.at[0])
    branch_out.start()
    stage_keys(kv_up_ref[:, :kv_width], keys_s)
    stage_values(kv_up_ref[:, kv_width:], values_s)

    queries = dot(normed_s[...], qw_ref[...], ((1,), (0,))).astype(BF16)
    q_ref[...] = queries[:half]
    upper_q_s[...] = queries[half:]

    def queries_of(unit):
        return upper_q_s[:, unit.lane : unit.lane + 2 * LANES]

    causal_heads(queries_of, keys_s, values_s, bias_ref, out_s, q_width, lambda unit: None)
    upper_out = pltpu.make_async_copy(out_s, out_ref.at[pl.ds(half, half)], sems.at[1])
    upper_out.start()
    kv_ref[...] = dot(normed_s[:half, :], pair_ref[...], ((1,), (0,))).astype(BF16)
    branch_out.wait()
    upper_out.wait()

    @pl.when(lax.axis_index("ctx") == 0)
    def _():
        stage_keys(kv_ref[:, :kv_width], keys_s)
        stage_values(kv_ref[:, kv_width:], values_s)
        attend_lower(q_ref, keys_s, values_s, lower_bias_ref.at[pl.ds(half, half)], out_s, out_ref, unit_sems)


def attend_lower(q_ref, keys_s, values_s, bias_ref, out_s, out_ref, sems):
    half, q_width = q_ref.shape
    copies = []

    def queries_of(unit):
        return q_ref[:, unit.lane : unit.lane + 2 * LANES]

    def ready(unit):
        columns = pl.ds(unit.lane, 2 * LANES)
        copy = pltpu.make_async_copy(
            out_s.at[:, columns], out_ref.at[pl.ds(0, half), columns], sems.at[len(copies)]
        )
        copy.start()
        copies.append(copy)

    causal_heads(queries_of, keys_s, values_s, bias_ref, out_s, q_width, ready)
    for copy in copies:
        copy.wait()


def causal_lower_kernel(
    q_ref, kv_ref, halo_ref, bias_ref, given_ref, out_ref, out_s, keys_s, values_s, sems
):
    half, q_width = q_ref.shape
    kv_width = kv_ref.shape[1] // 2

    @pl.when(lax.axis_index("ctx") != 0)
    def _():
        stage_keys(jnp.concatenate([halo_ref[:, :kv_width], kv_ref[:, :kv_width]], axis=0), keys_s)
        stage_values(jnp.concatenate([halo_ref[:, kv_width:], kv_ref[:, kv_width:]], axis=0), values_s)
        attend_lower(q_ref, keys_s, values_s, bias_ref, out_s, out_ref, sems)


def attention_scratch(kv_heads, keys):
    return [
        pltpu.VMEM((kv_heads, 2, keys, LANES), BF16),
        pltpu.VMEM((kv_heads, HD + TAIL, keys), BF16),
    ]


def local(
    window_queries,
    window_keys,
    window_values,
    out_weight,
    norm_gain,
    query_weight,
    key_weight,
    value_weight,
    doc_lengths,
):
    rows, q_width = window_queries.shape
    kv_width = window_keys.shape[1]
    kv_heads = kv_width // HD
    width = out_weight.shape[1]
    half = rows // 2
    chunk = width // 2
    dma = pltpu.SemaphoreType.DMA
    lengths, queries, keys, values = [
        in_hbm(x) for x in (doc_lengths, window_queries, window_keys, window_values)
    ]

    packed = pl.pallas_call(
        pack_kernel,
        out_shape=jax.ShapeDtypeStruct((half, 2 * kv_width), BF16),
        in_specs=hbm_specs(2),
        out_specs=vmem_specs(1)[0],
        scratch_shapes=[dma((2,))],
        compiler_params=params(16),
        cost_estimate=pl.CostEstimate(flops=10**10, bytes_accessed=10**6, transcendentals=0),
        name="pack",
    )(keys, values)
    halo = shifted(packed, "ctx")
    attn_s = pltpu.VMEM((q_width, half), BF16)
    (
        attn_upper, q_held, k_held, v_held, window_bias, upper_causal, lower_causal, gain
    ) = pl.pallas_call(
        window_upper_kernel,
        out_shape=(
            attn_s,
            pltpu.VMEM((rows, q_width), BF16),
            pltpu.VMEM((rows, kv_width), BF16),
            pltpu.VMEM((rows, kv_width), BF16),
            pltpu.VMEM((rows, half), F32),
            pltpu.VMEM((half, half), F32),
            pltpu.VMEM((rows, half), F32),
            pltpu.VMEM((width,), F32),
        ),
        in_specs=hbm_specs(5),
        out_specs=tuple(vmem_specs(8)),
        scratch_shapes=[pltpu.SMEM(doc_lengths.shape, jnp.int32)]
        + attention_scratch(kv_heads, half)
        + [pltpu.VMEM((half, half), F32), dma((8,))],
        compiler_params=params(8),
        name="window_upper",
    )(lengths, queries, keys, values, in_hbm(norm_gain))
    held = in_vmem(jnp.transpose(out_weight))
    own_upper, attn_first = pl.pallas_call(
        functools.partial(project_upper_kernel, chunk=chunk),
        out_shape=(pltpu.VMEM((width, half), BF16), attn_s),
        in_specs=vmem_specs(6),
        out_specs=tuple(vmem_specs(2)),
        scratch_shapes=attention_scratch(kv_heads, half),
        compiler_params=params(8),
        name="project_upper",
    )(held, attn_upper, q_held, k_held, v_held, window_bias)
    query_held = in_vmem(query_weight)
    other_upper = swapped(own_upper, "head")
    own_lower, pair_held = pl.pallas_call(
        functools.partial(window_lower_kernel, chunk=chunk),
        out_shape=(pltpu.VMEM((width, half), BF16), pltpu.VMEM((width, 2 * kv_width), BF16)),
        in_specs=vmem_specs(7) + hbm_specs(2),
        out_specs=tuple(vmem_specs(2)),
        scratch_shapes=[attn_s] + attention_scratch(kv_heads, rows) + [dma((2,))],
        compiler_params=params(16),
        name="window_lower",
    )(q_held, k_held, v_held, in_vmem(halo), held, window_bias, attn_first, in_hbm(key_weight), in_hbm(value_weight))
    other_lower = swapped(own_lower, "head")
    branch_upper, normed_upper, pairs_upper = pl.pallas_call(
        functools.partial(norm_upper_kernel, chunk=192),
        out_shape=(
            pltpu.VMEM((width, half), BF16),
            pltpu.VMEM((half, width), BF16),
            pltpu.VMEM((half, 2 * kv_width), BF16),
        ),
        in_specs=vmem_specs(4),
        out_specs=tuple(vmem_specs(3)),
        scratch_shapes=[pltpu.VMEM((width, half), F32)],
        compiler_params=params(16),
        name="norm_upper",
    )(own_upper, other_upper, gain, pair_held)
    earlier = shifted(pairs_upper, "ctx")
    branch, causal_queries, pairs_lower, causal_out = pl.pallas_call(
        functools.partial(causal_upper_kernel, chunk=192),
        out_shape=(
            pltpu.HBM((width, half), BF16),
            pltpu.VMEM((half, q_width), BF16),
            pltpu.VMEM((half, 2 * kv_width), BF16),
            pltpu.HBM((rows, q_width), BF16),
        ),
        in_specs=vmem_specs(10),
        out_specs=(hbm_specs(1)[0], *vmem_specs(2), hbm_specs(1)[0]),
        scratch_shapes=[
            pltpu.VMEM((width, half), BF16),
            pltpu.VMEM((half, q_width), BF16),
            pltpu.VMEM((half, q_width), BF16),
            pltpu.VMEM((rows, width), BF16),
            pltpu.VMEM((width, half), F32),
        ]
        + attention_scratch(kv_heads, half)
        + [dma((2,)), dma((q_width // (2 * LANES),))],
        compiler_params=params(16),
        name="causal_upper",
    )(
        own_lower, other_lower, gain, pair_held, query_held,
        branch_upper, normed_upper, pairs_upper, upper_causal, lower_causal,
    )
    causal_out = pl.pallas_call(
        causal_lower_kernel,
        out_shape=pltpu.HBM((rows, q_width), BF16),
        in_specs=vmem_specs(4) + hbm_specs(1),
        out_specs=hbm_specs(1)[0],
        scratch_shapes=[pltpu.VMEM((half, q_width), BF16)]
        + attention_scratch(kv_heads, rows)
        + [dma((q_width // (2 * LANES),))],
        input_output_aliases={4: 0},
        compiler_params=params(16),
        name="causal_lower",
    )(causal_queries, pairs_lower, in_vmem(earlier), lower_causal, causal_out)
    return (jnp.transpose(branch), causal_out)


def solution(mesh):
    placed = (
        P("ctx", "head"),
        P("ctx", "head"),
        P("ctx", "head"),
        P("head", None),
        P(),
        P(None, "head"),
        P(None, "head"),
        P(None, "head"),
        P(),
    )
    return jax.shard_map(
        local,
        mesh=mesh,
        in_specs=placed,
        out_specs=(P(("ctx", "head"), None), P("ctx", "head")),
        check_vma=False,
    )
```

```python
import functools

import jax
import jax.numpy as jnp
from jax import lax
from jax.experimental import pallas as pl
from jax.experimental.pallas import tpu as pltpu
from jax.sharding import PartitionSpec as P

HD = 64
WIN = 128
LANES = 128
NEG = -1e30
TAIL = 16

F32 = jnp.float32
BF16 = jnp.bfloat16
MIB = 1024 * 1024


def params(mib):
    return pltpu.CompilerParams(vmem_limit_bytes=mib * MIB)


def in_vmem(array):
    return pltpu.with_memory_space_constraint(array, pltpu.VMEM)


def in_hbm(array):
    return pltpu.with_memory_space_constraint(array, pltpu.HBM)


def hbm_specs(count):
    return [pl.BlockSpec(memory_space=pltpu.HBM)] * count


def vmem_specs(count):
    return [pl.BlockSpec(memory_space=pltpu.VMEM)] * count


def dot(a, b, dims):
    return lax.dot_general(a, b, (dims, ((), ())), preferred_element_type=F32)


def shifted(block, axis):
    size = lax.axis_size(axis)
    return lax.ppermute(block, axis, [(i, (i + 1) % size) for i in range(size)])


def swapped(block, axis):
    size = lax.axis_size(axis)
    return lax.ppermute(block, axis, [(i, size - 1 - i) for i in range(size)])


def lower_bias(lengths_ref, half, width):
    ctx = lax.axis_index("ctx")
    first = jnp.where(ctx == 0, half, 0)
    split = first + lengths_ref[2 * ctx]
    return bias_of(2 * half, half, half, first, split, width)


def upper_bias(lengths_ref, half, width):
    ctx = lax.axis_index("ctx")
    last = lengths_ref.shape[0] - 1
    split = lengths_ref[jnp.minimum(2 * ctx + 2, last)]
    split = jnp.where(ctx == lax.axis_size("ctx") - 1, 2 * half, split)
    return bias_of(half, half, 0, 0, split, width)


def bias_of(keys, rows, row_offset, first, split, width):
    key = lax.broadcasted_iota(jnp.int32, (keys, rows), 0)
    row = lax.broadcasted_iota(jnp.int32, (keys, rows), 1) + row_offset
    lowest = jnp.where(row >= split, split, first)
    if width is not None:
        lowest = jnp.maximum(lowest, row - (width - 1))
    return jnp.where((key >= lowest) & (key <= row), 0.0, NEG).astype(F32)


def stage_keys(keys, keys_ref):
    scaled = (keys.astype(F32) * HD ** (-0.5)).astype(BF16)
    lane = lax.broadcasted_iota(jnp.int32, (keys.shape[0], LANES), 1)
    zero = jnp.zeros((keys.shape[0], LANES), BF16)
    for pair in range(keys.shape[1] // LANES):
        tile = scaled[:, pair * LANES : (pair + 1) * LANES]
        turned = jnp.concatenate([tile[:, HD:], tile[:, :HD]], axis=1)
        keys_ref[2 * pair, 0] = jnp.where(lane < HD, tile, zero)
        keys_ref[2 * pair, 1] = jnp.where(lane < HD, zero, turned)
        keys_ref[2 * pair + 1, 0] = jnp.where(lane < HD, turned, zero)
        keys_ref[2 * pair + 1, 1] = jnp.where(lane < HD, zero, tile)


def stage_values(values, values_ref):
    count = values.shape[0]
    turned = jnp.transpose(values)
    for head in range(values.shape[1] // HD):
        values_ref[head, :HD, :] = turned[head * HD : (head + 1) * HD]
        values_ref[head, HD:, :] = jnp.ones((TAIL, count), BF16)


class Unit:
    def __init__(self, g, lane):
        self.g, self.lane = g, lane


def units_of(kv_heads, q_width):
    step = 2 * LANES
    group = q_width // kv_heads
    return [Unit(lane // group, lane) for lane in range(0, q_width, step)]


def unit_scores(queries, unit, keys_ref):
    stacked = jnp.concatenate([queries[:, :LANES], queries[:, LANES:]], axis=0)
    keys = jnp.concatenate([keys_ref[unit.g, 0], keys_ref[unit.g, 1]], axis=0)
    return dot(keys, stacked, ((1,), (1,)))


def unit_weighted(scores, unit, values_ref, bias):
    count = bias.shape[0]
    wide = jnp.concatenate([bias, bias], axis=1)
    patterns = []
    for side in range(2):
        masked = scores[side * count : (side + 1) * count] + wide
        highest = jnp.max(masked, axis=0, keepdims=True)
        patterns.append(jnp.exp((masked - highest).astype(BF16)))
    return dot(values_ref[unit.g], jnp.concatenate(patterns, axis=1), ((1,), (0,)))


def pipelined(units, queries_of, keys_ref, values_ref, bias, write):
    count = len(units)
    scores = [unit_scores(queries_of(unit), unit, keys_ref) for unit in units[:2]]

    def finish(unit, weighted):
        write(unit, weighted[:HD] * (1.0 / weighted[HD : HD + 1]))

    before = None
    for i, unit in enumerate(units):
        now = scores.pop(0)
        if i + 2 < count:
            scores.append(unit_scores(queries_of(units[i + 2]), units[i + 2], keys_ref))
        weighted = unit_weighted(now, unit, values_ref, bias)
        if before is not None:
            finish(*before)
        before = (unit, weighted)
    finish(*before)


def window_heads(queries_of, keys_ref, values_ref, bias_ref, out_ref, q_width):
    def write(unit, part):
        rows = part.shape[1] // 4
        rounded = part.astype(BF16)
        for side in range(2):
            for t in range(2):
                at = (side * 2 + t) * rows
                start = unit.lane + t * LANES + side * HD
                out_ref[start : start + HD, :] = rounded[:, at : at + rows]

    pipelined(units_of(keys_ref.shape[0], q_width), queries_of, keys_ref, values_ref, bias_ref[...], write)


def causal_heads(queries_of, keys_ref, values_ref, bias_ref, out_ref, q_width, ready):
    def write(unit, part):
        rows = part.shape[1] // 4
        for t in range(2):
            low = part[:, t * rows : (t + 1) * rows]
            high = part[:, (2 + t) * rows : (3 + t) * rows]
            lane = unit.lane + t * LANES
            out_ref[:, lane : lane + LANES] = jnp.transpose(
                jnp.concatenate([low, high], axis=0).astype(BF16)
            )
        ready(unit)

    pipelined(units_of(keys_ref.shape[0], q_width), queries_of, keys_ref, values_ref, bias_ref[...], write)


def pack_kernel(k_ref, v_ref, out_ref, sems):
    half = out_ref.shape[0]
    kv_width = k_ref.shape[1]
    copies = [
        pltpu.make_async_copy(k_ref.at[pl.ds(half, half)], out_ref.at[:, pl.ds(0, kv_width)], sems.at[0]),
        pltpu.make_async_copy(
            v_ref.at[pl.ds(half, half)], out_ref.at[:, pl.ds(kv_width, kv_width)], sems.at[1]
        ),
    ]
    for copy in copies:
        copy.start()
    for copy in copies:
        copy.wait()


def window_upper_kernel(
    lengths_ref, q_ref, k_ref, v_ref, gain_ref,
    attn_ref, q_held, k_held, v_held, window_bias, upper_causal, lower_causal, gain_held,
    lengths_s, keys_s, values_s, bias_s, sems
):
    half = attn_ref.shape[1]
    upper, lower = pl.ds(half, half), pl.ds(0, half)
    first = [
        pltpu.make_async_copy(lengths_ref, lengths_s, sems.at[0]),
        pltpu.make_async_copy(k_ref.at[upper], k_held.at[upper], sems.at[1]),
        pltpu.make_async_copy(v_ref.at[upper], v_held.at[upper], sems.at[2]),
        pltpu.make_async_copy(q_ref.at[upper], q_held.at[upper], sems.at[3]),
    ]
    last = [
        pltpu.make_async_copy(k_ref.at[lower], k_held.at[lower], sems.at[4]),
        pltpu.make_async_copy(v_ref.at[lower], v_held.at[lower], sems.at[5]),
        pltpu.make_async_copy(q_ref.at[lower], q_held.at[lower], sems.at[6]),
        pltpu.make_async_copy(gain_ref, gain_held, sems.at[7]),
    ]
    for copy in first + last:
        copy.start()
    first[0].wait()
    bias_s[...] = upper_bias(lengths_s, half, WIN)
    window_bias[...] = lower_bias(lengths_s, half, WIN)
    upper_causal[...] = upper_bias(lengths_s, half, None)
    lower_causal[...] = lower_bias(lengths_s, half, None)
    first[1].wait()
    stage_keys(k_held[half:], keys_s)
    first[2].wait()
    stage_values(v_held[half:], values_s)
    first[3].wait()

    def queries_of(unit):
        return q_held[half:, unit.lane : unit.lane + 2 * LANES]

    window_heads(queries_of, keys_s, values_s, bias_s, attn_ref, q_held.shape[1])
    for copy in last:
        copy.wait()


def project(weight_ref, attn_ref, out_ref, chunk):
    for first in range(0, out_ref.shape[0], chunk):
        part = slice(first, first + chunk)
        out_ref[part, :] = dot(weight_ref[part, :], attn_ref[...], ((1,), (0,))).astype(BF16)


def project_upper_kernel(
    weight_ref, attn_ref, q_ref, k_ref, v_ref, bias_ref, out_ref, first_ref, keys_s, values_s, *, chunk
):
    half = attn_ref.shape[1]
    project(weight_ref, attn_ref, out_ref, chunk)

    @pl.when(lax.axis_index("ctx") == 0)
    def _():
        stage_keys(k_ref[:half], keys_s)
        stage_values(v_ref[:half], values_s)

        def queries_of(unit):
            return q_ref[:half, unit.lane : unit.lane + 2 * LANES]

        window_heads(queries_of, keys_s, values_s, bias_ref.at[pl.ds(half, half)], first_ref, q_ref.shape[1])


def window_lower_kernel(
    q_ref, k_ref, v_ref, halo_ref, weight_ref, bias_ref, first_ref, kw_ref, vw_ref,
    out_ref, pair_held, attn_s, keys_s, values_s, sems, *, chunk
):
    width = kw_ref.shape[1]
    copies = [
        pltpu.make_async_copy(kw_ref, pair_held.at[:, pl.ds(0, width)], sems.at[0]),
        pltpu.make_async_copy(vw_ref, pair_held.at[:, pl.ds(width, width)], sems.at[1]),
    ]
    for copy in copies:
        copy.start()
    half = halo_ref.shape[0]
    kv_width = k_ref.shape[1]
    ctx = lax.axis_index("ctx")

    @pl.when(ctx == 0)
    def _():
        attn_s[...] = first_ref[...]

    @pl.when(ctx != 0)
    def _():
        stage_keys(jnp.concatenate([halo_ref[:, :kv_width], k_ref[:half]], axis=0), keys_s)
        stage_values(jnp.concatenate([halo_ref[:, kv_width:], v_ref[:half]], axis=0), values_s)

        def queries_of(unit):
            return q_ref[:half, unit.lane : unit.lane + 2 * LANES]

        window_heads(queries_of, keys_s, values_s, bias_ref, attn_s, q_ref.shape[1])

    project(weight_ref, attn_s, out_ref, chunk)
    for copy in copies:
        copy.wait()


def add_and_norm(own_ref, other_ref, gain_ref, branch_ref, normed_ref, first_row, sum_s, keep_ref, chunk):
    width, rows = own_ref.shape
    head = lax.axis_index("head")

    partial = jnp.zeros((8, rows), F32)
    for first in range(0, width, chunk):
        part = slice(first, first + chunk)
        total = own_ref[part, :].astype(F32) + other_ref[part, :].astype(F32)
        sum_s[part, :] = total
        rounded = total.astype(BF16)
        if keep_ref is not None:
            rounded = jnp.where(head == 0, rounded, keep_ref[part, :])
        branch_ref[part, :] = rounded
        partial += jnp.sum((total * total).reshape(chunk // 8, 8, rows), axis=0)
    squares = jnp.sum(partial, axis=0, keepdims=True)
    factor = lax.rsqrt(squares * (1.0 / width) + 1e-05)
    for first in range(0, width, LANES):
        last = min(first + LANES, width)
        piece = jnp.transpose(sum_s[first:last, :] * factor) * gain_ref[first:last][None, :]
        normed_ref[first_row : first_row + rows, first:last] = piece.astype(BF16)


def norm_upper_kernel(
    own_ref, other_ref, gain_ref, pair_ref, branch_ref, normed_ref, kv_ref, sum_s, *, chunk
):
    add_and_norm(own_ref, other_ref, gain_ref, branch_ref, normed_ref, 0, sum_s, None, chunk)
    kv_ref[...] = dot(normed_ref[...], pair_ref[...], ((1,), (0,))).astype(BF16)


def causal_upper_kernel(
    own_ref, other_ref, gain_ref, pair_ref, qw_ref, kept_ref, normed_ref, kv_up_ref, bias_ref,
    lower_bias_ref, branch_ref, q_ref, kv_ref, out_ref,
    branch_s, out_s, upper_q_s, normed_s, sum_s, keys_s, values_s, sems, unit_sems, *, chunk
):
    half = own_ref.shape[1]
    kv_width = kv_ref.shape[1] // 2
    q_width = qw_ref.shape[1]
    normed_s[half:, :] = normed_ref[...]
    add_and_norm(own_ref, other_ref, gain_ref, branch_s, normed_s, 0, sum_s, kept_ref, chunk)
    branch_out = pltpu.make_async_copy(branch_s, branch_ref, sems.at[0])
    branch_out.start()
    stage_keys(kv_up_ref[:, :kv_width], keys_s)
    stage_values(kv_up_ref[:, kv_width:], values_s)

    queries = dot(normed_s[...], qw_ref[...], ((1,), (0,))).astype(BF16)
    q_ref[...] = queries[:half]
    upper_q_s[...] = queries[half:]

    def queries_of(unit):
        return upper_q_s[:, unit.lane : unit.lane + 2 * LANES]

    causal_heads(queries_of, keys_s, values_s, bias_ref, out_s, q_width, lambda unit: None)
    upper_out = pltpu.make_async_copy(out_s, out_ref.at[pl.ds(half, half)], sems.at[1])
    upper_out.start()
    kv_ref[...] = dot(normed_s[:half, :], pair_ref[...], ((1,), (0,))).astype(BF16)
    branch_out.wait()
    upper_out.wait()

    @pl.when(lax.axis_index("ctx") == 0)
    def _():
        stage_keys(kv_ref[:, :kv_width], keys_s)
        stage_values(kv_ref[:, kv_width:], values_s)
        attend_lower(q_ref, keys_s, values_s, lower_bias_ref.at[pl.ds(half, half)], out_s, out_ref, unit_sems)


def attend_lower(q_ref, keys_s, values_s, bias_ref, out_s, out_ref, sems):
    half, q_width = q_ref.shape
    copies = []

    def queries_of(unit):
        return q_ref[:, unit.lane : unit.lane + 2 * LANES]

    def ready(unit):
        columns = pl.ds(unit.lane, 2 * LANES)
        copy = pltpu.make_async_copy(
            out_s.at[:, columns], out_ref.at[pl.ds(0, half), columns], sems.at[len(copies)]
        )
        copy.start()
        copies.append(copy)

    causal_heads(queries_of, keys_s, values_s, bias_ref, out_s, q_width, ready)
    for copy in copies:
        copy.wait()


def causal_lower_kernel(
    q_ref, kv_ref, halo_ref, bias_ref, given_ref, out_ref, out_s, keys_s, values_s, sems
):
    half, q_width = q_ref.shape
    kv_width = kv_ref.shape[1] // 2

    @pl.when(lax.axis_index("ctx") != 0)
    def _():
        stage_keys(jnp.concatenate([halo_ref[:, :kv_width], kv_ref[:, :kv_width]], axis=0), keys_s)
        stage_values(jnp.concatenate([halo_ref[:, kv_width:], kv_ref[:, kv_width:]], axis=0), values_s)
        attend_lower(q_ref, keys_s, values_s, bias_ref, out_s, out_ref, sems)


def attention_scratch(kv_heads, keys):
    return [
        pltpu.VMEM((kv_heads, 2, keys, LANES), BF16),
        pltpu.VMEM((kv_heads, HD + TAIL, keys), BF16),
    ]


def local(
    window_queries,
    window_keys,
    window_values,
    out_weight,
    norm_gain,
    query_weight,
    key_weight,
    value_weight,
    doc_lengths,
):
    rows, q_width = window_queries.shape
    kv_width = window_keys.shape[1]
    kv_heads = kv_width // HD
    width = out_weight.shape[1]
    half = rows // 2
    chunk = width // 2
    dma = pltpu.SemaphoreType.DMA
    lengths, queries, keys, values = [
        in_hbm(x) for x in (doc_lengths, window_queries, window_keys, window_values)
    ]

    packed = pl.pallas_call(
        pack_kernel,
        out_shape=jax.ShapeDtypeStruct((half, 2 * kv_width), BF16),
        in_specs=hbm_specs(2),
        out_specs=vmem_specs(1)[0],
        scratch_shapes=[dma((2,))],
        compiler_params=params(16),
        cost_estimate=pl.CostEstimate(flops=10**10, bytes_accessed=10**6, transcendentals=0),
        name="pack",
    )(keys, values)
    halo = shifted(packed, "ctx")
    attn_s = pltpu.VMEM((q_width, half), BF16)
    (
        attn_upper, q_held, k_held, v_held, window_bias, upper_causal, lower_causal, gain
    ) = pl.pallas_call(
        window_upper_kernel,
        out_shape=(
            attn_s,
            pltpu.VMEM((rows, q_width), BF16),
            pltpu.VMEM((rows, kv_width), BF16),
            pltpu.VMEM((rows, kv_width), BF16),
            pltpu.VMEM((rows, half), F32),
            pltpu.VMEM((half, half), F32),
            pltpu.VMEM((rows, half), F32),
            pltpu.VMEM((width,), F32),
        ),
        in_specs=hbm_specs(5),
        out_specs=tuple(vmem_specs(8)),
        scratch_shapes=[pltpu.SMEM(doc_lengths.shape, jnp.int32)]
        + attention_scratch(kv_heads, half)
        + [pltpu.VMEM((half, half), F32), dma((8,))],
        compiler_params=params(8),
        name="window_upper",
    )(lengths, queries, keys, values, in_hbm(norm_gain))
    held = in_vmem(jnp.transpose(out_weight))
    own_upper, attn_first = pl.pallas_call(
        functools.partial(project_upper_kernel, chunk=chunk),
        out_shape=(pltpu.VMEM((width, half), BF16), attn_s),
        in_specs=vmem_specs(6),
        out_specs=tuple(vmem_specs(2)),
        scratch_shapes=attention_scratch(kv_heads, half),
        compiler_params=params(8),
        name="project_upper",
    )(held, attn_upper, q_held, k_held, v_held, window_bias)
    query_held = in_vmem(query_weight)
    other_upper = swapped(own_upper, "head")
    own_lower, pair_held = pl.pallas_call(
        functools.partial(window_lower_kernel, chunk=chunk),
        out_shape=(pltpu.VMEM((width, half), BF16), pltpu.VMEM((width, 2 * kv_width), BF16)),
        in_specs=vmem_specs(7) + hbm_specs(2),
        out_specs=tuple(vmem_specs(2)),
        scratch_shapes=[attn_s] + attention_scratch(kv_heads, rows) + [dma((2,))],
        compiler_params=params(16),
        name="window_lower",
    )(q_held, k_held, v_held, in_vmem(halo), held, window_bias, attn_first, in_hbm(key_weight), in_hbm(value_weight))
    other_lower = swapped(own_lower, "head")
    branch_upper, normed_upper, pairs_upper = pl.pallas_call(
        functools.partial(norm_upper_kernel, chunk=192),
        out_shape=(
            pltpu.VMEM((width, half), BF16),
            pltpu.VMEM((half, width), BF16),
            pltpu.VMEM((half, 2 * kv_width), BF16),
        ),
        in_specs=vmem_specs(4),
        out_specs=tuple(vmem_specs(3)),
        scratch_shapes=[pltpu.VMEM((width, half), F32)],
        compiler_params=params(16),
        name="norm_upper",
    )(own_upper, other_upper, gain, pair_held)
    earlier = shifted(pairs_upper, "ctx")
    branch, causal_queries, pairs_lower, causal_out = pl.pallas_call(
        functools.partial(causal_upper_kernel, chunk=192),
        out_shape=(
            pltpu.HBM((width, half), BF16),
            pltpu.VMEM((half, q_width), BF16),
            pltpu.VMEM((half, 2 * kv_width), BF16),
            pltpu.HBM((rows, q_width), BF16),
        ),
        in_specs=vmem_specs(10),
        out_specs=(hbm_specs(1)[0], *vmem_specs(2), hbm_specs(1)[0]),
        scratch_shapes=[
            pltpu.VMEM((width, half), BF16),
            pltpu.VMEM((half, q_width), BF16),
            pltpu.VMEM((half, q_width), BF16),
            pltpu.VMEM((rows, width), BF16),
            pltpu.VMEM((width, half), F32),
        ]
        + attention_scratch(kv_heads, half)
        + [dma((2,)), dma((q_width // (2 * LANES),))],
        compiler_params=params(16),
        name="causal_upper",
    )(
        own_lower, other_lower, gain, pair_held, query_held,
        branch_upper, normed_upper, pairs_upper, upper_causal, lower_causal,
    )
    causal_out = pl.pallas_call(
        causal_lower_kernel,
        out_shape=pltpu.HBM((rows, q_width), BF16),
        in_specs=vmem_specs(4) + hbm_specs(1),
        out_specs=hbm_specs(1)[0],
        scratch_shapes=[pltpu.VMEM((half, q_width), BF16)]
        + attention_scratch(kv_heads, rows)
        + [dma((q_width // (2 * LANES),))],
        input_output_aliases={4: 0},
        compiler_params=params(16),
        name="causal_lower",
    )(causal_queries, pairs_lower, in_vmem(earlier), lower_causal, causal_out)
    return (jnp.transpose(branch), causal_out)


def solution(mesh):
    placed = (
        P("ctx", "head"),
        P("ctx", "head"),
        P("ctx", "head"),
        P("head", None),
        P(),
        P(None, "head"),
        P(None, "head"),
        P(None, "head"),
        P(),
    )
    return jax.shard_map(
        local,
        mesh=mesh,
        in_specs=placed,
        out_specs=(P(("ctx", "head"), None), P("ctx", "head")),
        check_vma=False,
    )
```

```python
import functools

import jax
import jax.numpy as jnp
from jax import lax
from jax.experimental import pallas as pl
from jax.experimental.pallas import tpu as pltpu
from jax.sharding import PartitionSpec as P

HD = 64
WIN = 128
LANES = 128
NEG = -1e30
TAIL = 16

F32 = jnp.float32
BF16 = jnp.bfloat16
MIB = 1024 * 1024


def params(mib):
    return pltpu.CompilerParams(vmem_limit_bytes=mib * MIB)


def in_vmem(array):
    return pltpu.with_memory_space_constraint(array, pltpu.VMEM)


def in_hbm(array):
    return pltpu.with_memory_space_constraint(array, pltpu.HBM)


def hbm_specs(count):
    return [pl.BlockSpec(memory_space=pltpu.HBM)] * count


def vmem_specs(count):
    return [pl.BlockSpec(memory_space=pltpu.VMEM)] * count


def dot(a, b, dims):
    return lax.dot_general(a, b, (dims, ((), ())), preferred_element_type=F32)


def shifted(block, axis):
    size = lax.axis_size(axis)
    return lax.ppermute(block, axis, [(i, (i + 1) % size) for i in range(size)])


def swapped(block, axis):
    size = lax.axis_size(axis)
    return lax.ppermute(block, axis, [(i, size - 1 - i) for i in range(size)])


def lower_bias(lengths_ref, half, width):
    ctx = lax.axis_index("ctx")
    first = jnp.where(ctx == 0, half, 0)
    split = first + lengths_ref[2 * ctx]
    return bias_of(2 * half, half, half, first, split, width)


def upper_bias(lengths_ref, half, width):
    ctx = lax.axis_index("ctx")
    last = lengths_ref.shape[0] - 1
    split = lengths_ref[jnp.minimum(2 * ctx + 2, last)]
    split = jnp.where(ctx == lax.axis_size("ctx") - 1, 2 * half, split)
    return bias_of(half, half, 0, 0, split, width)


def bias_of(keys, rows, row_offset, first, split, width):
    key = lax.broadcasted_iota(jnp.int32, (keys, rows), 0)
    row = lax.broadcasted_iota(jnp.int32, (keys, rows), 1) + row_offset
    lowest = jnp.where(row >= split, split, first)
    if width is not None:
        lowest = jnp.maximum(lowest, row - (width - 1))
    return jnp.where((key >= lowest) & (key <= row), 0.0, NEG).astype(F32)


def stage_keys(keys, keys_ref):
    scaled = keys * jnp.asarray(HD ** (-0.5), BF16)
    lane = lax.broadcasted_iota(jnp.int32, (keys.shape[0], LANES), 1)
    zero = jnp.zeros((keys.shape[0], LANES), BF16)
    for pair in range(keys.shape[1] // LANES):
        tile = scaled[:, pair * LANES : (pair + 1) * LANES]
        turned = jnp.concatenate([tile[:, HD:], tile[:, :HD]], axis=1)
        keys_ref[2 * pair, 0] = jnp.where(lane < HD, tile, zero)
        keys_ref[2 * pair, 1] = jnp.where(lane < HD, zero, turned)
        keys_ref[2 * pair + 1, 0] = jnp.where(lane < HD, turned, zero)
        keys_ref[2 * pair + 1, 1] = jnp.where(lane < HD, zero, tile)


def stage_values(values, values_ref):
    count = values.shape[0]
    turned = jnp.transpose(values)
    for head in range(values.shape[1] // HD):
        values_ref[head, :HD, :] = turned[head * HD : (head + 1) * HD]
        values_ref[head, HD:, :] = jnp.ones((TAIL, count), BF16)


class Unit:
    def __init__(self, g, lane):
        self.g, self.lane = g, lane


def units_of(kv_heads, q_width):
    step = 2 * LANES
    group = q_width // kv_heads
    return [Unit(lane // group, lane) for lane in range(0, q_width, step)]


def unit_scores(queries, unit, keys_ref):
    stacked = jnp.concatenate([queries[:, :LANES], queries[:, LANES:]], axis=0)
    keys = jnp.concatenate([keys_ref[unit.g, 0], keys_ref[unit.g, 1]], axis=0)
    return dot(keys, stacked, ((1,), (1,)))


def unit_weighted(scores, unit, values_ref, bias):
    count = bias.shape[0]
    wide = jnp.concatenate([bias, bias], axis=1)
    patterns = []
    for side in range(2):
        masked = scores[side * count : (side + 1) * count] + wide
        highest = jnp.max(masked, axis=0, keepdims=True)
        patterns.append(jnp.exp((masked - highest).astype(BF16)))
    return dot(values_ref[unit.g], jnp.concatenate(patterns, axis=1), ((1,), (0,)))


def pipelined(units, queries_of, keys_ref, values_ref, bias, write):
    count = len(units)
    scores = [unit_scores(queries_of(unit), unit, keys_ref) for unit in units[:2]]

    def finish(unit, weighted):
        write(unit, weighted[:HD] * (1.0 / weighted[HD : HD + 1]))

    before = None
    for i, unit in enumerate(units):
        now = scores.pop(0)
        if i + 2 < count:
            scores.append(unit_scores(queries_of(units[i + 2]), units[i + 2], keys_ref))
        weighted = unit_weighted(now, unit, values_ref, bias)
        if before is not None:
            finish(*before)
        before = (unit, weighted)
    finish(*before)


def window_heads(queries_of, keys_ref, values_ref, bias_ref, out_ref, q_width):
    def write(unit, part):
        rows = part.shape[1] // 4
        rounded = part.astype(BF16)
        for side in range(2):
            for t in range(2):
                at = (side * 2 + t) * rows
                start = unit.lane + t * LANES + side * HD
                out_ref[start : start + HD, :] = rounded[:, at : at + rows]

    pipelined(units_of(keys_ref.shape[0], q_width), queries_of, keys_ref, values_ref, bias_ref[...], write)


def causal_heads(queries_of, keys_ref, values_ref, bias_ref, out_ref, q_width, ready):
    def write(unit, part):
        rows = part.shape[1] // 4
        for t in range(2):
            low = part[:, t * rows : (t + 1) * rows]
            high = part[:, (2 + t) * rows : (3 + t) * rows]
            lane = unit.lane + t * LANES
            out_ref[:, lane : lane + LANES] = jnp.transpose(
                jnp.concatenate([low, high], axis=0).astype(BF16)
            )
        ready(unit)

    pipelined(units_of(keys_ref.shape[0], q_width), queries_of, keys_ref, values_ref, bias_ref[...], write)


def pack_kernel(k_ref, v_ref, out_ref, sems):
    half = out_ref.shape[0]
    kv_width = k_ref.shape[1]
    copies = [
        pltpu.make_async_copy(k_ref.at[pl.ds(half, half)], out_ref.at[:, pl.ds(0, kv_width)], sems.at[0]),
        pltpu.make_async_copy(
            v_ref.at[pl.ds(half, half)], out_ref.at[:, pl.ds(kv_width, kv_width)], sems.at[1]
        ),
    ]
    for copy in copies:
        copy.start()
    for copy in copies:
        copy.wait()


def window_upper_kernel(
    lengths_ref, q_ref, k_ref, v_ref, gain_ref,
    attn_ref, q_held, k_held, v_held, window_bias, upper_causal, lower_causal, gain_held,
    lengths_s, keys_s, values_s, bias_s, sems
):
    half = attn_ref.shape[1]
    upper, lower = pl.ds(half, half), pl.ds(0, half)
    first = [
        pltpu.make_async_copy(lengths_ref, lengths_s, sems.at[0]),
        pltpu.make_async_copy(k_ref.at[upper], k_held.at[upper], sems.at[1]),
        pltpu.make_async_copy(v_ref.at[upper], v_held.at[upper], sems.at[2]),
        pltpu.make_async_copy(q_ref.at[upper], q_held.at[upper], sems.at[3]),
    ]
    last = [
        pltpu.make_async_copy(k_ref.at[lower], k_held.at[lower], sems.at[4]),
        pltpu.make_async_copy(v_ref.at[lower], v_held.at[lower], sems.at[5]),
        pltpu.make_async_copy(q_ref.at[lower], q_held.at[lower], sems.at[6]),
        pltpu.make_async_copy(gain_ref, gain_held, sems.at[7]),
    ]
    for copy in first + last:
        copy.start()
    first[0].wait()
    bias_s[...] = upper_bias(lengths_s, half, WIN)
    window_bias[...] = lower_bias(lengths_s, half, WIN)
    upper_causal[...] = upper_bias(lengths_s, half, None)
    lower_causal[...] = lower_bias(lengths_s, half, None)
    first[1].wait()
    stage_keys(k_held[half:], keys_s)
    first[2].wait()
    stage_values(v_held[half:], values_s)
    first[3].wait()

    def queries_of(unit):
        return q_held[half:, unit.lane : unit.lane + 2 * LANES]

    window_heads(queries_of, keys_s, values_s, bias_s, attn_ref, q_held.shape[1])
    for copy in last:
        copy.wait()


def project(weight_ref, attn_ref, out_ref, chunk):
    for first in range(0, out_ref.shape[0], chunk):
        part = slice(first, first + chunk)
        out_ref[part, :] = dot(weight_ref[part, :], attn_ref[...], ((1,), (0,))).astype(BF16)


def project_upper_kernel(
    weight_ref, attn_ref, q_ref, k_ref, v_ref, bias_ref, out_ref, first_ref, keys_s, values_s, *, chunk
):
    half = attn_ref.shape[1]
    project(weight_ref, attn_ref, out_ref, chunk)

    @pl.when(lax.axis_index("ctx") == 0)
    def _():
        stage_keys(k_ref[:half], keys_s)
        stage_values(v_ref[:half], values_s)

        def queries_of(unit):
            return q_ref[:half, unit.lane : unit.lane + 2 * LANES]

        window_heads(queries_of, keys_s, values_s, bias_ref.at[pl.ds(half, half)], first_ref, q_ref.shape[1])


def window_lower_kernel(
    q_ref, k_ref, v_ref, halo_ref, weight_ref, bias_ref, first_ref, kw_ref, vw_ref,
    out_ref, pair_held, attn_s, keys_s, values_s, sems, *, chunk
):
    width = kw_ref.shape[1]
    copies = [
        pltpu.make_async_copy(kw_ref, pair_held.at[:, pl.ds(0, width)], sems.at[0]),
        pltpu.make_async_copy(vw_ref, pair_held.at[:, pl.ds(width, width)], sems.at[1]),
    ]
    for copy in copies:
        copy.start()
    half = halo_ref.shape[0]
    kv_width = k_ref.shape[1]
    ctx = lax.axis_index("ctx")

    @pl.when(ctx == 0)
    def _():
        attn_s[...] = first_ref[...]

    @pl.when(ctx != 0)
    def _():
        stage_keys(jnp.concatenate([halo_ref[:, :kv_width], k_ref[:half]], axis=0), keys_s)
        stage_values(jnp.concatenate([halo_ref[:, kv_width:], v_ref[:half]], axis=0), values_s)

        def queries_of(unit):
            return q_ref[:half, unit.lane : unit.lane + 2 * LANES]

        window_heads(queries_of, keys_s, values_s, bias_ref, attn_s, q_ref.shape[1])

    project(weight_ref, attn_s, out_ref, chunk)
    for copy in copies:
        copy.wait()


def add_and_norm(own_ref, other_ref, gain_ref, branch_ref, normed_ref, first_row, sum_s, keep_ref, chunk):
    width, rows = own_ref.shape
    head = lax.axis_index("head")

    partial = jnp.zeros((8, rows), F32)
    for first in range(0, width, chunk):
        part = slice(first, first + chunk)
        total = own_ref[part, :].astype(F32) + other_ref[part, :].astype(F32)
        sum_s[part, :] = total
        rounded = total.astype(BF16)
        if keep_ref is not None:
            rounded = jnp.where(head == 0, rounded, keep_ref[part, :])
        branch_ref[part, :] = rounded
        partial += jnp.sum((total * total).reshape(chunk // 8, 8, rows), axis=0)
    squares = jnp.sum(partial, axis=0, keepdims=True)
    factor = lax.rsqrt(squares * (1.0 / width) + 1e-05)
    for first in range(0, width, LANES):
        last = min(first + LANES, width)
        piece = jnp.transpose(sum_s[first:last, :] * factor) * gain_ref[first:last][None, :]
        normed_ref[first_row : first_row + rows, first:last] = piece.astype(BF16)


def norm_upper_kernel(
    own_ref, other_ref, gain_ref, pair_ref, branch_ref, normed_ref, kv_ref, sum_s, *, chunk
):
    add_and_norm(own_ref, other_ref, gain_ref, branch_ref, normed_ref, 0, sum_s, None, chunk)
    kv_ref[...] = dot(normed_ref[...], pair_ref[...], ((1,), (0,))).astype(BF16)


def causal_upper_kernel(
    own_ref, other_ref, gain_ref, pair_ref, qw_ref, kept_ref, normed_ref, kv_up_ref, bias_ref,
    lower_bias_ref, branch_ref, q_ref, kv_ref, out_ref,
    branch_s, out_s, upper_q_s, normed_s, sum_s, keys_s, values_s, sems, unit_sems, *, chunk
):
    half = own_ref.shape[1]
    kv_width = kv_ref.shape[1] // 2
    q_width = qw_ref.shape[1]
    normed_s[half:, :] = normed_ref[...]
    add_and_norm(own_ref, other_ref, gain_ref, branch_s, normed_s, 0, sum_s, kept_ref, chunk)
    branch_out = pltpu.make_async_copy(branch_s, branch_ref, sems.at[0])
    branch_out.start()
    stage_keys(kv_up_ref[:, :kv_width], keys_s)
    stage_values(kv_up_ref[:, kv_width:], values_s)

    queries = dot(normed_s[...], qw_ref[...], ((1,), (0,))).astype(BF16)
    q_ref[...] = queries[:half]
    upper_q_s[...] = queries[half:]

    def queries_of(unit):
        return upper_q_s[:, unit.lane : unit.lane + 2 * LANES]

    causal_heads(queries_of, keys_s, values_s, bias_ref, out_s, q_width, lambda unit: None)
    upper_out = pltpu.make_async_copy(out_s, out_ref.at[pl.ds(half, half)], sems.at[1])
    upper_out.start()
    kv_ref[...] = dot(normed_s[:half, :], pair_ref[...], ((1,), (0,))).astype(BF16)
    branch_out.wait()
    upper_out.wait()

    @pl.when(lax.axis_index("ctx") == 0)
    def _():
        stage_keys(kv_ref[:, :kv_width], keys_s)
        stage_values(kv_ref[:, kv_width:], values_s)
        attend_lower(q_ref, keys_s, values_s, lower_bias_ref.at[pl.ds(half, half)], out_s, out_ref, unit_sems)


def attend_lower(q_ref, keys_s, values_s, bias_ref, out_s, out_ref, sems):
    half, q_width = q_ref.shape
    copies = []

    def queries_of(unit):
        return q_ref[:, unit.lane : unit.lane + 2 * LANES]

    def ready(unit):
        columns = pl.ds(unit.lane, 2 * LANES)
        copy = pltpu.make_async_copy(
            out_s.at[:, columns], out_ref.at[pl.ds(0, half), columns], sems.at[len(copies)]
        )
        copy.start()
        copies.append(copy)

    causal_heads(queries_of, keys_s, values_s, bias_ref, out_s, q_width, ready)
    for copy in copies:
        copy.wait()


def causal_lower_kernel(
    q_ref, kv_ref, halo_ref, bias_ref, given_ref, out_ref, out_s, keys_s, values_s, sems
):
    half, q_width = q_ref.shape
    kv_width = kv_ref.shape[1] // 2

    @pl.when(lax.axis_index("ctx") != 0)
    def _():
        stage_keys(jnp.concatenate([halo_ref[:, :kv_width], kv_ref[:, :kv_width]], axis=0), keys_s)
        stage_values(jnp.concatenate([halo_ref[:, kv_width:], kv_ref[:, kv_width:]], axis=0), values_s)
        attend_lower(q_ref, keys_s, values_s, bias_ref, out_s, out_ref, sems)


def attention_scratch(kv_heads, keys):
    return [
        pltpu.VMEM((kv_heads, 2, keys, LANES), BF16),
        pltpu.VMEM((kv_heads, HD + TAIL, keys), BF16),
    ]


def local(
    window_queries,
    window_keys,
    window_values,
    out_weight,
    norm_gain,
    query_weight,
    key_weight,
    value_weight,
    doc_lengths,
):
    rows, q_width = window_queries.shape
    kv_width = window_keys.shape[1]
    kv_heads = kv_width // HD
    width = out_weight.shape[1]
    half = rows // 2
    chunk = width // 2
    dma = pltpu.SemaphoreType.DMA
    lengths, queries, keys, values = [
        in_hbm(x) for x in (doc_lengths, window_queries, window_keys, window_values)
    ]

    packed = pl.pallas_call(
        pack_kernel,
        out_shape=jax.ShapeDtypeStruct((half, 2 * kv_width), BF16),
        in_specs=hbm_specs(2),
        out_specs=vmem_specs(1)[0],
        scratch_shapes=[dma((2,))],
        compiler_params=params(16),
        cost_estimate=pl.CostEstimate(flops=10**10, bytes_accessed=10**6, transcendentals=0),
        name="pack",
    )(keys, values)
    halo = shifted(packed, "ctx")
    attn_s = pltpu.VMEM((q_width, half), BF16)
    (
        attn_upper, q_held, k_held, v_held, window_bias, upper_causal, lower_causal, gain
    ) = pl.pallas_call(
        window_upper_kernel,
        out_shape=(
            attn_s,
            pltpu.VMEM((rows, q_width), BF16),
            pltpu.VMEM((rows, kv_width), BF16),
            pltpu.VMEM((rows, kv_width), BF16),
            pltpu.VMEM((rows, half), F32),
            pltpu.VMEM((half, half), F32),
            pltpu.VMEM((rows, half), F32),
            pltpu.VMEM((width,), F32),
        ),
        in_specs=hbm_specs(5),
        out_specs=tuple(vmem_specs(8)),
        scratch_shapes=[pltpu.SMEM(doc_lengths.shape, jnp.int32)]
        + attention_scratch(kv_heads, half)
        + [pltpu.VMEM((half, half), F32), dma((8,))],
        compiler_params=params(8),
        name="window_upper",
    )(lengths, queries, keys, values, in_hbm(norm_gain))
    held = in_vmem(jnp.transpose(out_weight))
    own_upper, attn_first = pl.pallas_call(
        functools.partial(project_upper_kernel, chunk=chunk),
        out_shape=(pltpu.VMEM((width, half), BF16), attn_s),
        in_specs=vmem_specs(6),
        out_specs=tuple(vmem_specs(2)),
        scratch_shapes=attention_scratch(kv_heads, half),
        compiler_params=params(8),
        name="project_upper",
    )(held, attn_upper, q_held, k_held, v_held, window_bias)
    query_held = in_vmem(query_weight)
    other_upper = swapped(own_upper, "head")
    own_lower, pair_held = pl.pallas_call(
        functools.partial(window_lower_kernel, chunk=chunk),
        out_shape=(pltpu.VMEM((width, half), BF16), pltpu.VMEM((width, 2 * kv_width), BF16)),
        in_specs=vmem_specs(7) + hbm_specs(2),
        out_specs=tuple(vmem_specs(2)),
        scratch_shapes=[attn_s] + attention_scratch(kv_heads, rows) + [dma((2,))],
        compiler_params=params(16),
        name="window_lower",
    )(q_held, k_held, v_held, in_vmem(halo), held, window_bias, attn_first, in_hbm(key_weight), in_hbm(value_weight))
    other_lower = swapped(own_lower, "head")
    branch_upper, normed_upper, pairs_upper = pl.pallas_call(
        functools.partial(norm_upper_kernel, chunk=192),
        out_shape=(
            pltpu.VMEM((width, half), BF16),
            pltpu.VMEM((half, width), BF16),
            pltpu.VMEM((half, 2 * kv_width), BF16),
        ),
        in_specs=vmem_specs(4),
        out_specs=tuple(vmem_specs(3)),
        scratch_shapes=[pltpu.VMEM((width, half), F32)],
        compiler_params=params(16),
        name="norm_upper",
    )(own_upper, other_upper, gain, pair_held)
    earlier = shifted(pairs_upper, "ctx")
    branch, causal_queries, pairs_lower, causal_out = pl.pallas_call(
        functools.partial(causal_upper_kernel, chunk=192),
        out_shape=(
            pltpu.HBM((width, half), BF16),
            pltpu.VMEM((half, q_width), BF16),
            pltpu.VMEM((half, 2 * kv_width), BF16),
            pltpu.HBM((rows, q_width), BF16),
        ),
        in_specs=vmem_specs(10),
        out_specs=(hbm_specs(1)[0], *vmem_specs(2), hbm_specs(1)[0]),
        scratch_shapes=[
            pltpu.VMEM((width, half), BF16),
            pltpu.VMEM((half, q_width), BF16),
            pltpu.VMEM((half, q_width), BF16),
            pltpu.VMEM((rows, width), BF16),
            pltpu.VMEM((width, half), F32),
        ]
        + attention_scratch(kv_heads, half)
        + [dma((2,)), dma((q_width // (2 * LANES),))],
        compiler_params=params(16),
        name="causal_upper",
    )(
        own_lower, other_lower, gain, pair_held, query_held,
        branch_upper, normed_upper, pairs_upper, upper_causal, lower_causal,
    )
    causal_out = pl.pallas_call(
        causal_lower_kernel,
        out_shape=pltpu.HBM((rows, q_width), BF16),
        in_specs=vmem_specs(4) + hbm_specs(1),
        out_specs=hbm_specs(1)[0],
        scratch_shapes=[pltpu.VMEM((half, q_width), BF16)]
        + attention_scratch(kv_heads, rows)
        + [dma((q_width // (2 * LANES),))],
        input_output_aliases={4: 0},
        compiler_params=params(16),
        name="causal_lower",
    )(causal_queries, pairs_lower, in_vmem(earlier), lower_causal, causal_out)
    return (jnp.transpose(branch), causal_out)


def solution(mesh):
    placed = (
        P("ctx", "head"),
        P("ctx", "head"),
        P("ctx", "head"),
        P("head", None),
        P(),
        P(None, "head"),
        P(None, "head"),
        P(None, "head"),
        P(),
    )
    return jax.shard_map(
        local,
        mesh=mesh,
        in_specs=placed,
        out_specs=(P(("ctx", "head"), None), P("ctx", "head")),
        check_vma=False,
    )
```
